32 devices in a mesh: ep: 8 (over y, x, core), hs: 4 (over z).
Axes of the slice: x: 2, y: 2, z: 4, core: 2. Of those that a mesh axis runs over, the one named last changes fastest.
Arguments:
- tokens: bfloat16 [8192, 1152], P(('ep', 'hs')), may hold values from -6 to 6
- starts: int32 [8192], P(('ep', 'hs')), may hold values from 0 to 1, as said below
- counts: int32 [32], P(('ep', 'hs')), may hold values from 192 to 256, as said below
- routes: int32 [8192], P(('ep', 'hs')), may hold values from 0 to 7
- slot_index: int32 [8192], P(('ep', 'hs')), may hold values from -1 to 39, as said below
- gain_mix: float32 [1152], replicated, may hold values from 0.5 to 1.5
- in_proj: bfloat16 [1152, 4608], replicated, may hold values from -0.1875 to 0.1875
- conv_weight: float32 [4, 2304], replicated, may hold values from -3 to 3
- conv_bias: float32 [2304], replicated, may hold values from -3 to 3
- x_proj: bfloat16 [2304, 104], replicated, may hold values from -1 to 1
- dt_proj: bfloat16 [72, 2304], replicated, may hold values from -0.75 to 0.75
- dt_bias: float32 [2304], replicated, may hold values from -12 to 0
- a_log: float32 [2304, 16], replicated, may hold values from -3 to -1
- skip_gain: float32 [2304], replicated, may hold values from 0.5 to 1.5
- out_proj: bfloat16 [2304, 1152], replicated, may hold values from -0.375 to 0.375
- gain_ffn: float32 [1152], replicated, may hold values from 0.5 to 1.5
- router: float32 [1152, 8], replicated, may hold values from -0.125 to 0.125
- up_proj: bfloat16 [8, 1152, 3072], P('ep', None, 'hs'), may hold values from -0.1875 to 0.1875
- down_proj: bfloat16 [8, 3072, 1152], P('ep', 'hs'), may hold values from -0.875 to 0.875
- out_grad: bfloat16 [8192, 1152], P(('ep', 'hs')), may hold values from -6 to 6
Outputs:
- block_out: bfloat16 [8192, 1152], P(('ep', 'hs'))
- tokens_grad: float32 [8192, 1152], P(('ep', 'hs'))
- gains_grad: float32 [2304], P(('ep', 'hs'))
- router_grad: float32 [9216], P(('ep', 'hs'))
- in_proj_grad: float32 [1152, 4608], P(None, ('ep', 'hs'))
- conv_weight_grad: float32 [4, 2304], P(None, ('ep', 'hs'))
- conv_bias_grad: float32 [2304], P(('ep', 'hs'))
- x_proj_grad: float32 [2304, 104], P(('ep', 'hs'))
- dt_proj_grad: float32 [72, 2304], P(None, ('ep', 'hs'))
- dt_bias_grad: float32 [2304], P(('ep', 'hs'))
- a_log_grad: float32 [2304, 16], P(('ep', 'hs'))
- skip_gain_grad: float32 [2304], P(('ep', 'hs'))
- out_proj_grad: float32 [2304, 1152], P(('ep', 'hs'))
- up_proj_grad: float32 [8, 1152, 3072], P('ep', None, 'hs')
- down_proj_grad: float32 [8, 3072, 1152], P('ep', 'hs')
The draws below stay inside these ranges and needn't reach their ends.
Inputs may be any that keep to these rules, and one draw needn't show every extreme that they name: `starts`: 1 exactly at the first real row of each sequence, 0 elsewhere; the real rows of the 4 devices of one index of ep, in device order, form three whole sequences, the first starting at the group's first real row and the second having real rows on every one of these devices. `counts`: a device's real rows are its first rows, the rest is padding. `slot_index`: -1 on padding rows and where a device has already given 40 earlier real rows to the same expert; else the number of earlier real rows of the same device with the same route.
All inputs are finite; a program needn't handle non-finite values.
Results may differ from the reference program's by a relative error of at most 0.012.
The reference program's roundings to bfloat16 on the way count: a program that leaves them out, or rounds other values in their place, can miss the bound.
Values may be sent and summed in bfloat16 or wider, within the bound.
No kernel may reach another device: no remote copies, remote signals or barrier semaphores. Data moves between devices by JAX's collectives and lax.ppermute only.
A program may use at most 448 MiB of HBM per device.

```python
import jax
import jax.numpy as jnp
from jax import lax

D = 1152
DI = 2304
DT_RANK = 72
STATE = 16
FF = 3072
CONV = 4
SCAN_BLOCK = 16
TOK_DEV = 256
EXPERTS = 8
TOKENS = 8192
CAP = 40
N_EP = 8
N_HS = 4
DEVICES = 32


def shuffle_rows(row_key):
    return jax.random.permutation(row_key, TOK_DEV)


def layout(key):
    key_count, key_ends, key_first, key_last, key_route, key_hot, key_pick = jax.random.split(key, 7)
    fewest = TOK_DEV * 3 // 4
    counts = jax.random.randint(key_count, (DEVICES,), fewest, TOK_DEV + 1)
    shuffle = jax.random.permutation(key_ends, DEVICES)
    counts = counts.at[shuffle[0]].set(TOK_DEV).at[shuffle[1]].set(fewest)
    grouped = counts.reshape(N_EP, N_HS)
    offsets = jnp.cumsum(grouped, axis=1) - grouped
    totals = jnp.sum(grouped, axis=1)
    first_len = jax.random.randint(key_first, (N_EP,), grouped[:, 0] // 4, grouped[:, 0] // 2 + 1)
    last_len = jax.random.randint(key_last, (N_EP,), grouped[:, N_HS - 1] // 4, grouped[:, N_HS - 1] // 2 + 1)
    positions = jnp.arange(TOK_DEV, dtype=jnp.int32)
    position = offsets[:, :, None] + positions[None, None, :]
    is_real = positions[None, None, :] < grouped[:, :, None]
    begins = (position == 0) | (position == first_len[:, None, None]) | (position == (totals - last_len)[:, None, None])
    starts = (is_real & begins).astype(jnp.int32).reshape(DEVICES, TOK_DEV)
    is_real = is_real.reshape(DEVICES, TOK_DEV)
    routes = jax.random.randint(key_route, (DEVICES, TOK_DEV), 0, EXPERTS)
    favored = jax.random.randint(key_hot, (), 0, EXPERTS)
    shuffled = jax.vmap(shuffle_rows)(jax.random.split(key_pick, DEVICES))
    scores = jnp.where(is_real, shuffled, -1)
    forced = CAP + CAP // 2
    cutoff = lax.top_k(scores, forced)[0][:, forced - 1]
    routes = jnp.where(scores >= cutoff[:, None], favored, routes)
    member = ((routes[:, :, None] == jnp.arange(EXPERTS)[None, None, :]) & is_real[:, :, None]).astype(jnp.int32)
    before = jnp.cumsum(member, axis=1) - member
    rank_row = jnp.sum(before * member, axis=2)
    slot_index = jnp.where(is_real & (rank_row < CAP), rank_row, -1)
    return (counts.astype(jnp.int32), starts.reshape(-1), routes.reshape(-1).astype(jnp.int32), slot_index.reshape(-1).astype(jnp.int32))


def draw_counts(key, part):
    return layout(key)[0]


def draw_starts(key, part):
    return layout(key)[1]


def draw_routes(key, part):
    return layout(key)[2]


def draw_slot_index(key, part):
    return layout(key)[3]


def draw_x_proj(key, part):
    key = jax.random.fold_in(key, 12)
    normal_draw = jax.random.normal(key, (DI, DT_RANK + 2 * STATE), jnp.float32)
    columns = jnp.arange(DT_RANK + 2 * STATE)
    column_scale = jnp.where(columns < DT_RANK, 1.0, 2.0) * DI ** (-0.5)
    values = jnp.clip(normal_draw, -5.0, 5.0) * column_scale[None, :]
    return values.astype(jnp.bfloat16)


def draw_dt_bias(key, part):
    key = jax.random.fold_in(key, 11)
    key_coin, key_slow, key_fast = jax.random.split(key, 3)
    chain_length = TOK_DEV * N_HS
    slow_share = 0.5
    is_slow = jax.random.uniform(key_coin, (DI,)) < slow_share
    slow_step = jnp.exp(jax.random.uniform(key_slow, (DI,), jnp.float32, jnp.log(1.0 / chain_length), jnp.log(4.0 / chain_length)))
    fast_step = jnp.exp(jax.random.uniform(key_fast, (DI,), jnp.float32, jnp.log(0.02), jnp.log(0.2)))
    step_value = jnp.where(is_slow, slow_step, fast_step)
    return jnp.log(jnp.expm1(step_value)).astype(jnp.float32)


def steps_of(own_key, shape, shards, smallest, high):
    level = 1.0
    for dim, shards_of in shards:
        heights = jax.random.uniform(jax.random.fold_in(jax.random.fold_in(own_key, 6), dim), (shards_of,), jnp.float32, smallest / len(shards), high / len(shards))
        level = level * jnp.repeat(jnp.exp(heights), shape[dim] // shards_of).reshape((-1,) + (1,) * (len(shape) - 1 - dim))
    return level


def normal_values(stream_key, dims, deviation, most, cuts=(), held_as=jnp.bfloat16):
    values = deviation * jax.random.normal(stream_key, dims, jnp.float32)
    if cuts:
        values = values * steps_of(stream_key, dims, cuts, -0.22, 0.18)
    return jnp.clip(values, -most, most).astype(held_as)


def setup_inputs(seed: int = 0) -> dict:
    seeds = jax.random.split(jax.random.key(seed), 21)
    return {
        "tokens": normal_values(seeds[0], (TOKENS, D), 1.0, 6.0, ((0, 32),)),
        "starts": draw_starts(jax.random.fold_in(seeds[20], 71), 0),
        "counts": draw_counts(jax.random.fold_in(seeds[20], 71), 0),
        "routes": draw_routes(jax.random.fold_in(seeds[20], 71), 0),
        "slot_index": draw_slot_index(jax.random.fold_in(seeds[20], 71), 0),
        "gain_mix": jnp.clip(1.0 + 0.1 * jax.random.normal(seeds[5], (D,), jnp.float32), 0.5, 1.5),
        "in_proj": normal_values(seeds[6], (D, 2 * DI), D ** -0.5, 0.1875),
        "conv_weight": normal_values(seeds[7], (CONV, DI), CONV ** -0.5, 3.0, (), jnp.float32),
        "conv_bias": normal_values(seeds[8], (DI,), 0.5, 3.0, (), jnp.float32),
        "x_proj": draw_x_proj(jax.random.fold_in(seeds[20], 71), 0),
        "dt_proj": normal_values(seeds[10], (DT_RANK, DI), DT_RANK ** -0.5, 0.75),
        "dt_bias": draw_dt_bias(jax.random.fold_in(seeds[20], 71), 0),
        "a_log": jnp.clip(jax.random.uniform(seeds[12], (DI, STATE), jnp.float32, -3.0, -1.0), -3.0, -1.0),
        "skip_gain": jnp.clip(jax.random.uniform(seeds[13], (DI,), jnp.float32, 0.5, 1.5), 0.5, 1.5),
        "out_proj": normal_values(seeds[14], (DI, D), (DI // 8) ** -0.5, 0.375),
        "gain_ffn": jnp.clip(1.0 + 0.1 * jax.random.normal(seeds[15], (D,), jnp.float32), 0.5, 1.5),
        "router": normal_values(seeds[16], (D, EXPERTS), (2 * D) ** -0.5, 0.125, (), jnp.float32),
        "up_proj": normal_values(seeds[17], (EXPERTS, D, FF), D ** -0.5, 0.1875, ((0, 8), (2, 4))),
        "down_proj": normal_values(seeds[18], (EXPERTS, FF, D), (max(1, FF // (EXPERTS * EXPERTS))) ** -0.5, 0.875, ((0, 8), (1, 4))),
        "out_grad": normal_values(seeds[19], (TOKENS, D), 1.0, 6.0, ((0, 32),)),
    }


norm_epsilon = 1e-05
highest = lax.Precision.HIGHEST

@jax.custom_vjp
def low(v):
    return lax.optimization_barrier(v.astype(jnp.bfloat16)).astype(jnp.float32)

@jax.custom_vjp
def low_back(v):
    return v

def low_keep(v):
    return (low(v), None)

def low_pass(kept, grad):
    return (grad,)

def back_keep(v):
    return (v, None)

def back_low(kept, grad):
    return (low(grad),)
low.defvjp(low_keep, low_pass)
low_back.defvjp(back_keep, back_low)

def full_dot(left, right):
    return jnp.dot(left, right, precision=highest, preferred_element_type=jnp.float32)

def rms_scale(values):
    return lax.rsqrt(lax.optimization_barrier(jnp.mean(values * values, axis=1, keepdims=True)) + norm_epsilon)

def scaled_norm(values, gain_row):
    return values * rms_scale(values) * gain_row[None, :]

def gelu_tanh(values):
    return jax.nn.gelu(values, approximate=True)

def join_forward(earlier, latter):
    return (earlier[0] * latter[0], latter[0] * earlier[1] + latter[1])

def conv_mix(x_inner, halo_rows, halo_flags, start_flags, conv_w, conv_b):
    tap_count = conv_w.shape[0]
    length = x_inner.shape[0]
    extended = jnp.concatenate([halo_rows, x_inner], axis=0)
    flag_line = jnp.concatenate([halo_flags, start_flags], axis=0)
    result = conv_b[None, :] + conv_w[tap_count - 1][None, :] * x_inner
    survive = jnp.ones((length,), jnp.float32)
    for offset in range(1, tap_count):
        survive = survive * (1.0 - flag_line[tap_count - offset:tap_count - offset + length])
        shifted = extended[tap_count - 1 - offset:tap_count - 1 - offset + length]
        result = result + conv_w[tap_count - 1 - offset][None, :] * shifted * survive[:, None]
    return jax.nn.silu(result)

def delta_apply(step_pre, bias_row, real_rows):
    return jax.nn.softplus(step_pre + bias_row[None, :]) * real_rows[:, None]

def block_view(values, block_size):
    blocked = values.reshape((values.shape[0] // block_size, block_size) + values.shape[1:])
    return jnp.swapaxes(blocked, 0, 1)

def block_summaries(mixer_in, step_size, input_map, start_flags, log_rates, block_size):
    rate_table = -jnp.exp(log_rates)
    blocks = mixer_in.shape[0] // block_size
    staying = 1.0 - start_flags
    sequence = (block_view(mixer_in * step_size, block_size), block_view(step_size, block_size), block_view(input_map, block_size), block_view(staying, block_size))

    def advance(memory, element):
        driven, stride, in_map, remain = element
        decays = jnp.exp(stride[:, :, None] * rate_table[None]) * remain[:, None, None]
        return (decays * memory + driven[:, :, None] * in_map[:, None, :], None)
    initial = jnp.zeros((blocks,) + rate_table.shape, jnp.float32)
    block_ends, _ = lax.scan(jax.checkpoint(advance), initial, sequence)
    stride_total = lax.optimization_barrier(jnp.sum(step_size.reshape(blocks, block_size, -1), axis=1))
    kept_total = jnp.prod(staying.reshape(blocks, block_size), axis=1)
    block_spans = jnp.exp(stride_total[:, :, None] * rate_table[None]) * kept_total[:, None, None]
    return lax.associative_scan(join_forward, (block_spans, block_ends), axis=0)

def block_outputs(mixer_in, step_size, input_map, output_map, start_flags, log_rates, skip_w, gate_pre, spans_cum, ends_cum, state_in, block_size):
    rate_table = -jnp.exp(log_rates)
    staying = 1.0 - start_flags
    first_span = jnp.ones((1,) + rate_table.shape, jnp.float32)
    first_end = jnp.zeros((1,) + rate_table.shape, jnp.float32)
    prior_span = jnp.concatenate([first_span, spans_cum[:-1]], axis=0)
    prior_end = jnp.concatenate([first_end, ends_cum[:-1]], axis=0)
    opening = prior_span * state_in[None] + prior_end
    sequence = (block_view(mixer_in * step_size, block_size), block_view(step_size, block_size), block_view(input_map, block_size), block_view(output_map, block_size), block_view(staying, block_size))

    def advance(memory, element):
        driven, stride, in_map, out_map, remain = element
        decays = jnp.exp(stride[:, :, None] * rate_table[None]) * remain[:, None, None]
        memory = decays * memory + driven[:, :, None] * in_map[:, None, :]
        return (memory, lax.optimization_barrier(jnp.sum(memory * out_map[:, None, :], axis=2)))
    _, readout = lax.scan(jax.checkpoint(advance), opening, sequence)
    scan_out = jnp.swapaxes(readout, 0, 1).reshape(mixer_in.shape) + skip_w[None, :] * mixer_in
    return scan_out * jax.nn.silu(gate_pre)

def group_major(values):
    shaped = values.reshape((N_EP, N_HS) + values.shape[1:])
    return jnp.swapaxes(shaped, 0, 1)

def reference(tokens, starts, counts, routes, slot_index, gain_mix, in_proj, conv_weight, conv_bias, x_proj, dt_proj, dt_bias, a_log, skip_gain, out_proj, gain_ffn, router, up_proj, down_proj, out_grad):
    float_type = jnp.float32
    start_flags = starts.astype(float_type).reshape(DEVICES, TOK_DEV)
    positions = jnp.arange(TOK_DEV, dtype=jnp.int32)
    real_rows = (positions[None, :] < counts[:, None]).astype(float_type)
    chosen = (routes[:, None] == jnp.arange(EXPERTS, dtype=jnp.int32)[None, :]).astype(float_type)
    column = routes * CAP + slot_index
    placed = ((column[:, None] == jnp.arange(EXPERTS * CAP, dtype=jnp.int32)[None, :]) & (slot_index[:, None] >= 0)).astype(float_type)
    placed = placed.reshape(DEVICES, TOK_DEV, EXPERTS * CAP)
    edge_starts = (counts - (CONV - 1)).astype(jnp.int32)
    flags_grouped = group_major(start_flags)
    real_grouped = group_major(real_rows)
    edges_grouped = group_major(edge_starts)

    def forward(tokens_in, gain_one, in_weight, conv_w, conv_b, x_weight, dt_weight, dt_shift, log_rates, skip_w, out_weight, gain_two, router_w, up_weight, down_weight):
        normed_one = scaled_norm(tokens_in, gain_one)
        projected = low_back(full_dot(low(normed_one), in_weight))
        inner_x = group_major(projected[:, :DI].reshape(DEVICES, TOK_DEV, DI))
        inner_gate = group_major(projected[:, DI:].reshape(DEVICES, TOK_DEV, DI))

        def device_mixer(carried, element):
            memory, halo_rows, halo_flags = carried
            x_part, gate_part, flag_part, real_part, edge_start = element
            mixer_in = conv_mix(x_part, halo_rows, halo_flags, flag_part, conv_w, conv_b)
            small_proj = low_back(full_dot(low(mixer_in), x_weight))
            step_pre = low_back(full_dot(low(small_proj[:, :DT_RANK]), dt_weight))
            step_size = delta_apply(step_pre, dt_shift, real_part)
            input_map = small_proj[:, DT_RANK:DT_RANK + STATE]
            output_map = small_proj[:, DT_RANK + STATE:]
            spans_cum, ends_cum = block_summaries(mixer_in, step_size, input_map, flag_part, log_rates, SCAN_BLOCK)
            gated_out = block_outputs(mixer_in, step_size, input_map, output_map, flag_part, log_rates, skip_w, gate_part, spans_cum, ends_cum, memory, SCAN_BLOCK)
            memory = spans_cum[-1] * memory + ends_cum[-1]
            next_rows = lax.dynamic_slice_in_dim(x_part, edge_start, CONV - 1, 0)
            next_flags = lax.dynamic_slice_in_dim(flag_part, edge_start, CONV - 1, 0)
            return ((memory, next_rows, next_flags), gated_out)
        initial = (jnp.zeros((N_EP, DI, STATE), float_type), jnp.zeros((N_EP, CONV - 1, DI), float_type), jnp.zeros((N_EP, CONV - 1), float_type))
        _, gated_all = lax.scan(jax.checkpoint(jax.vmap(device_mixer)), initial, (inner_x, inner_gate, flags_grouped, real_grouped, edges_grouped))
        gated_all = jnp.swapaxes(gated_all, 0, 1).reshape(TOKENS, DI)
        mixer_out = low_back(full_dot(low(gated_all), out_weight))
        middle = tokens_in + mixer_out * real_rows.reshape(TOKENS, 1)
        normed_two = scaled_norm(middle, gain_two)
        router_probs = jax.nn.softmax(full_dot(normed_two, router_w), axis=1)
        gate_value = lax.optimization_barrier(jnp.sum(router_probs * chosen, axis=1))
        dispatched = jnp.einsum('dts,dtk->dsk', placed, low(normed_two).reshape(DEVICES, TOK_DEV, D), precision=highest)
        dispatched = low_back(dispatched)
        expert_rows = dispatched.reshape(DEVICES, EXPERTS, CAP, D).transpose(1, 0, 2, 3)
        expert_rows = expert_rows.reshape(EXPERTS, DEVICES * CAP, D)

        def expert_apply(operands):
            rows_in, up_one, down_one = operands
            hidden_pre = low_back(full_dot(rows_in, up_one))
            hidden = low(gelu_tanh(hidden_pre))
            return low(low_back(full_dot(hidden, down_one)))
        returned = lax.map(jax.checkpoint(expert_apply), (expert_rows, up_weight, down_weight))
        back_rows = returned.reshape(EXPERTS, DEVICES, CAP, D).transpose(1, 0, 2, 3)
        back_rows = back_rows.reshape(DEVICES, EXPERTS * CAP, D)
        expert_out = jnp.einsum('dts,dsk->dtk', placed, back_rows, precision=highest).reshape(TOKENS, D)
        return middle + gate_value[:, None] * expert_out
    primals = (tokens.astype(float_type), gain_mix, in_proj.astype(float_type), conv_weight, conv_bias, x_proj.astype(float_type), dt_proj.astype(float_type), dt_bias, a_log, skip_gain, out_proj.astype(float_type), gain_ffn, router, up_proj.astype(float_type), down_proj.astype(float_type))
    block_value, pullback = jax.vjp(forward, *primals)
    gradients = pullback(out_grad.astype(float_type))
    tokens_grad, gain_one_grad, in_grad, conv_w_grad, conv_b_grad, x_grad, dt_grad, shift_grad, log_grad, skip_grad, out_w_grad, gain_two_grad, router_grad, up_grad, down_grad = gradients
    return (block_value.astype(jnp.bfloat16), tokens_grad, jnp.concatenate([gain_one_grad, gain_two_grad]), router_grad.reshape(D * EXPERTS), in_grad, conv_w_grad, conv_b_grad, x_grad, dt_grad, shift_grad, log_grad, skip_grad, out_w_grad, up_grad, down_grad)
```

```python
import jax
import jax.numpy as jnp
from jax import lax
from jax.experimental import pallas as pl
from jax.experimental.pallas import tpu as pltpu
from jax.sharding import PartitionSpec as P

DT_RANK = 72
CONV = 4
STATE = 16
SEGMENTS = 8
LANES = 128
RESET = 1e30
LN2 = 0.6931471805599453


def spread_columns(target, source, staging, steps):
    rows = source.shape[0]
    for n in range(STATE):
        staging[...] = jnp.broadcast_to(source[:, n : n + 1], (rows, LANES))

        @pl.loop(0, steps)
        def _(i, n=n):
            target[i, n] = staging[pl.ds(i, SEGMENTS, stride=steps), :]


def spread_flags(target, source, staging, steps):
    staging[...] = jnp.broadcast_to(source[...] * RESET, (source.shape[0], LANES))

    @pl.loop(0, steps)
    def _(i):
        target[i] = staging[pl.ds(i, SEGMENTS, stride=steps), :]


def spread_rates(target, rates):
    for n in range(STATE):
        target[n] = jnp.broadcast_to(rates[n : n + 1, :], (SEGMENTS, LANES))


def ends_kernel(x, dt, in_map, starts, rates, ends_ex, cum_ex, end_all, cum_all,
                in_wide, big, staging, rate_wide, end_scr, sum_scr):
    steps = x.shape[0] // SEGMENTS

    @pl.when(pl.program_id(0) == 0)
    def _():
        spread_columns(in_wide, in_map, staging, steps)
        spread_flags(big, starts, staging, steps)

    spread_rates(rate_wide, rates)

    def step(i, carry):
        total, states = carry[0], carry[1:]
        rows = pl.ds(i, SEGMENTS, stride=steps)
        stride = dt[rows, :]
        driven = stride * x[rows, :]
        stride = stride + big[i]
        new = [total + stride]
        for n in range(STATE):
            new.append(jnp.exp2(stride * rate_wide[n]) * states[n] + driven * in_wide[i, n])
        return tuple(new)

    zero = jnp.zeros((SEGMENTS, LANES), jnp.float32)
    done = lax.fori_loop(0, steps, step, (zero,) * (STATE + 1), unroll=2)
    sum_scr[...] = done[0]
    for n in range(STATE):
        end_scr[n * SEGMENTS : (n + 1) * SEGMENTS, :] = done[1 + n]
    state = jnp.zeros((STATE, LANES), jnp.float32)
    cum = jnp.zeros((1, LANES), jnp.float32)
    for s in range(SEGMENTS):
        ends_ex[s * STATE : (s + 1) * STATE, :] = state
        cum_ex[s : s + 1, :] = cum
        own = sum_scr[s : s + 1, :]
        state = jnp.exp2(own * rates[...]) * state + end_scr[pl.ds(s, STATE, stride=SEGMENTS), :]
        cum = cum + own
    end_all[...] = state
    cum_all[...] = cum


def outputs_kernel(x, dt, in_map, out_map, starts, rates, ends_ex, cum_ex, entering, skip, gate,
                   scan_out, gated, in_wide, out_wide, big, staging, rate_wide):
    steps = x.shape[0] // SEGMENTS

    @pl.when(pl.program_id(0) == 0)
    def _():
        spread_columns(in_wide, in_map, staging, steps)
        spread_columns(out_wide, out_map, staging, steps)
        spread_flags(big, starts, staging, steps)

    spread_rates(rate_wide, rates)
    cum = cum_ex[...]
    opening = tuple(
        jnp.exp2(cum * rate_wide[n]) * entering[n : n + 1, :]
        + ends_ex[pl.ds(n, SEGMENTS, stride=STATE), :]
        for n in range(STATE)
    )

    def step(i, states):
        rows = pl.ds(i, SEGMENTS, stride=steps)
        stride = dt[rows, :]
        driven = stride * x[rows, :]
        stride = stride + big[i]
        new, total = [], None
        for n in range(STATE):
            state = jnp.exp2(stride * rate_wide[n]) * states[n] + driven * in_wide[i, n]
            new.append(state)
            term = state * out_wide[i, n]
            total = term if total is None else total + term
        scan_out[rows, :] = total
        return tuple(new)

    lax.fori_loop(0, steps, step, opening, unroll=2)
    value = scan_out[...] + skip[...] * x[...]
    scan_out[...] = value
    gated[...] = (value * jax.nn.silu(gate[...])).astype(gated.dtype)


def adjoint_kernel(gated_grad, gate, scan_out, dt, out_map, starts, rates,
                   scan_grad, gate_grad, adj_ex, cum_ex, adj_all,
                   out_wide, big, staging, rate_wide, end_scr, sum_scr):
    steps = dt.shape[0] // SEGMENTS

    @pl.when(pl.program_id(0) == 0)
    def _():
        spread_columns(out_wide, out_map, staging, steps)
        spread_flags(big, starts, staging, steps)

    spread_rates(rate_wide, rates)
    incoming = gated_grad[...]
    gate_in = gate[...]
    chance = jax.nn.sigmoid(gate_in)
    scan_grad[...] = incoming * (gate_in * chance)
    gate_grad[...] = (
        incoming * scan_out[...] * (chance * (1.0 + gate_in * (1.0 - chance)))
    ).astype(gate_grad.dtype)

    def step(k, carry):
        i = steps - 1 - k
        total, tails = carry[0], carry[1:]
        rows = pl.ds(i, SEGMENTS, stride=steps)
        grad = scan_grad[rows, :]
        stride = dt[rows, :] + big[i]
        new = [total + stride]
        for n in range(STATE):
            new.append(jnp.exp2(stride * rate_wide[n]) * (grad * out_wide[i, n] + tails[n]))
        return tuple(new)

    zero = jnp.zeros((SEGMENTS, LANES), jnp.float32)
    done = lax.fori_loop(0, steps, step, (zero,) * (STATE + 1), unroll=2)
    sum_scr[...] = done[0]
    for n in range(STATE):
        end_scr[n * SEGMENTS : (n + 1) * SEGMENTS, :] = done[1 + n]
    tail = jnp.zeros((STATE, LANES), jnp.float32)
    cum = jnp.zeros((1, LANES), jnp.float32)
    for s in reversed(range(SEGMENTS)):
        adj_ex[s * STATE : (s + 1) * STATE, :] = tail
        cum_ex[s : s + 1, :] = cum
        own = sum_scr[s : s + 1, :]
        tail = jnp.exp2(own * rates[...]) * tail + end_scr[pl.ds(s, STATE, stride=SEGMENTS), :]
        cum = cum + own
    adj_all[...] = tail


def grads_kernel(x, dt, in_map, out_map, starts, rates, ends_ex, cum_ex, entering, skip,
                 scan_grad, adj_ex, back_cum_ex, returning,
                 x_grad, dt_grad, in_grad, out_grad, log_grad, skip_grad,
                 in_wide, out_wide, big, staging, rate_wide, kept, log_scr):
    steps = x.shape[0] // SEGMENTS

    @pl.when(pl.program_id(0) == 0)
    def _():
        spread_columns(in_wide, in_map, staging, steps)
        spread_columns(out_wide, out_map, staging, steps)
        spread_flags(big, starts, staging, steps)
        in_grad[...] = jnp.zeros_like(in_grad)
        out_grad[...] = jnp.zeros_like(out_grad)

    spread_rates(rate_wide, rates)
    cum = cum_ex[...]
    opening = tuple(
        jnp.exp2(cum * rate_wide[n]) * entering[n : n + 1, :]
        + ends_ex[pl.ds(n, SEGMENTS, stride=STATE), :]
        for n in range(STATE)
    )

    def forward(i, states):
        rows = pl.ds(i, SEGMENTS, stride=steps)
        stride = dt[rows, :]
        driven = stride * x[rows, :]
        stride = stride + big[i]
        new = []
        for n in range(STATE):
            remain = jnp.exp2(stride * rate_wide[n]) * states[n]
            kept[i, n] = remain
            new.append(remain + driven * in_wide[i, n])
        return tuple(new)

    lax.fori_loop(0, steps, forward, opening, unroll=2)

    back_cum = back_cum_ex[...]
    tails = tuple(
        jnp.exp2(back_cum * rate_wide[n]) * returning[n : n + 1, :]
        + adj_ex[pl.ds(n, SEGMENTS, stride=STATE), :]
        for n in range(STATE)
    )
    zero = jnp.zeros((SEGMENTS, LANES), jnp.float32)
    for n in range(STATE):
        log_scr[n] = zero

    def backward(k, tails):
        i = steps - 1 - k
        rows = pl.ds(i, SEGMENTS, stride=steps)
        stride = dt[rows, :]
        value = x[rows, :]
        driven = stride * value
        grad = scan_grad[rows, :]
        marked = stride + big[i]
        new = []
        drive_sum, rate_sum = None, None
        for n in range(STATE):
            rate = rate_wide[n]
            in_n = in_wide[i, n]
            adjoint = grad * out_wide[i, n] + tails[n]
            remain = kept[i, n]
            out_grad[i, n] += grad * (remain + driven * in_n)
            in_grad[i, n] += adjoint * driven
            drive = adjoint * in_n
            touched = adjoint * remain
            slope = touched * rate
            log_scr[n] += touched * stride
            drive_sum = drive if drive_sum is None else drive_sum + drive
            rate_sum = slope if rate_sum is None else rate_sum + slope
            new.append(jnp.exp2(marked * rate) * adjoint)
        x_grad[rows, :] = stride * drive_sum
        dt_grad[rows, :] = value * drive_sum + LN2 * rate_sum
        return tuple(new)

    lax.fori_loop(0, steps, backward, tails)
    for n in range(STATE):
        log_grad[n : n + 1, :] = (
            jnp.sum(log_scr[n], axis=0, keepdims=True) * rates[n : n + 1, :] * LN2
        )
    skip_grad[...] = jnp.sum(scan_grad[...] * x[...], axis=0, keepdims=True)
    x_grad[...] += skip[...] * scan_grad[...]


def tile(rows):
    return pl.BlockSpec((rows, LANES), lambda j: (0, j))


def whole(shape):
    return pl.BlockSpec(shape, lambda j: (0,) * len(shape))


def shape_of(rows, width, dtype=jnp.float32):
    return jax.ShapeDtypeStruct((rows, width), dtype)


PARAMS = pltpu.CompilerParams(
    dimension_semantics=("arbitrary",), vmem_limit_bytes=56 * 1024 * 1024
)
WIDE = lambda steps: pltpu.VMEM((steps, STATE, SEGMENTS, LANES), jnp.float32)
FLAG = lambda steps: pltpu.VMEM((steps, SEGMENTS, LANES), jnp.float32)
BLOCK = lambda rows: pltpu.VMEM((rows, LANES), jnp.float32)
RATE = pltpu.VMEM((STATE, SEGMENTS, LANES), jnp.float32)


def scan_ends(x, dt, in_map, starts, rates):
    rows, width = x.shape
    steps = rows // SEGMENTS
    return pl.pallas_call(
        ends_kernel,
        grid=(width // LANES,),
        in_specs=[tile(rows), tile(rows), whole((rows, STATE)), whole((rows, 1)), tile(STATE)],
        out_specs=[tile(SEGMENTS * STATE), tile(SEGMENTS), tile(STATE), tile(1)],
        out_shape=[shape_of(SEGMENTS * STATE, width), shape_of(SEGMENTS, width),
                   shape_of(STATE, width), shape_of(1, width)],
        scratch_shapes=[WIDE(steps), FLAG(steps), BLOCK(rows), RATE, BLOCK(SEGMENTS * STATE),
                        BLOCK(SEGMENTS)],
        compiler_params=PARAMS, name="scan_ends",
    )(x, dt, in_map, starts, rates)


def scan_outputs(x, dt, in_map, out_map, starts, rates, ends_ex, cum_ex, entering, skip, gate):
    rows, width = x.shape
    steps = rows // SEGMENTS
    return pl.pallas_call(
        outputs_kernel,
        grid=(width // LANES,),
        in_specs=[tile(rows), tile(rows), whole((rows, STATE)), whole((rows, STATE)),
                  whole((rows, 1)), tile(STATE), tile(SEGMENTS * STATE), tile(SEGMENTS),
                  tile(STATE), tile(1), tile(rows)],
        out_specs=[tile(rows), tile(rows)],
        out_shape=[shape_of(rows, width), shape_of(rows, width, jnp.bfloat16)],
        scratch_shapes=[WIDE(steps), WIDE(steps), FLAG(steps), BLOCK(rows), RATE],
        compiler_params=PARAMS, name="scan_outputs",
    )(x, dt, in_map, out_map, starts, rates, ends_ex, cum_ex, entering, skip, gate)


def scan_adjoints(gated_grad, gate, scan_out, dt, out_map, starts, rates):
    rows, width = dt.shape
    steps = rows // SEGMENTS
    return pl.pallas_call(
        adjoint_kernel,
        grid=(width // LANES,),
        in_specs=[tile(rows), tile(rows), tile(rows), tile(rows), whole((rows, STATE)),
                  whole((rows, 1)), tile(STATE)],
        out_specs=[tile(rows), tile(rows), tile(SEGMENTS * STATE), tile(SEGMENTS), tile(STATE)],
        out_shape=[shape_of(rows, width), shape_of(rows, width, jnp.bfloat16),
                   shape_of(SEGMENTS * STATE, width), shape_of(SEGMENTS, width),
                   shape_of(STATE, width)],
        scratch_shapes=[WIDE(steps), FLAG(steps), BLOCK(rows), RATE, BLOCK(SEGMENTS * STATE),
                        BLOCK(SEGMENTS)],
        compiler_params=PARAMS, name="scan_adjoints",
    )(gated_grad, gate, scan_out, dt, out_map, starts, rates)


def scan_grads(x, dt, in_map, out_map, starts, rates, ends_ex, cum_ex, entering, skip,
               scan_grad, adj_ex, back_cum_ex, returning):
    rows, width = x.shape
    steps = rows // SEGMENTS
    wide_shape = (steps, STATE, SEGMENTS, LANES)
    return pl.pallas_call(
        grads_kernel,
        grid=(width // LANES,),
        in_specs=[tile(rows), tile(rows), whole((rows, STATE)), whole((rows, STATE)),
                  whole((rows, 1)), tile(STATE), tile(SEGMENTS * STATE), tile(SEGMENTS),
                  tile(STATE), tile(1), tile(rows), tile(SEGMENTS * STATE), tile(SEGMENTS),
                  tile(STATE)],
        out_specs=[tile(rows), tile(rows), whole(wide_shape), whole(wide_shape), tile(STATE),
                   tile(1)],
        out_shape=[shape_of(rows, width), shape_of(rows, width),
                   jax.ShapeDtypeStruct(wide_shape, jnp.float32),
                   jax.ShapeDtypeStruct(wide_shape, jnp.float32),
                   shape_of(STATE, width), shape_of(1, width)],
        scratch_shapes=[WIDE(steps), WIDE(steps), FLAG(steps), BLOCK(rows), RATE, WIDE(steps),
                        RATE],
        compiler_params=PARAMS, name="scan_grads",
    )(x, dt, in_map, out_map, starts, rates, ends_ex, cum_ex, entering, skip, scan_grad, adj_ex,
      back_cum_ex, returning)


def fold_map(wide):
    summed = jnp.sum(wide, axis=3)
    return jnp.transpose(summed, (2, 0, 1)).reshape(-1, STATE)


norm_epsilon = 1e-05
highest = lax.Precision.HIGHEST


def shifted_2(block, axis, distance):
    devices = range(lax.axis_size(axis))
    route = [(i - distance, i) for i in devices if i - distance in devices]
    return lax.ppermute(block, axis, route)


def state_before(cum, end, rates, axis):
    count, mine = lax.axis_size(axis), lax.axis_index(axis)
    cums = lax.all_gather(cum, axis)
    ends = lax.all_gather(end.astype(jnp.bfloat16), axis).astype(jnp.float32)
    state = jnp.zeros_like(end)
    for d in range(count - 1):
        state = jnp.where(d < mine, jnp.exp2(cums[d] * rates) * state + ends[d], state)
    return state, cums


def state_after(cums, tail, rates, axis):
    count, mine = lax.axis_size(axis), lax.axis_index(axis)
    tails = lax.all_gather(tail.astype(jnp.bfloat16), axis).astype(jnp.float32)
    state = jnp.zeros_like(tail)
    for d in reversed(range(1, count)):
        state = jnp.where(d > mine, jnp.exp2(cums[d] * rates) * state + tails[d], state)
    return state


def rms_scale(values):
    return lax.rsqrt(jnp.mean(values * values, axis=1, keepdims=True) + norm_epsilon)


def scaled_norm(values, gain_row):
    return values * rms_scale(values) * gain_row[None, :]


def gelu_tanh(values):
    return jax.nn.gelu(values, approximate=True)


def conv_mix(x_inner, halo_rows, halo_flags, start_flags, conv_w, conv_b):
    tap_count = conv_w.shape[0]
    length = x_inner.shape[0]
    extended = jnp.concatenate([halo_rows, x_inner], axis=0)
    flag_line = jnp.concatenate([halo_flags, start_flags], axis=0)
    result = conv_b[None, :] + conv_w[tap_count - 1][None, :] * x_inner
    survive = jnp.ones((length,), jnp.float32)
    for offset in range(1, tap_count):
        survive = survive * (1.0 - flag_line[tap_count - offset : tap_count - offset + length])
        shifted = extended[tap_count - 1 - offset : tap_count - 1 - offset + length]
        result = result + conv_w[tap_count - 1 - offset][None, :] * shifted * survive[:, None]
    return jax.nn.silu(result)


def delta_apply(step_pre, bias_row, real_rows):
    return jax.nn.softplus(step_pre + bias_row[None, :]) * real_rows[:, None]


def body(
    tokens,
    starts,
    counts,
    routes,
    slot_index,
    gain_mix,
    in_proj,
    conv_weight,
    conv_bias,
    x_proj,
    dt_proj,
    dt_bias,
    a_log,
    skip_gain,
    out_proj,
    gain_ffn,
    router,
    up_proj,
    down_proj,
    out_grad,
):
    float_type = jnp.float32
    low_type = jnp.bfloat16
    rows_first = (((0,), (0,)), ((), ()))
    last_dims = (((1,), (1,)), ((), ()))
    length = tokens.shape[0]
    model_width = tokens.shape[1]
    inner_width = conv_bias.shape[0]
    experts = router.shape[1]
    capacity = 5 * length // (4 * experts)
    edge_start = counts[0] - (CONV - 1)
    start_flags = starts.astype(float_type)
    real_rows = (jnp.arange(length, dtype=jnp.int32) < counts[0]).astype(float_type)
    tokens_float = tokens.astype(float_type)
    normed_one, norm_one_back = jax.vjp(scaled_norm, tokens_float, gain_mix)
    normed_low = normed_one.astype(low_type)
    projected = jnp.dot(normed_low, in_proj, preferred_element_type=float_type)
    inner_x = projected[:, :inner_width]
    inner_gate = projected[:, inner_width:]
    edge_rows = lax.dynamic_slice_in_dim(inner_x, edge_start, CONV - 1, 0)
    edge_flags = lax.dynamic_slice_in_dim(start_flags, edge_start, CONV - 1, 0)
    halo_rows, halo_flags = shifted_2((edge_rows, edge_flags), "hs", 1)

    def conv_part(x_part, rows_part, weight_part, bias_part):
        return conv_mix(x_part, rows_part, halo_flags, start_flags, weight_part, bias_part)

    mixer_in, conv_back = jax.vjp(conv_part, inner_x, halo_rows, conv_weight, conv_bias)
    mixer_low = mixer_in.astype(low_type)
    small_proj = jnp.dot(mixer_low, x_proj, preferred_element_type=float_type)
    rank_low = small_proj[:, :DT_RANK].astype(low_type)
    step_pre = jnp.dot(rank_low, dt_proj, preferred_element_type=float_type)
    input_map = small_proj[:, DT_RANK : DT_RANK + STATE]
    output_map = small_proj[:, DT_RANK + STATE :]

    def step_part(pre_part, bias_part):
        return delta_apply(pre_part, bias_part, real_rows)

    step_size, step_back = jax.vjp(step_part, step_pre, dt_bias)

    start_column = start_flags[:, None]
    rates = -(jnp.exp(a_log) / LN2).T
    skip_row = skip_gain[None, :]
    ends_ex, cum_ex, end_all, cum_all = scan_ends(
        mixer_in, step_size, input_map, start_column, rates
    )
    entering, cums = state_before(cum_all, end_all, rates, "hs")
    scan_out, gated_low = scan_outputs(
        mixer_in,
        step_size,
        input_map,
        output_map,
        start_column,
        rates,
        ends_ex,
        cum_ex,
        entering,
        skip_row,
        inner_gate,
    )
    mixer_out = jnp.dot(gated_low, out_proj, preferred_element_type=float_type)
    middle = tokens_float + mixer_out * real_rows[:, None]
    normed_two, norm_two_back = jax.vjp(scaled_norm, middle, gain_ffn)
    router_probs = jax.nn.softmax(
        jnp.dot(normed_two, router, precision=highest, preferred_element_type=float_type), axis=1
    )
    chosen = (routes[:, None] == jnp.arange(experts, dtype=jnp.int32)[None, :]).astype(float_type)
    gate_value = jnp.sum(router_probs * chosen, axis=1)
    column = routes * capacity + slot_index
    placed = (
        (column[:, None] == jnp.arange(experts * capacity, dtype=jnp.int32)[None, :])
        & (slot_index[:, None] >= 0)
    ).astype(low_type)
    dispatched = lax.dot_general(
        placed, normed_two.astype(low_type), rows_first, preferred_element_type=float_type
    ).astype(low_type)
    arrived = lax.all_to_all(
        dispatched.reshape(experts, capacity, model_width),
        "ep",
        split_axis=0,
        concat_axis=0,
        tiled=True,
    )
    gathered_rows = lax.all_gather(arrived, "hs", axis=0, tiled=True).reshape(-1, model_width)
    hidden_pre = jnp.dot(gathered_rows, up_proj[0], preferred_element_type=float_type)
    hidden, gelu_back = jax.vjp(gelu_tanh, hidden_pre)
    hidden_low = hidden.astype(low_type)
    partial_out = jnp.dot(hidden_low, down_proj[0], preferred_element_type=float_type)
    returned = lax.psum_scatter(partial_out, "hs", scatter_dimension=0, tiled=True).astype(low_type)
    home_rows = lax.all_to_all(
        returned.reshape(-1, capacity, model_width), "ep", split_axis=0, concat_axis=0, tiled=True
    )
    expert_out = jnp.dot(
        placed,
        home_rows.reshape(experts * capacity, model_width),
        preferred_element_type=float_type,
    )
    block_out = (middle + gate_value[:, None] * expert_out).astype(low_type)
    grad_out = out_grad.astype(float_type)
    gate_grad = jnp.sum(grad_out * expert_out, axis=1)
    token_grad = grad_out * gate_value[:, None]
    placed_full = placed.astype(float_type)
    rows_grad = lax.dot_general(
        placed_full, token_grad, rows_first, precision=highest, preferred_element_type=float_type
    ).astype(low_type)
    arrived_grad = lax.all_to_all(
        rows_grad.reshape(experts, capacity, model_width),
        "ep",
        split_axis=0,
        concat_axis=0,
        tiled=True,
    )
    gathered_grad = lax.all_gather(arrived_grad, "hs", axis=0, tiled=True).reshape(-1, model_width)
    hidden_grad = lax.dot_general(
        gathered_grad, down_proj[0], last_dims, preferred_element_type=float_type
    )
    down_grad = lax.dot_general(
        hidden_low, gathered_grad, rows_first, preferred_element_type=float_type
    )
    pre_grad = gelu_back(hidden_grad)[0].astype(low_type)
    up_grad = lax.dot_general(
        gathered_rows, pre_grad, rows_first, preferred_element_type=float_type
    )
    partial_grad = lax.dot_general(
        pre_grad, up_proj[0], last_dims, preferred_element_type=float_type
    )
    own_grad = (
        lax.psum_scatter(partial_grad.astype(jnp.bfloat16), "hs", scatter_dimension=0, tiled=True)
        .astype(jnp.float32)
        .astype(low_type)
    )
    home_grad = lax.all_to_all(
        own_grad.reshape(-1, capacity, model_width), "ep", split_axis=0, concat_axis=0, tiled=True
    )
    normed_two_grad = jnp.dot(
        placed_full,
        home_grad.reshape(experts * capacity, model_width).astype(float_type),
        precision=highest,
        preferred_element_type=float_type,
    )
    logit_grad = router_probs * gate_grad[:, None] * (chosen - gate_value[:, None])
    router_grad = lax.dot_general(
        normed_two, logit_grad, rows_first, precision=highest, preferred_element_type=float_type
    )
    normed_two_grad = normed_two_grad + lax.dot_general(
        logit_grad, router, last_dims, precision=highest, preferred_element_type=float_type
    )
    middle_norm_grad, gain_ffn_grad = norm_two_back(normed_two_grad)
    middle_grad = grad_out + middle_norm_grad
    mixer_grad = (middle_grad * real_rows[:, None]).astype(low_type)
    out_proj_grad = lax.dot_general(
        gated_low, mixer_grad, rows_first, preferred_element_type=float_type
    )
    gated_grad = lax.dot_general(mixer_grad, out_proj, last_dims, preferred_element_type=float_type)
    scan_grad, gate_pre_low, adj_ex, back_cum_ex, adj_all = scan_adjoints(
        gated_grad, inner_gate, scan_out, step_size, output_map, start_column, rates
    )
    returning = state_after(cums, adj_all, rates, "hs")
    scan_in_grad, size_grad, in_wide_grad, out_wide_grad, log_grad, skip_grad = scan_grads(
        mixer_in,
        step_size,
        input_map,
        output_map,
        start_column,
        rates,
        ends_ex,
        cum_ex,
        entering,
        skip_row,
        scan_grad,
        adj_ex,
        back_cum_ex,
        returning,
    )
    pre_step_grad, dt_bias_grad = step_back(size_grad)
    pre_step_low = pre_step_grad.astype(low_type)
    dt_proj_grad = lax.dot_general(
        pre_step_low, rank_low, rows_first, preferred_element_type=float_type
    )
    rank_grad = lax.dot_general(pre_step_low, dt_proj, last_dims, preferred_element_type=float_type)
    small_grad = jnp.concatenate(
        [rank_grad, fold_map(in_wide_grad), fold_map(out_wide_grad)], axis=1
    ).astype(low_type)
    x_proj_grad = lax.dot_general(
        mixer_low, small_grad, rows_first, preferred_element_type=float_type
    )
    mixer_in_grad = (
        scan_in_grad
        + lax.dot_general(small_grad, x_proj, last_dims, preferred_element_type=float_type)
    )
    inner_x_grad, halo_grad, conv_weight_grad, conv_bias_grad = conv_back(mixer_in_grad)
    edge_grad = shifted_2(halo_grad, "hs", -1)
    edge_total = lax.dynamic_slice_in_dim(inner_x_grad, edge_start, CONV - 1, 0) + edge_grad
    inner_x_grad = lax.dynamic_update_slice_in_dim(inner_x_grad, edge_total, edge_start, 0)
    projected_grad = jnp.concatenate([inner_x_grad.astype(low_type), gate_pre_low], axis=1)
    in_proj_grad = lax.dot_general(
        normed_low, projected_grad, rows_first, preferred_element_type=float_type
    )
    normed_one_grad = lax.dot_general(
        projected_grad, in_proj, last_dims, preferred_element_type=float_type
    )
    tokens_norm_grad, gain_mix_grad = norm_one_back(normed_one_grad)
    tokens_grad = middle_grad + tokens_norm_grad
    gains_local = jnp.concatenate([gain_mix_grad, gain_ffn_grad])
    columns = [
        x_proj_grad,
        dt_proj_grad,
        log_grad.T,
        conv_weight_grad.T,
        conv_bias_grad[:, None],
        dt_bias_grad[:, None],
        skip_grad.T,
        gains_local[:, None],
        router_grad.reshape(inner_width, -1),
    ]
    packed = jnp.concatenate(columns, axis=1)
    summed = lax.psum_scatter(packed, ("ep", "hs"), scatter_dimension=0, tiled=True)
    pieces, at = [], 0
    for column in columns:
        pieces.append(summed[:, at : at + column.shape[1]])
        at += column.shape[1]
    x_proj_sum = pieces[0]
    dt_proj_sum = pieces[1].T
    a_log_sum = pieces[2]
    conv_weight_sum = pieces[3].T
    conv_bias_sum, dt_bias_sum, skip_sum, gains_sum = [p[:, 0] for p in pieces[4:8]]
    router_sum = pieces[8].reshape(-1)
    in_proj_sum = lax.psum_scatter(
        in_proj_grad.astype(low_type), ("ep", "hs"), scatter_dimension=1, tiled=True
    ).astype(float_type)
    out_proj_sum = lax.psum_scatter(
        out_proj_grad.astype(low_type), ("ep", "hs"), scatter_dimension=0, tiled=True
    ).astype(float_type)
    return (
        block_out,
        tokens_grad,
        gains_sum,
        router_sum,
        in_proj_sum,
        conv_weight_sum,
        conv_bias_sum,
        x_proj_sum,
        dt_proj_sum,
        dt_bias_sum,
        a_log_sum,
        skip_sum,
        out_proj_sum,
        up_grad[None],
        down_grad[None],
    )


def solution(mesh):
    return jax.shard_map(
        body,
        mesh=mesh,
        in_specs=(
            P(("ep", "hs"), None),
            P(("ep", "hs")),
            P(("ep", "hs")),
            P(("ep", "hs")),
            P(("ep", "hs")),
            P(),
            P(),
            P(),
            P(),
            P(),
            P(),
            P(),
            P(),
            P(),
            P(),
            P(),
            P(),
            P("ep", None, "hs"),
            P("ep", "hs", None),
            P(("ep", "hs"), None),
        ),
        out_specs=(
            P(("ep", "hs"), None),
            P(("ep", "hs"), None),
            P(("ep", "hs")),
            P(("ep", "hs")),
            P(None, ("ep", "hs")),
            P(None, ("ep", "hs")),
            P(("ep", "hs")),
            P(("ep", "hs"), None),
            P(None, ("ep", "hs")),
            P(("ep", "hs")),
            P(("ep", "hs"), None),
            P(("ep", "hs")),
            P(("ep", "hs"), None),
            P("ep", None, "hs"),
            P("ep", "hs", None),
        ),
        check_vma=False,
    )
```

```python
import jax
import jax.numpy as jnp
from jax import lax
from jax.experimental import pallas as pl
from jax.experimental.pallas import tpu as pltpu
from jax.sharding import PartitionSpec as P

DT_RANK = 72
CONV = 4
STATE = 16
SEGMENTS = 8
LANES = 128
TILES = 3
RESET = 1e30
LN2 = 0.6931471805599453


def widened(values):
    shaped = values.reshape(SEGMENTS, -1, values.shape[1])
    shaped = jnp.transpose(shaped, (1, 2, 0))[..., None]
    return jnp.broadcast_to(shaped, shaped.shape[:3] + (LANES,))


def each_tile(work):
    @pl.loop(0, TILES)
    def _(k):
        work(pl.ds(pl.multiple_of(k * LANES, LANES), LANES))


def spread_rates(target, rates, lanes):
    for n in range(STATE):
        target[n] = jnp.broadcast_to(rates[n : n + 1, lanes], (SEGMENTS, LANES))


def ends_kernel(x, dt, in_wide, big, rates, ends_ex, cum_ex, end_all, cum_all,
                rate_wide, end_scr, sum_scr, x_scr, dt_scr):
    steps = x.shape[0] // SEGMENTS

    def work(lanes):
        spread_rates(rate_wide, rates, lanes)
        x_scr[...] = x[:, lanes]
        dt_scr[...] = dt[:, lanes]

        def step(i, carry):
            total, states = carry[0], carry[1:]
            rows = pl.ds(i, SEGMENTS, stride=steps)
            stride = dt_scr[rows, :]
            driven = stride * x_scr[rows, :]
            stride = stride + big[i, 0]
            new = [total + stride]
            for n in range(STATE):
                new.append(jnp.exp2(stride * rate_wide[n]) * states[n] + driven * in_wide[i, n])
            return tuple(new)

        zero = jnp.zeros((SEGMENTS, LANES), jnp.float32)
        done = lax.fori_loop(0, steps, step, (zero,) * (STATE + 1), unroll=4)
        sum_scr[...] = done[0]
        for n in range(STATE):
            end_scr[n * SEGMENTS : (n + 1) * SEGMENTS, :] = done[1 + n]
        state = jnp.zeros((STATE, LANES), jnp.float32)
        cum = jnp.zeros((1, LANES), jnp.float32)
        for s in range(SEGMENTS):
            ends_ex[s * STATE : (s + 1) * STATE, lanes] = state
            cum_ex[s : s + 1, lanes] = cum
            own = sum_scr[s : s + 1, :]
            state = (
                jnp.exp2(own * rates[:, lanes]) * state
                + end_scr[pl.ds(s, STATE, stride=SEGMENTS), :]
            )
            cum = cum + own
        end_all[:, lanes] = state
        cum_all[:, lanes] = cum

    each_tile(work)


def opening_states(cum, rate_wide, entering, ends_ex, end_scr, lanes):
    end_scr[...] = ends_ex[:, lanes]
    return tuple(
        jnp.exp2(cum * rate_wide[n]) * entering[n : n + 1, lanes]
        + end_scr[pl.ds(n, SEGMENTS, stride=STATE), :]
        for n in range(STATE)
    )


def outputs_kernel(x, dt, in_wide, out_wide, big, rates, ends_ex, cum_ex, entering, skip, gate,
                   scan_out, gated, rate_wide, end_scr, x_scr, dt_scr, out_scr):
    steps = x.shape[0] // SEGMENTS

    def work(lanes):
        spread_rates(rate_wide, rates, lanes)
        x_scr[...] = x[:, lanes]
        dt_scr[...] = dt[:, lanes]
        opening = opening_states(cum_ex[:, lanes], rate_wide, entering, ends_ex, end_scr, lanes)

        def step(i, states):
            rows = pl.ds(i, SEGMENTS, stride=steps)
            stride = dt_scr[rows, :]
            driven = stride * x_scr[rows, :]
            stride = stride + big[i, 0]
            new, total = [], None
            for n in range(STATE):
                state = jnp.exp2(stride * rate_wide[n]) * states[n] + driven * in_wide[i, n]
                new.append(state)
                term = state * out_wide[i, n]
                total = term if total is None else total + term
            out_scr[rows, :] = total
            return tuple(new)

        lax.fori_loop(0, steps, step, opening, unroll=4)
        value = out_scr[...] + skip[:, lanes] * x_scr[...]
        scan_out[:, lanes] = value
        gated[:, lanes] = (value * jax.nn.silu(gate[:, lanes])).astype(gated.dtype)

    each_tile(work)


def adjoint_kernel(gated_grad, gate, scan_out, dt, out_wide, big, rates,
                   scan_grad, gate_grad, adj_ex, cum_ex, adj_all,
                   rate_wide, end_scr, sum_scr, grad_scr, dt_scr):
    steps = dt.shape[0] // SEGMENTS

    def work(lanes):
        spread_rates(rate_wide, rates, lanes)
        incoming = gated_grad[:, lanes]
        gate_in = gate[:, lanes]
        chance = jax.nn.sigmoid(gate_in)
        moved = incoming * (gate_in * chance)
        scan_grad[:, lanes] = moved
        grad_scr[...] = moved
        dt_scr[...] = dt[:, lanes]
        gate_grad[:, lanes] = (
            incoming * scan_out[:, lanes] * (chance * (1.0 + gate_in * (1.0 - chance)))
        ).astype(gate_grad.dtype)

        def step(k, carry):
            i = steps - 1 - k
            total, tails = carry[0], carry[1:]
            rows = pl.ds(i, SEGMENTS, stride=steps)
            grad = grad_scr[rows, :]
            stride = dt_scr[rows, :] + big[i, 0]
            new = [total + stride]
            for n in range(STATE):
                new.append(jnp.exp2(stride * rate_wide[n]) * (grad * out_wide[i, n] + tails[n]))
            return tuple(new)

        zero = jnp.zeros((SEGMENTS, LANES), jnp.float32)
        done = lax.fori_loop(0, steps, step, (zero,) * (STATE + 1), unroll=4)
        sum_scr[...] = done[0]
        for n in range(STATE):
            end_scr[n * SEGMENTS : (n + 1) * SEGMENTS, :] = done[1 + n]
        tail = jnp.zeros((STATE, LANES), jnp.float32)
        cum = jnp.zeros((1, LANES), jnp.float32)
        for s in reversed(range(SEGMENTS)):
            adj_ex[s * STATE : (s + 1) * STATE, lanes] = tail
            cum_ex[s : s + 1, lanes] = cum
            own = sum_scr[s : s + 1, :]
            tail = (
                jnp.exp2(own * rates[:, lanes]) * tail
                + end_scr[pl.ds(s, STATE, stride=SEGMENTS), :]
            )
            cum = cum + own
        adj_all[:, lanes] = tail

    each_tile(work)


def grads_kernel(x, dt, in_wide, out_wide, big, rates, ends_ex, cum_ex, entering, skip,
                 scan_grad, adj_ex, back_cum_ex, returning,
                 x_grad, dt_grad, map_grad, log_grad, skip_grad,
                 rate_wide, kept, log_scr, end_scr, x_scr, dt_scr, grad_scr, x_out, dt_out):
    steps = x.shape[0] // SEGMENTS

    @pl.when(pl.program_id(0) == 0)
    def _():
        map_grad[...] = jnp.zeros_like(map_grad)

    def work(lanes):
        spread_rates(rate_wide, rates, lanes)
        x_scr[...] = x[:, lanes]
        dt_scr[...] = dt[:, lanes]
        opening = opening_states(cum_ex[:, lanes], rate_wide, entering, ends_ex, end_scr, lanes)

        def forward(i, states):
            rows = pl.ds(i, SEGMENTS, stride=steps)
            stride = dt_scr[rows, :]
            driven = stride * x_scr[rows, :]
            stride = stride + big[i, 0]
            new = []
            for n in range(STATE):
                remain = jnp.exp2(stride * rate_wide[n]) * states[n]
                kept[i, n] = remain
                new.append(remain + driven * in_wide[i, n])
            return tuple(new)

        lax.fori_loop(0, steps, forward, opening, unroll=4)
        tails = opening_states(back_cum_ex[:, lanes], rate_wide, returning, adj_ex, end_scr, lanes)
        zero = jnp.zeros((SEGMENTS, LANES), jnp.float32)
        for n in range(STATE):
            log_scr[n] = zero

        def backward(k, tails):
            i = steps - 1 - k
            rows = pl.ds(i, SEGMENTS, stride=steps)
            stride = dt_scr[rows, :]
            value = x_scr[rows, :]
            driven = stride * value
            grad = grad_scr[rows, :]
            marked = stride + big[i, 0]
            new = []
            drive_sum, rate_sum = None, None
            for n in range(STATE):
                rate = rate_wide[n]
                in_n = in_wide[i, n]
                adjoint = grad * out_wide[i, n] + tails[n]
                remain = kept[i, n]
                map_grad[1, i, n] += grad * (remain + driven * in_n)
                map_grad[0, i, n] += adjoint * driven
                drive = adjoint * in_n
                touched = adjoint * remain
                slope = touched * rate
                log_scr[n] += touched * stride
                drive_sum = drive if drive_sum is None else drive_sum + drive
                rate_sum = slope if rate_sum is None else rate_sum + slope
                new.append(jnp.exp2(marked * rate) * adjoint)
            x_out[rows, :] = stride * drive_sum
            dt_out[rows, :] = value * drive_sum + LN2 * rate_sum
            return tuple(new)

        grad_scr[...] = scan_grad[:, lanes]
        lax.fori_loop(0, steps, backward, tails, unroll=2)
        dt_grad[:, lanes] = dt_out[...]
        x_grad[:, lanes] = x_out[...] + skip[:, lanes] * grad_scr[...]
        skip_grad[:, lanes] = jnp.sum(grad_scr[...] * x_scr[...], axis=0, keepdims=True)
        for n in range(STATE):
            log_grad[n : n + 1, lanes] = (
                jnp.sum(log_scr[n], axis=0, keepdims=True) * rates[n : n + 1, lanes] * LN2
            )

    each_tile(work)


def tile(rows):
    return pl.BlockSpec((rows, TILES * LANES), lambda j: (0, j))


def whole(shape):
    return pl.BlockSpec(shape, lambda j: (0,) * len(shape))


def shape_of(rows, width, dtype=jnp.float32):
    return jax.ShapeDtypeStruct((rows, width), dtype)


PARAMS = pltpu.CompilerParams(
    dimension_semantics=("arbitrary",), vmem_limit_bytes=56 * 1024 * 1024
)
RATE = pltpu.VMEM((STATE, SEGMENTS, LANES), jnp.float32)
ENDS = pltpu.VMEM((SEGMENTS * STATE, LANES), jnp.float32)
SUMS = pltpu.VMEM((SEGMENTS, LANES), jnp.float32)


def call(kernel, waits, micros, **options):
    specs = options.pop("in_specs")

    def waiting(*refs):
        kernel(*refs[: len(specs)], *refs[len(specs) + len(waits) :])

    waiting.__name__ = options["name"]
    run = pl.pallas_call(
        waiting,
        in_specs=specs + [pl.BlockSpec(memory_space=pl.ANY)] * len(waits),
        compiler_params=PARAMS,
        cost_estimate=pl.CostEstimate(
            flops=0, bytes_accessed=micros * 3_000_000, transcendentals=0
        ),
        **options,
    )
    return lambda *operands: run(*operands, *waits)


def rows_of(rows):
    return pltpu.VMEM((rows, LANES), jnp.float32)


def scan_ends(x, dt, in_wide, big, rates, waits=()):
    rows, width = x.shape
    return call(
        ends_kernel,
        waits,
        15,
        grid=(width // (TILES * LANES),),
        in_specs=[tile(rows), tile(rows), whole(in_wide.shape), whole(big.shape), tile(STATE)],
        out_specs=[tile(SEGMENTS * STATE), tile(SEGMENTS), tile(STATE), tile(1)],
        out_shape=[shape_of(SEGMENTS * STATE, width), shape_of(SEGMENTS, width),
                   shape_of(STATE, width), shape_of(1, width)],
        scratch_shapes=[RATE, ENDS, SUMS, rows_of(rows), rows_of(rows)],
        name="scan_ends",
    )(x, dt, in_wide, big, rates)


def scan_outputs(x, dt, in_wide, out_wide, big, rates, ends_ex, cum_ex, entering, skip, gate, waits=()):
    rows, width = x.shape
    return call(
        outputs_kernel,
        waits,
        20,
        grid=(width // (TILES * LANES),),
        in_specs=[tile(rows), tile(rows), whole(in_wide.shape), whole(out_wide.shape),
                  whole(big.shape), tile(STATE), tile(SEGMENTS * STATE), tile(SEGMENTS),
                  tile(STATE), tile(1), tile(rows)],
        out_specs=[tile(rows), tile(rows)],
        out_shape=[shape_of(rows, width), shape_of(rows, width, jnp.bfloat16)],
        scratch_shapes=[RATE, ENDS] + [rows_of(rows)] * 3,
        name="scan_outputs",
    )(x, dt, in_wide, out_wide, big, rates, ends_ex, cum_ex, entering, skip, gate)


def scan_adjoints(gated_grad, gate, scan_out, dt, out_wide, big, rates, waits=()):
    rows, width = dt.shape
    return call(
        adjoint_kernel,
        waits,
        17,
        grid=(width // (TILES * LANES),),
        in_specs=[tile(rows), tile(rows), tile(rows), tile(rows), whole(out_wide.shape),
                  whole(big.shape), tile(STATE)],
        out_specs=[tile(rows), tile(rows), tile(SEGMENTS * STATE), tile(SEGMENTS), tile(STATE)],
        out_shape=[shape_of(rows, width), shape_of(rows, width, jnp.bfloat16),
                   shape_of(SEGMENTS * STATE, width), shape_of(SEGMENTS, width),
                   shape_of(STATE, width)],
        scratch_shapes=[RATE, ENDS, SUMS, rows_of(rows), rows_of(rows)],
        name="scan_adjoints",
    )(gated_grad, gate, scan_out, dt, out_wide, big, rates)


def scan_grads(x, dt, in_wide, out_wide, big, rates, ends_ex, cum_ex, entering, skip,
               scan_grad, adj_ex, back_cum_ex, returning, waits=()):
    rows, width = x.shape
    steps = rows // SEGMENTS
    wide_shape = (steps, STATE, SEGMENTS, LANES)
    return call(
        grads_kernel,
        waits,
        55,
        grid=(width // (TILES * LANES),),
        in_specs=[tile(rows), tile(rows), whole(in_wide.shape), whole(out_wide.shape),
                  whole(big.shape), tile(STATE), tile(SEGMENTS * STATE), tile(SEGMENTS),
                  tile(STATE), tile(1), tile(rows), tile(SEGMENTS * STATE), tile(SEGMENTS),
                  tile(STATE)],
        out_specs=[tile(rows), tile(rows), whole((2,) + wide_shape), tile(STATE), tile(1)],
        out_shape=[shape_of(rows, width), shape_of(rows, width),
                   jax.ShapeDtypeStruct((2,) + wide_shape, jnp.float32),
                   shape_of(STATE, width), shape_of(1, width)],
        scratch_shapes=[RATE, pltpu.VMEM(wide_shape, jnp.float32), RATE, ENDS]
        + [rows_of(rows)] * 5,
        name="scan_grads",
    )(x, dt, in_wide, out_wide, big, rates, ends_ex, cum_ex, entering, skip, scan_grad, adj_ex,
      back_cum_ex, returning)


def fold_maps(wide):
    summed = jnp.sum(wide, axis=4)
    return jnp.transpose(summed, (3, 1, 0, 2)).reshape(-1, 2 * STATE)


norm_epsilon = 1e-05
highest = lax.Precision.HIGHEST
ROWS_FIRST = (((0,), (0,)), ((), ()))
LAST_DIMS = (((1,), (1,)), ((), ()))


def shifted_2(block, axis, distance):
    devices = range(lax.axis_size(axis))
    route = [(i - distance, i) for i in devices if i - distance in devices]
    return lax.ppermute(block, axis, route)


def crossed(block, axis, mask):
    return lax.ppermute(block, axis, [(i, i ^ mask) for i in range(lax.axis_size(axis))])


def exchanged(blocks, axis):
    return [block if k == 0 else crossed(block, axis, k) for k, block in enumerate(blocks)]


def after(value, *others):
    return lax.optimization_barrier((value,) + others)[0]


def summed_shares(parts, axis):
    count, mine = lax.axis_size(axis), lax.axis_index(axis)
    total = lax.dynamic_index_in_dim(parts, mine, 0, False)
    for shift in range(1, count):
        share = lax.dynamic_index_in_dim(parts, lax.rem(mine + shift, count), 0, False)
        route = [(i, (i + shift) % count) for i in range(count)]
        total = total + lax.ppermute(share.astype(jnp.bfloat16), axis, route).astype(jnp.float32)
    return total


def state_before(cum, end, rates, axis):
    count, mine = lax.axis_size(axis), lax.axis_index(axis)
    first = lax.reduce_precision(cum, 8, 7)
    second = lax.reduce_precision(cum - first, 8, 7)
    sent = jnp.concatenate([end, first, second, cum - first - second], axis=0)
    got = lax.all_gather(sent.astype(jnp.bfloat16), axis).astype(jnp.float32)
    ends, terms = got[:, : end.shape[0]], got[:, end.shape[0] :]
    cums = jnp.sum(terms, axis=1, keepdims=True)
    state = jnp.zeros_like(end)
    for d in range(count - 1):
        state = jnp.where(d < mine, jnp.exp2(cums[d] * rates) * state + ends[d], state)
    return state, cums


def state_after(cums, tail, rates, axis):
    count, mine = lax.axis_size(axis), lax.axis_index(axis)
    tails = lax.all_gather(tail.astype(jnp.bfloat16), axis).astype(jnp.float32)
    state = jnp.zeros_like(tail)
    for d in reversed(range(1, count)):
        state = jnp.where(d > mine, jnp.exp2(cums[d] * rates) * state + tails[d], state)
    return state


def rms_scale(values):
    return lax.rsqrt(jnp.mean(values * values, axis=1, keepdims=True) + norm_epsilon)


def scaled_norm(values, gain_row):
    return values * rms_scale(values) * gain_row[None, :]


def gelu_tanh(values):
    return jax.nn.gelu(values, approximate=True)


def conv_mix(x_inner, halo_rows, start_flags, conv_w, conv_b):
    tap_count = conv_w.shape[0]
    length = x_inner.shape[0]
    extended = jnp.concatenate([halo_rows, x_inner], axis=0)
    flag_line = jnp.concatenate([jnp.zeros((tap_count - 1,), jnp.float32), start_flags], axis=0)
    result = conv_b[None, :] + conv_w[tap_count - 1][None, :] * x_inner
    survive = jnp.ones((length,), jnp.float32)
    for offset in range(1, tap_count):
        survive = survive * (1.0 - flag_line[tap_count - offset : tap_count - offset + length])
        shifted = extended[tap_count - 1 - offset : tap_count - 1 - offset + length]
        result = result + conv_w[tap_count - 1 - offset][None, :] * shifted * survive[:, None]
    return jax.nn.silu(result)


def delta_apply(step_pre, bias_row, real_rows):
    return jax.nn.softplus(step_pre + bias_row[None, :]) * real_rows[:, None]


def mm(left, right):
    return jnp.dot(left, right, preferred_element_type=jnp.float32)


def mm_t(left, right):
    return lax.dot_general(left, right, LAST_DIMS, preferred_element_type=jnp.float32)


def t_mm(left, right):
    return lax.dot_general(left, right, ROWS_FIRST, preferred_element_type=jnp.float32)


def block_mm(left, right):
    return lax.dot_general(
        left, right, (((0, 2), (0, 1)), ((), ())), preferred_element_type=jnp.float32
    )


def body(
    tokens,
    starts,
    counts,
    routes,
    slot_index,
    gain_mix,
    in_proj,
    conv_weight,
    conv_bias,
    x_proj,
    dt_proj,
    dt_bias,
    a_log,
    skip_gain,
    out_proj,
    gain_ffn,
    router,
    up_proj,
    down_proj,
    out_grad,
):
    float_type = jnp.float32
    low_type = jnp.bfloat16
    length = tokens.shape[0]
    model_width = tokens.shape[1]
    inner_width = conv_bias.shape[0]
    experts = router.shape[1]
    capacity = 5 * length // (4 * experts)
    groups, members = lax.axis_size("ep"), lax.axis_size("hs")
    group, member = lax.axis_index("ep"), lax.axis_index("hs")
    half = groups // 2
    upper = group >= half

    def blocks_home(values):
        return lax.all_to_all(values, "ep", split_axis=0, concat_axis=0, tiled=True)

    def by_owner(values):
        wide = inner_width // (half * members * 2)
        shaped = values.T.reshape(half, members, 2, wide, length)
        return jnp.transpose(shaped, (2, 0, 1, 3, 4)).reshape(groups, -1, length)

    up_own, down_own = up_proj[0], down_proj[0]
    far = members // 2
    masks = range(1, far)
    near = [[first + k for k in range(far)] for first in range(0, members, far)]
    ups = lax.all_gather(up_own, "hs", axis_index_groups=near)
    downs = lax.all_gather(down_own, "hs", axis_index_groups=near)

    edge_start = counts[0] - (CONV - 1)
    start_flags = starts.astype(float_type)
    real_rows = (jnp.arange(length, dtype=jnp.int32) < counts[0]).astype(float_type)
    tokens_float = tokens.astype(float_type)
    normed_one, norm_one_back = jax.vjp(scaled_norm, tokens_float, gain_mix)
    normed_low = normed_one.astype(low_type)
    projected = mm(normed_low, in_proj)
    inner_x = projected[:, :inner_width]
    inner_gate = projected[:, inner_width:]
    edge_rows = lax.dynamic_slice_in_dim(inner_x, edge_start, CONV - 1, 0)
    edge_flags = lax.dynamic_slice_in_dim(start_flags, edge_start, CONV - 1, 0)
    later = [jnp.prod(1.0 - edge_flags[k + 1 :]) for k in range(CONV - 1)]
    edge_mask = jnp.stack(later)[:, None]
    halo_rows = shifted_2(edge_rows * edge_mask, "hs", 1)

    def conv_part(x_part, rows_part, weight_part, bias_part):
        return conv_mix(x_part, rows_part, start_flags, weight_part, bias_part)

    mixer_in, conv_back = jax.vjp(conv_part, inner_x, halo_rows, conv_weight, conv_bias)
    mixer_low = mixer_in.astype(low_type)
    small_proj = mm(mixer_low, x_proj)
    rank_low = small_proj[:, :DT_RANK].astype(low_type)
    step_pre = mm(rank_low, dt_proj)
    input_map = small_proj[:, DT_RANK : DT_RANK + STATE]
    output_map = small_proj[:, DT_RANK + STATE :]

    def step_part(pre_part, bias_part):
        return delta_apply(pre_part, bias_part, real_rows)

    step_size, step_back = jax.vjp(step_part, step_pre, dt_bias)
    in_wide, out_wide = widened(input_map), widened(output_map)
    reset_wide = widened(start_flags[:, None] * RESET)
    rates = -(jnp.exp(a_log) / LN2).T
    skip_row = skip_gain[None, :]
    ends_ex, cum_ex, end_all, cum_all = scan_ends(
        mixer_in, step_size, in_wide, reset_wide, rates
    )
    entering, cums = state_before(cum_all, end_all, rates, "hs")
    scan_out, gated_low = scan_outputs(
        mixer_in,
        step_size,
        in_wide,
        out_wide,
        reset_wide,
        rates,
        ends_ex,
        cum_ex,
        entering,
        skip_row,
        inner_gate,
        waits=[ups],
    )
    mixer_out = mm(gated_low, out_proj)
    middle = tokens_float + mixer_out * real_rows[:, None]
    normed_two, norm_two_back = jax.vjp(scaled_norm, middle, gain_ffn)
    router_probs = jax.nn.softmax(
        jnp.dot(normed_two, router, precision=highest, preferred_element_type=float_type), axis=1
    )
    chosen = (routes[:, None] == jnp.arange(experts, dtype=jnp.int32)[None, :]).astype(float_type)
    gate_value = jnp.sum(router_probs * chosen, axis=1)
    column = routes * capacity + slot_index
    placed = (
        (column[:, None] == jnp.arange(experts * capacity, dtype=jnp.int32)[None, :])
        & (slot_index[:, None] >= 0)
    ).astype(low_type)
    grad_out = out_grad.astype(float_type)
    token_grad = grad_out * gate_value[:, None]

    rows_low = t_mm(placed, normed_two.astype(low_type)).astype(low_type)
    rows_own = blocks_home(rows_low.reshape(experts, capacity, model_width)).reshape(
        -1, model_width
    )
    rows_pair = crossed(rows_own, "hs", far)
    grads_low = t_mm(placed, token_grad.astype(low_type)).astype(low_type)
    grads_own = blocks_home(grads_low.reshape(experts, capacity, model_width)).reshape(
        -1, model_width
    )
    grads_pair = crossed(after(grads_own, rows_pair), "hs", far)
    gated_blocks = blocks_home(after(gated_low, grads_own).T.reshape(groups, -1, length))
    normed_all = lax.all_gather(after(normed_low, grads_own), "ep")
    rows = jnp.concatenate([rows_own, rows_pair], axis=0)
    grads = jnp.concatenate([grads_own, grads_pair], axis=0)
    place = lax.rem(member, far)

    def near_parts(gathered):
        return [
            lax.dynamic_index_in_dim(gathered, jnp.bitwise_xor(place, mask), 0, False)
            for mask in range(far)
        ]

    up_all, down_all = near_parts(ups), near_parts(downs)
    pre_all = [mm(rows, up) for up in up_all]
    hidden_all, gelu_backs = zip(*[jax.vjp(gelu_tanh, pre) for pre in pre_all])
    hidden_all = [hidden.astype(low_type) for hidden in hidden_all]
    expert_part = sum(mm(hidden, down) for hidden, down in zip(hidden_all, down_all))
    count = rows_own.shape[0]

    def pair_sum(partial, *earlier):
        other = crossed(after(partial[count:].astype(low_type), *earlier), "hs", far)
        return (partial[:count] + other.astype(float_type)).astype(low_type)

    home_rows = blocks_home(pair_sum(expert_part, grads_pair).reshape(groups, -1, model_width))
    pre_grads = [
        back(mm_t(grads, down))[0].astype(low_type) for back, down in zip(gelu_backs, down_all)
    ]
    grad_part = sum(mm_t(pre_grad, up) for pre_grad, up in zip(pre_grads, up_all))
    up_parts = [t_mm(rows, pre_grad) for pre_grad in pre_grads]
    down_parts = [t_mm(hidden, grads) for hidden in hidden_all]
    up_sent = [part.astype(low_type) for part in up_parts[1:]]
    down_sent = [part.astype(low_type) for part in down_parts[1:]]
    grad_rows = pair_sum(grad_part)
    grad_rows, up_sent, down_sent = lax.optimization_barrier((grad_rows, up_sent, down_sent))
    home_grad = blocks_home(grad_rows.reshape(groups, -1, model_width))

    expert_out = mm(placed, home_rows.reshape(experts * capacity, model_width))
    block_out = (middle + gate_value[:, None] * expert_out).astype(low_type)
    gate_grad = jnp.sum(grad_out * expert_out, axis=1)
    logit_grad = router_probs * gate_grad[:, None] * (chosen - gate_value[:, None])
    router_grad = lax.dot_general(
        normed_two, logit_grad, ROWS_FIRST, precision=highest, preferred_element_type=float_type
    )
    normed_two_grad = mm(
        placed, home_grad.reshape(experts * capacity, model_width)
    ) + lax.dot_general(
        logit_grad, router, LAST_DIMS, precision=highest, preferred_element_type=float_type
    )
    middle_norm_grad, gain_ffn_grad = norm_two_back(normed_two_grad)
    middle_grad = grad_out + middle_norm_grad
    mixer_grad = (middle_grad * real_rows[:, None]).astype(low_type)
    mixer_grad_all = lax.all_gather(mixer_grad, "ep")
    gated_grad = mm_t(mixer_grad, out_proj)
    scan_grad, gate_pre_low, adj_ex, back_cum_ex, adj_all = scan_adjoints(
        gated_grad,
        inner_gate,
        scan_out,
        step_size,
        out_wide,
        reset_wide,
        rates,
        waits=[gated_blocks],
    )
    returning = state_after(cums, adj_all, rates, "hs")
    returning, up_sent, down_sent, gate_sent = lax.optimization_barrier(
        (returning, up_sent, down_sent, by_owner(gate_pre_low))
    )
    gate_blocks = blocks_home(gate_sent)
    up_got = [crossed(part, "hs", mask) for part, mask in zip(up_sent, masks)]
    scan_in_grad, size_grad, wide_grads, log_grad, skip_grad = scan_grads(
        mixer_in,
        step_size,
        in_wide,
        out_wide,
        reset_wide,
        rates,
        ends_ex,
        cum_ex,
        entering,
        skip_row,
        scan_grad,
        adj_ex,
        back_cum_ex,
        returning,
    )
    size_grad, gate_blocks, up_got, down_sent = lax.optimization_barrier(
        (size_grad, gate_blocks, up_got, down_sent)
    )
    down_got = [crossed(part, "hs", mask) for part, mask in zip(down_sent, masks)]
    pre_step_grad, dt_bias_grad = step_back(size_grad)
    pre_step_low = pre_step_grad.astype(low_type)
    rank_grad = mm_t(pre_step_low, dt_proj)
    small_grad = jnp.concatenate([rank_grad, fold_maps(wide_grads)], axis=1).astype(low_type)
    mixer_in_grad = scan_in_grad + mm_t(small_grad, x_proj)
    inner_x_grad, halo_grad, conv_weight_grad, conv_bias_grad = conv_back(mixer_in_grad)
    edge_grad = shifted_2(halo_grad, "hs", -1) * edge_mask
    edge_total = lax.dynamic_slice_in_dim(inner_x_grad, edge_start, CONV - 1, 0) + edge_grad
    inner_x_grad = lax.dynamic_update_slice_in_dim(inner_x_grad, edge_total, edge_start, 0)
    inner_low = inner_x_grad.astype(low_type)

    inner_sent = by_owner(inner_low)
    inner_blocks = blocks_home(inner_sent)
    gated_blocks = after(gated_blocks, inner_sent)
    gate_blocks = after(gate_blocks, inner_sent)
    small_late, step_late = after(small_grad, inner_sent), after(pre_step_low, inner_sent)

    def row_blocks(values):
        blocks = values.reshape(values.shape[0], groups, -1)
        return blocks_home(jnp.transpose(blocks, (1, 0, 2)))

    def row_shares(blocks):
        part = jnp.sum(blocks.astype(float_type), axis=0)
        shares = part.reshape(part.shape[0], members, -1)
        return summed_shares(jnp.transpose(shares, (1, 0, 2)), "hs")

    pieces = [
        t_mm(small_late, mixer_low),
        t_mm(rank_low, step_late),
        log_grad,
        dt_bias_grad[None, :],
        skip_grad,
        router_grad.reshape(inner_width, -1).T,
    ]
    packed = jnp.concatenate([after(pieces[0], inner_blocks)] + pieces[1:], axis=0)
    packed = row_blocks(packed.astype(low_type))
    inner_low = after(inner_low, inner_blocks)
    normed_one_grad = mm_t(inner_low, in_proj[:, :inner_width]) + mm_t(
        gate_pre_low, in_proj[:, inner_width:]
    )
    tokens_norm_grad, gain_mix_grad = norm_one_back(normed_one_grad)
    tokens_grad = middle_grad + tokens_norm_grad
    late = jnp.concatenate(
        [
            conv_weight_grad,
            conv_bias_grad[None, :],
            jnp.concatenate([gain_mix_grad, gain_ffn_grad])[None, :],
        ],
        axis=0,
    )
    late = row_blocks(after(late, packed))
    up_grad, down_grad = up_parts[0], down_parts[0]
    for up_other, down_other in zip(up_got, down_got):
        up_grad = up_grad + up_other.astype(float_type)
        down_grad = down_grad + down_other.astype(float_type)

    def member_sum(part):
        return summed_shares(part.reshape(members, -1, model_width), "hs")

    out_proj_sum = member_sum(block_mm(gated_blocks, mixer_grad_all))
    gate_sum = member_sum(block_mm(gate_blocks, normed_all))
    packed_sum = row_shares(packed)
    inner_sum = member_sum(block_mm(inner_blocks, normed_all))
    late_sum = row_shares(late)
    given = jnp.where(upper, inner_sum, gate_sum).astype(low_type)
    kept = jnp.where(upper, gate_sum, inner_sum)
    taken = crossed(given, "ep", half).astype(float_type)
    in_proj_sum = jnp.concatenate(
        [jnp.where(upper, taken, kept), jnp.where(upper, kept, taken)], axis=0
    ).T
    cut, at = [], 0
    for piece in pieces:
        cut.append(packed_sum[at : at + piece.shape[0]])
        at += piece.shape[0]
    return (
        block_out,
        tokens_grad,
        late_sum[CONV + 1],
        cut[5].T.reshape(-1),
        in_proj_sum,
        late_sum[:CONV],
        late_sum[CONV],
        cut[0].T,
        cut[1],
        cut[3][0],
        cut[2].T,
        cut[4][0],
        out_proj_sum,
        up_grad[None],
        down_grad[None],
    )


def solution(mesh):
    return jax.shard_map(
        body,
        mesh=mesh,
        in_specs=(
            P(("ep", "hs"), None),
            P(("ep", "hs")),
            P(("ep", "hs")),
            P(("ep", "hs")),
            P(("ep", "hs")),
            P(),
            P(),
            P(),
            P(),
            P(),
            P(),
            P(),
            P(),
            P(),
            P(),
            P(),
            P(),
            P("ep", None, "hs"),
            P("ep", "hs", None),
            P(("ep", "hs"), None),
        ),
        out_specs=(
            P(("ep", "hs"), None),
            P(("ep", "hs"), None),
            P(("ep", "hs")),
            P(("ep", "hs")),
            P(None, ("ep", "hs")),
            P(None, ("ep", "hs")),
            P(("ep", "hs")),
            P(("ep", "hs"), None),
            P(None, ("ep", "hs")),
            P(("ep", "hs")),
            P(("ep", "hs"), None),
            P(("ep", "hs")),
            P(("ep", "hs"), None),
            P("ep", None, "hs"),
            P("ep", "hs", None),
        ),
        check_vma=False,
    )
```

```python
import jax
import jax.numpy as jnp
from jax import lax
from jax.experimental import pallas as pl
from jax.experimental.pallas import tpu as pltpu
from jax.sharding import PartitionSpec as P

DT_RANK = 72
CONV = 4
STATE = 16
SEGMENTS = 8
LANES = 128
TILES = 3
RESET = 1e30
LN2 = 0.6931471805599453


def widened(values):
    shaped = values.reshape(SEGMENTS, -1, values.shape[1])
    shaped = jnp.transpose(shaped, (1, 2, 0))[..., None]
    return jnp.broadcast_to(shaped, shaped.shape[:3] + (LANES,))


def each_tile(work):
    @pl.loop(0, TILES)
    def _(k):
        work(pl.ds(pl.multiple_of(k * LANES, LANES), LANES))


def spread_rates(target, rates, lanes):
    for n in range(STATE):
        target[n] = jnp.broadcast_to(rates[n : n + 1, lanes], (SEGMENTS, LANES))


def ends_kernel(x, dt, in_wide, big, rates, ends_ex, cum_ex, end_all, cum_all,
                rate_wide, end_scr, sum_scr, x_scr, dt_scr):
    steps = x.shape[0] // SEGMENTS

    def work(lanes):
        spread_rates(rate_wide, rates, lanes)
        x_scr[...] = x[:, lanes]
        dt_scr[...] = dt[:, lanes]

        def step(i, carry):
            total, states = carry[0], carry[1:]
            rows = pl.ds(i, SEGMENTS, stride=steps)
            stride = dt_scr[rows, :]
            driven = stride * x_scr[rows, :]
            stride = stride + big[i, 0]
            new = [total + stride]
            for n in range(STATE):
                new.append(jnp.exp2(stride * rate_wide[n]) * states[n] + driven * in_wide[i, n])
            return tuple(new)

        zero = jnp.zeros((SEGMENTS, LANES), jnp.float32)
        done = lax.fori_loop(0, steps, step, (zero,) * (STATE + 1), unroll=4)
        sum_scr[...] = done[0]
        for n in range(STATE):
            end_scr[n * SEGMENTS : (n + 1) * SEGMENTS, :] = done[1 + n]
        state = jnp.zeros((STATE, LANES), jnp.float32)
        cum = jnp.zeros((1, LANES), jnp.float32)
        for s in range(SEGMENTS):
            ends_ex[s * STATE : (s + 1) * STATE, lanes] = state
            cum_ex[s : s + 1, lanes] = cum
            own = sum_scr[s : s + 1, :]
            state = (
                jnp.exp2(own * rates[:, lanes]) * state
                + end_scr[pl.ds(s, STATE, stride=SEGMENTS), :]
            )
            cum = cum + own
        end_all[:, lanes] = state
        cum_all[:, lanes] = cum

    each_tile(work)


def opening_states(cum, rate_wide, entering, ends_ex, end_scr, lanes):
    end_scr[...] = ends_ex[:, lanes]
    return tuple(
        jnp.exp2(cum * rate_wide[n]) * entering[n : n + 1, lanes]
        + end_scr[pl.ds(n, SEGMENTS, stride=STATE), :]
        for n in range(STATE)
    )


def outputs_kernel(x, dt, in_wide, out_wide, big, rates, ends_ex, cum_ex, entering, skip, gate,
                   scan_out, gated, gated_t, rate_wide, end_scr, x_scr, dt_scr, out_scr):
    steps = x.shape[0] // SEGMENTS

    def work(lanes):
        spread_rates(rate_wide, rates, lanes)
        x_scr[...] = x[:, lanes]
        dt_scr[...] = dt[:, lanes]
        opening = opening_states(cum_ex[:, lanes], rate_wide, entering, ends_ex, end_scr, lanes)

        def step(i, states):
            rows = pl.ds(i, SEGMENTS, stride=steps)
            stride = dt_scr[rows, :]
            driven = stride * x_scr[rows, :]
            stride = stride + big[i, 0]
            new, total = [], None
            for n in range(STATE):
                state = jnp.exp2(stride * rate_wide[n]) * states[n] + driven * in_wide[i, n]
                new.append(state)
                term = state * out_wide[i, n]
                total = term if total is None else total + term
            out_scr[rows, :] = total
            return tuple(new)

        lax.fori_loop(0, steps, step, opening, unroll=4)
        value = out_scr[...] + skip[:, lanes] * x_scr[...]
        scan_out[:, lanes] = value
        product = value * jax.nn.silu(gate[:, lanes])
        gated[:, lanes] = product.astype(gated.dtype)
        gated_t[lanes, :] = product.T.astype(gated.dtype)

    each_tile(work)


def adjoint_kernel(gated_grad, gate, scan_out, dt, out_wide, big, rates,
                   scan_grad, gate_grad, gate_grad_t, adj_ex, cum_ex, adj_all,
                   rate_wide, end_scr, sum_scr, grad_scr, dt_scr):
    steps = dt.shape[0] // SEGMENTS

    def work(lanes):
        spread_rates(rate_wide, rates, lanes)
        incoming = gated_grad[:, lanes]
        gate_in = gate[:, lanes]
        chance = jax.nn.sigmoid(gate_in)
        moved = incoming * (gate_in * chance)
        scan_grad[:, lanes] = moved
        grad_scr[...] = moved
        dt_scr[...] = dt[:, lanes]
        product = incoming * scan_out[:, lanes] * (chance * (1.0 + gate_in * (1.0 - chance)))
        gate_grad[:, lanes] = product.astype(gate_grad.dtype)
        gate_grad_t[lanes, :] = product.T.astype(gate_grad.dtype)

        def step(k, carry):
            i = steps - 1 - k
            total, tails = carry[0], carry[1:]
            rows = pl.ds(i, SEGMENTS, stride=steps)
            grad = grad_scr[rows, :]
            stride = dt_scr[rows, :] + big[i, 0]
            new = [total + stride]
            for n in range(STATE):
                new.append(jnp.exp2(stride * rate_wide[n]) * (grad * out_wide[i, n] + tails[n]))
            return tuple(new)

        zero = jnp.zeros((SEGMENTS, LANES), jnp.float32)
        done = lax.fori_loop(0, steps, step, (zero,) * (STATE + 1), unroll=4)
        sum_scr[...] = done[0]
        for n in range(STATE):
            end_scr[n * SEGMENTS : (n + 1) * SEGMENTS, :] = done[1 + n]
        tail = jnp.zeros((STATE, LANES), jnp.float32)
        cum = jnp.zeros((1, LANES), jnp.float32)
        for s in reversed(range(SEGMENTS)):
            adj_ex[s * STATE : (s + 1) * STATE, lanes] = tail
            cum_ex[s : s + 1, lanes] = cum
            own = sum_scr[s : s + 1, :]
            tail = (
                jnp.exp2(own * rates[:, lanes]) * tail
                + end_scr[pl.ds(s, STATE, stride=SEGMENTS), :]
            )
            cum = cum + own
        adj_all[:, lanes] = tail

    each_tile(work)


def grads_kernel(x, dt, in_wide, out_wide, big, rates, ends_ex, cum_ex, entering, skip,
                 scan_grad, adj_ex, back_cum_ex, returning,
                 x_grad, dt_grad, map_grad, log_grad, skip_grad,
                 rate_wide, kept, log_scr, end_scr, x_scr, dt_scr, grad_scr, x_out, dt_out):
    steps = x.shape[0] // SEGMENTS

    @pl.when(pl.program_id(0) == 0)
    def _():
        map_grad[...] = jnp.zeros_like(map_grad)

    def work(lanes):
        spread_rates(rate_wide, rates, lanes)
        x_scr[...] = x[:, lanes]
        dt_scr[...] = dt[:, lanes]
        opening = opening_states(cum_ex[:, lanes], rate_wide, entering, ends_ex, end_scr, lanes)

        def forward(i, states):
            rows = pl.ds(i, SEGMENTS, stride=steps)
            stride = dt_scr[rows, :]
            driven = stride * x_scr[rows, :]
            stride = stride + big[i, 0]
            new = []
            for n in range(STATE):
                remain = jnp.exp2(stride * rate_wide[n]) * states[n]
                kept[i, n] = remain
                new.append(remain + driven * in_wide[i, n])
            return tuple(new)

        lax.fori_loop(0, steps, forward, opening, unroll=4)
        tails = opening_states(back_cum_ex[:, lanes], rate_wide, returning, adj_ex, end_scr, lanes)
        zero = jnp.zeros((SEGMENTS, LANES), jnp.float32)
        for n in range(STATE):
            log_scr[n] = zero

        def backward(k, tails):
            i = steps - 1 - k
            rows = pl.ds(i, SEGMENTS, stride=steps)
            stride = dt_scr[rows, :]
            value = x_scr[rows, :]
            driven = stride * value
            grad = grad_scr[rows, :]
            marked = stride + big[i, 0]
            new = []
            drive_sum, rate_sum = None, None
            for n in range(STATE):
                rate = rate_wide[n]
                in_n = in_wide[i, n]
                adjoint = grad * out_wide[i, n] + tails[n]
                remain = kept[i, n]
                map_grad[1, i, n] += grad * (remain + driven * in_n)
                map_grad[0, i, n] += adjoint * driven
                drive = adjoint * in_n
                touched = adjoint * remain
                slope = touched * rate
                log_scr[n] += touched * stride
                drive_sum = drive if drive_sum is None else drive_sum + drive
                rate_sum = slope if rate_sum is None else rate_sum + slope
                new.append(jnp.exp2(marked * rate) * adjoint)
            x_out[rows, :] = stride * drive_sum
            dt_out[rows, :] = value * drive_sum + LN2 * rate_sum
            return tuple(new)

        grad_scr[...] = scan_grad[:, lanes]
        lax.fori_loop(0, steps, backward, tails, unroll=2)
        dt_grad[:, lanes] = dt_out[...]
        x_grad[:, lanes] = x_out[...] + skip[:, lanes] * grad_scr[...]
        skip_grad[:, lanes] = jnp.sum(grad_scr[...] * x_scr[...], axis=0, keepdims=True)
        for n in range(STATE):
            log_grad[n : n + 1, lanes] = (
                jnp.sum(log_scr[n], axis=0, keepdims=True) * rates[n : n + 1, lanes] * LN2
            )

    each_tile(work)


def tile(rows):
    return pl.BlockSpec((rows, TILES * LANES), lambda j: (0, j))


def turned(rows):
    return pl.BlockSpec((TILES * LANES, rows), lambda j: (j, 0))


def whole(shape):
    return pl.BlockSpec(shape, lambda j: (0,) * len(shape))


def shape_of(rows, width, dtype=jnp.float32):
    return jax.ShapeDtypeStruct((rows, width), dtype)


PARAMS = pltpu.CompilerParams(
    dimension_semantics=("arbitrary",), vmem_limit_bytes=56 * 1024 * 1024
)
RATE = pltpu.VMEM((STATE, SEGMENTS, LANES), jnp.float32)
ENDS = pltpu.VMEM((SEGMENTS * STATE, LANES), jnp.float32)
SUMS = pltpu.VMEM((SEGMENTS, LANES), jnp.float32)


def call(kernel, waits, micros, **options):
    specs = options.pop("in_specs")

    def waiting(*refs):
        kernel(*refs[: len(specs)], *refs[len(specs) + len(waits) :])

    waiting.__name__ = options["name"]
    run = pl.pallas_call(
        waiting,
        in_specs=specs + [pl.BlockSpec(memory_space=pl.ANY)] * len(waits),
        compiler_params=PARAMS,
        cost_estimate=pl.CostEstimate(
            flops=0, bytes_accessed=micros * 3_000_000, transcendentals=0
        ),
        **options,
    )
    return lambda *operands: run(*operands, *waits)


def rows_of(rows):
    return pltpu.VMEM((rows, LANES), jnp.float32)


def scan_ends(x, dt, in_wide, big, rates, waits=()):
    rows, width = x.shape
    return call(
        ends_kernel,
        waits,
        15,
        grid=(width // (TILES * LANES),),
        in_specs=[tile(rows), tile(rows), whole(in_wide.shape), whole(big.shape), tile(STATE)],
        out_specs=[tile(SEGMENTS * STATE), tile(SEGMENTS), tile(STATE), tile(1)],
        out_shape=[shape_of(SEGMENTS * STATE, width), shape_of(SEGMENTS, width),
                   shape_of(STATE, width), shape_of(1, width)],
        scratch_shapes=[RATE, ENDS, SUMS, rows_of(rows), rows_of(rows)],
        name="scan_ends",
    )(x, dt, in_wide, big, rates)


def scan_outputs(x, dt, in_wide, out_wide, big, rates, ends_ex, cum_ex, entering, skip, gate, waits=()):
    rows, width = x.shape
    return call(
        outputs_kernel,
        waits,
        20,
        grid=(width // (TILES * LANES),),
        in_specs=[tile(rows), tile(rows), whole(in_wide.shape), whole(out_wide.shape),
                  whole(big.shape), tile(STATE), tile(SEGMENTS * STATE), tile(SEGMENTS),
                  tile(STATE), tile(1), tile(rows)],
        out_specs=[tile(rows), tile(rows), turned(rows)],
        out_shape=[shape_of(rows, width), shape_of(rows, width, jnp.bfloat16),
                   shape_of(width, rows, jnp.bfloat16)],
        scratch_shapes=[RATE, ENDS] + [rows_of(rows)] * 3,
        name="scan_outputs",
    )(x, dt, in_wide, out_wide, big, rates, ends_ex, cum_ex, entering, skip, gate)


def scan_adjoints(gated_grad, gate, scan_out, dt, out_wide, big, rates, waits=()):
    rows, width = dt.shape
    return call(
        adjoint_kernel,
        waits,
        17,
        grid=(width // (TILES * LANES),),
        in_specs=[tile(rows), tile(rows), tile(rows), tile(rows), whole(out_wide.shape),
                  whole(big.shape), tile(STATE)],
        out_specs=[tile(rows), tile(rows), turned(rows), tile(SEGMENTS * STATE), tile(SEGMENTS),
                   tile(STATE)],
        out_shape=[shape_of(rows, width), shape_of(rows, width, jnp.bfloat16),
                   shape_of(width, rows, jnp.bfloat16),
                   shape_of(SEGMENTS * STATE, width), shape_of(SEGMENTS, width),
                   shape_of(STATE, width)],
        scratch_shapes=[RATE, ENDS, SUMS, rows_of(rows), rows_of(rows)],
        name="scan_adjoints",
    )(gated_grad, gate, scan_out, dt, out_wide, big, rates)


def scan_grads(x, dt, in_wide, out_wide, big, rates, ends_ex, cum_ex, entering, skip,
               scan_grad, adj_ex, back_cum_ex, returning, waits=()):
    rows, width = x.shape
    steps = rows // SEGMENTS
    wide_shape = (steps, STATE, SEGMENTS, LANES)
    return call(
        grads_kernel,
        waits,
        55,
        grid=(width // (TILES * LANES),),
        in_specs=[tile(rows), tile(rows), whole(in_wide.shape), whole(out_wide.shape),
                  whole(big.shape), tile(STATE), tile(SEGMENTS * STATE), tile(SEGMENTS),
                  tile(STATE), tile(1), tile(rows), tile(SEGMENTS * STATE), tile(SEGMENTS),
                  tile(STATE)],
        out_specs=[tile(rows), tile(rows), whole((2,) + wide_shape), tile(STATE), tile(1)],
        out_shape=[shape_of(rows, width), shape_of(rows, width),
                   jax.ShapeDtypeStruct((2,) + wide_shape, jnp.float32),
                   shape_of(STATE, width), shape_of(1, width)],
        scratch_shapes=[RATE, pltpu.VMEM(wide_shape, jnp.float32), RATE, ENDS]
        + [rows_of(rows)] * 5,
        name="scan_grads",
    )(x, dt, in_wide, out_wide, big, rates, ends_ex, cum_ex, entering, skip, scan_grad, adj_ex,
      back_cum_ex, returning)


def fold_maps(wide):
    summed = jnp.sum(wide, axis=4)
    return jnp.transpose(summed, (3, 1, 0, 2)).reshape(-1, 2 * STATE)


def conv_back_kernel(edge_start, scan_grad, small_grad, x_proj, x, halo, edge, valid, weight, bias,
                     x_grad, x_grad_t, weight_grad, bias_grad, x_ext, g_ext, valid_wide):
    rows = x.shape[0]
    taps = weight.shape[0]
    position = lax.broadcasted_iota(jnp.int32, (rows, LANES), 0)
    first = edge_start[0]

    @pl.when(pl.program_id(0) == 0)
    def _():
        for k in range(1, taps):
            valid_wide[k] = jnp.broadcast_to(valid[:, k : k + 1], (rows, LANES))
        g_ext[rows : rows + 8, :] = jnp.zeros((8, LANES), jnp.float32)

    def work(lanes):
        grad = scan_grad[:, lanes] + lax.dot_general(
            small_grad[...], x_proj[lanes, :], (((1,), (1,)), ((), ())),
            preferred_element_type=jnp.float32,
        )
        x_ext[0:8, :] = halo[:, lanes]
        x_ext[8 : 8 + rows, :] = x[:, lanes]
        pre = bias[:, lanes] + weight[taps - 1 : taps, lanes] * x[:, lanes]
        for k in range(1, taps):
            tap = weight[taps - 1 - k : taps - k, lanes]
            pre = pre + tap * x_ext[8 - k : 8 - k + rows, :] * valid_wide[k]
        chance = jax.nn.sigmoid(pre)
        grad = grad * (chance * (1.0 + pre * (1.0 - chance)))
        bias_grad[:, lanes] = jnp.sum(grad, axis=0, keepdims=True)
        weight_grad[taps - 1 : taps, lanes] = jnp.sum(grad * x[:, lanes], axis=0, keepdims=True)
        total = weight[taps - 1 : taps, lanes] * grad
        for k in range(1, taps):
            masked = grad * valid_wide[k]
            weight_grad[taps - 1 - k : taps - k, lanes] = jnp.sum(
                masked * x_ext[8 - k : 8 - k + rows, :], axis=0, keepdims=True
            )
            g_ext[0:rows, :] = masked
            total = total + weight[taps - 1 - k : taps - k, lanes] * g_ext[k : k + rows, :]
        for j in range(taps - 1):
            total = total + jnp.where(position == first + j, edge[j : j + 1, lanes], 0.0)
        x_grad[:, lanes] = total.astype(x_grad.dtype)
        x_grad_t[lanes, :] = total.T.astype(x_grad_t.dtype)

    each_tile(work)


def conv_back(edge_start, scan_grad, small_grad, x_proj, x, halo, edge, valid, weight, bias,
              waits=()):
    rows, width = scan_grad.shape
    taps = weight.shape[0]
    scratch = pltpu.VMEM((rows + 8, LANES), jnp.float32)
    return call(
        conv_back_kernel,
        waits,
        6,
        grid=(width // (TILES * LANES),),
        in_specs=[pl.BlockSpec(memory_space=pltpu.SMEM), tile(rows), whole(small_grad.shape),
                  pl.BlockSpec((TILES * LANES, x_proj.shape[1]), lambda j: (j, 0)), tile(rows),
                  tile(8), tile(8), whole(valid.shape), tile(taps), tile(1)],
        out_specs=[tile(rows), turned(rows), tile(taps), tile(1)],
        out_shape=[shape_of(rows, width, jnp.bfloat16), shape_of(width, rows, jnp.bfloat16),
                   shape_of(taps, width), shape_of(1, width)],
        scratch_shapes=[scratch, scratch, pltpu.VMEM((taps, rows, LANES), jnp.float32)],
        name="conv_back",
    )(edge_start, scan_grad, small_grad, x_proj, x, halo, edge, valid, weight, bias)


def shares_kernel(place, *refs):
    out, pairs = refs[-1], len(refs) // 2
    members, wide = out.shape[0], out.shape[2]
    for p in range(pairs):
        left, right = refs[p], refs[pairs + p]
        blocks = left.shape[0]
        whole_left = jnp.concatenate([left[b] for b in range(blocks)], axis=1)
        whole_right = right[...].reshape(-1, right.shape[2])
        total = jnp.dot(whole_left, whole_right, preferred_element_type=jnp.float32)
        for h in range(members):
            after_this = lax.rem(h - place[0] + members, members)
            out[after_this, p] = total[h * wide : (h + 1) * wide].astype(out.dtype)


def block_shares(lefts, rights, place, members, waits=()):
    blocks, channels, tokens = lefts[0].shape
    width = rights[0].shape[2]
    columns = TILES * LANES
    out = (members, len(lefts), channels // members)
    return call(
        shares_kernel,
        waits,
        0,
        grid=(width // columns,),
        in_specs=[pl.BlockSpec(memory_space=pltpu.SMEM)]
        + [whole(lefts[0].shape)] * len(lefts)
        + [pl.BlockSpec((blocks, tokens, columns), lambda j: (0, 0, j))] * len(lefts),
        out_specs=pl.BlockSpec(out + (columns,), lambda j: (0, 0, 0, j)),
        out_shape=jax.ShapeDtypeStruct(out + (width,), jnp.bfloat16),
        scratch_shapes=[],
        name="block_shares",
    )(place, *lefts, *rights)


def pack_kernel(mixer, small, step, rank, *refs):
    out, rows = refs[-1], refs[:-1]
    first = (((0,), (0,)), ((), ()))
    out[:, :LANES] = lax.dot_general(
        mixer[...], small[...], first, preferred_element_type=jnp.float32
    ).astype(out.dtype)
    total = lax.dot_general(step[...], rank[...], first, preferred_element_type=jnp.float32)
    at = DT_RANK
    for row in rows:
        size = row.shape[0]
        line = lax.broadcasted_iota(jnp.int32, (size, LANES), 0)
        lane = lax.broadcasted_iota(jnp.int32, (size, LANES), 1)
        spot = (lane == line + at).astype(jnp.float32).astype(out.dtype)
        total = total + lax.dot_general(
            row[...].astype(out.dtype), spot, first, preferred_element_type=jnp.float32
        )
        at += size
    out[:, LANES:] = total.astype(out.dtype)


def channel_pack(mixer, small, step, rank, rows, waits=()):
    length, width = mixer.shape
    return call(
        pack_kernel,
        waits,
        3,
        grid=(width // (TILES * LANES),),
        in_specs=[tile(length), whole(small.shape), tile(length), whole(rank.shape)]
        + [tile(row.shape[0]) for row in rows],
        out_specs=pl.BlockSpec((TILES * LANES, 2 * LANES), lambda j: (j, 0)),
        out_shape=shape_of(width, 2 * LANES, jnp.bfloat16),
        scratch_shapes=[],
        name="channel_pack",
    )(mixer, small, step, rank, *rows)


norm_epsilon = 1e-05
highest = lax.Precision.HIGHEST
ROWS_FIRST = (((0,), (0,)), ((), ()))
LAST_DIMS = (((1,), (1,)), ((), ()))


def shifted_2(block, axis, distance):
    devices = range(lax.axis_size(axis))
    route = [(i - distance, i) for i in devices if i - distance in devices]
    return lax.ppermute(block, axis, route)


def crossed(block, axis, mask):
    return lax.ppermute(block, axis, [(i, i ^ mask) for i in range(lax.axis_size(axis))])


def exchanged(blocks, axis):
    return [block if k == 0 else crossed(block, axis, k) for k, block in enumerate(blocks)]


def after(value, *others):
    return lax.optimization_barrier((value,) + others)[0]


def summed_ahead(parts, axis, *others):
    count = lax.axis_size(axis)
    total = parts[0].astype(jnp.float32)
    for k in range(1, count):
        route = [(i, (i + k) % count) for i in range(count)]
        total = total + after(lax.ppermute(parts[k], axis, route), *others).astype(jnp.float32)
    return total


def summed_shares(parts, axis):
    count, mine = lax.axis_size(axis), lax.axis_index(axis)
    return summed_ahead(
        [
            lax.dynamic_index_in_dim(parts, lax.rem(mine + k, count), 0, False)
            for k in range(count)
        ],
        axis,
    )


def around(value, axis):
    count = lax.axis_size(axis)
    return [value] + [
        lax.ppermute(value, axis, [(i, (i + k) % count) for i in range(count)])
        for k in range(1, count)
    ]


def state_before(cum, end, rates, axis):
    count, mine = lax.axis_size(axis), lax.axis_index(axis)
    first = lax.reduce_precision(cum, 8, 7)
    second = lax.reduce_precision(cum - first, 8, 7)
    sent = jnp.concatenate([end, first, second, cum - first - second], axis=0)
    got = [part.astype(jnp.float32) for part in around(sent.astype(jnp.bfloat16), axis)]
    cums = [jnp.sum(part[end.shape[0] :], axis=0, keepdims=True) for part in got]
    state = jnp.zeros_like(end)
    for k in reversed(range(1, count)):
        longer = jnp.exp2(cums[k] * rates) * state + got[k][: end.shape[0]]
        state = jnp.where(k <= mine, longer, state)
    return state, cums


def state_after(cums, tail, rates, axis):
    count, mine = lax.axis_size(axis), lax.axis_index(axis)
    got = [part.astype(jnp.float32) for part in around(tail.astype(jnp.bfloat16), axis)]
    state = jnp.zeros_like(tail)
    for k in range(1, count):
        longer = jnp.exp2(cums[k] * rates) * state + got[k]
        state = jnp.where(mine + count - k < count, longer, state)
    return state


def rms_scale(values):
    return lax.rsqrt(jnp.mean(values * values, axis=1, keepdims=True) + norm_epsilon)


def scaled_norm(values, gain_row):
    return values * rms_scale(values) * gain_row[None, :]


def gelu_tanh(values):
    return jax.nn.gelu(values, approximate=True)


def conv_mix(x_inner, halo_rows, start_flags, conv_w, conv_b):
    tap_count = conv_w.shape[0]
    length = x_inner.shape[0]
    extended = jnp.concatenate([halo_rows, x_inner], axis=0)
    flag_line = jnp.concatenate([jnp.zeros((tap_count - 1,), jnp.float32), start_flags], axis=0)
    result = conv_b[None, :] + conv_w[tap_count - 1][None, :] * x_inner
    survive = jnp.ones((length,), jnp.float32)
    for offset in range(1, tap_count):
        survive = survive * (1.0 - flag_line[tap_count - offset : tap_count - offset + length])
        shifted = extended[tap_count - 1 - offset : tap_count - 1 - offset + length]
        result = result + conv_w[tap_count - 1 - offset][None, :] * shifted * survive[:, None]
    return jax.nn.silu(result)


def delta_apply(step_pre, bias_row, real_rows):
    return jax.nn.softplus(step_pre + bias_row[None, :]) * real_rows[:, None]


def mm(left, right):
    return jnp.dot(left, right, preferred_element_type=jnp.float32)


def mm_t(left, right):
    return lax.dot_general(left, right, LAST_DIMS, preferred_element_type=jnp.float32)


def t_mm(left, right):
    return lax.dot_general(left, right, ROWS_FIRST, preferred_element_type=jnp.float32)


def body(
    tokens,
    starts,
    counts,
    routes,
    slot_index,
    gain_mix,
    in_proj,
    conv_weight,
    conv_bias,
    x_proj,
    dt_proj,
    dt_bias,
    a_log,
    skip_gain,
    out_proj,
    gain_ffn,
    router,
    up_proj,
    down_proj,
    out_grad,
):
    float_type = jnp.float32
    low_type = jnp.bfloat16
    length = tokens.shape[0]
    model_width = tokens.shape[1]
    inner_width = conv_bias.shape[0]
    experts = router.shape[1]
    capacity = 5 * length // (4 * experts)
    groups, members = lax.axis_size("ep"), lax.axis_size("hs")
    group, member = lax.axis_index("ep"), lax.axis_index("hs")
    half = groups // 2
    upper = group >= half

    def blocks_home(values):
        return lax.all_to_all(values, "ep", split_axis=0, concat_axis=0, tiled=True)

    def by_owner(values):
        wide = inner_width // (half * members * 2)
        shaped = values.reshape(half, members, 2, wide, length)
        return jnp.transpose(shaped, (2, 0, 1, 3, 4)).reshape(groups, -1, length)

    up_own, down_own = up_proj[0], down_proj[0]
    shares = members // 2
    ones = [2 * k + k.bit_count() % 2 for k in range(shares)]
    alike = []
    for g in range(groups):
        if g % 2 == 0:
            halves = [range(shares), range(shares, members)]
        else:
            halves = [ones, [mask ^ 1 for mask in ones]]
        alike += [[g * members + h for h in chosen_half] for chosen_half in halves]
    odd_group = lax.rem(group, 2)
    place = jnp.where(odd_group == 0, lax.rem(member, shares), member // 2)

    def to_other_half(block):
        masks = [shares, 1]
        route = [
            (g * members + h, g * members + (h ^ masks[g % 2]))
            for g in range(groups)
            for h in range(members)
        ]
        return lax.ppermute(block, ("ep", "hs"), route)

    def from_half(block):
        return lax.all_gather(block, ("ep", "hs"), axis_index_groups=alike)


    edge_start = counts[0] - (CONV - 1)
    start_flags = starts.astype(float_type)
    real_rows = (jnp.arange(length, dtype=jnp.int32) < counts[0]).astype(float_type)
    tokens_float = tokens.astype(float_type)
    normed_one, norm_one_back = jax.vjp(scaled_norm, tokens_float, gain_mix)
    normed_low = normed_one.astype(low_type)
    normed_all = lax.all_gather(normed_low, "ep")
    projected = mm(normed_low, in_proj)
    inner_x = projected[:, :inner_width]
    inner_gate = projected[:, inner_width:]
    edge_rows = lax.dynamic_slice_in_dim(inner_x, edge_start, CONV - 1, 0)
    edge_flags = lax.dynamic_slice_in_dim(start_flags, edge_start, CONV - 1, 0)
    later = [jnp.prod(1.0 - edge_flags[k + 1 :]) for k in range(CONV - 1)]
    edge_mask = jnp.stack(later)[:, None]
    halo_rows = shifted_2(edge_rows * edge_mask, "hs", 1)
    kept_taps = [jnp.ones((length,), float_type)]
    flag_line = jnp.concatenate([jnp.zeros((CONV - 1,), float_type), start_flags])
    for k in range(1, CONV):
        kept_taps.append(kept_taps[-1] * (1.0 - flag_line[CONV - k : CONV - k + length]))
    valid = jnp.stack(kept_taps, axis=1)

    ups = from_half(after(up_own, halo_rows))

    mixer_in = conv_mix(inner_x, halo_rows, start_flags, conv_weight, conv_bias)
    mixer_low = mixer_in.astype(low_type)
    small_proj = mm(mixer_low, x_proj)
    rank_low = small_proj[:, :DT_RANK].astype(low_type)
    step_pre = mm(rank_low, dt_proj)
    input_map = small_proj[:, DT_RANK : DT_RANK + STATE]
    output_map = small_proj[:, DT_RANK + STATE :]

    def step_part(pre_part, bias_part):
        return delta_apply(pre_part, bias_part, real_rows)

    step_size, step_back = jax.vjp(step_part, step_pre, dt_bias)
    in_wide, out_wide = widened(input_map), widened(output_map)
    reset_wide = widened(start_flags[:, None] * RESET)
    rates = -(jnp.exp(a_log) / LN2).T
    skip_row = skip_gain[None, :]
    ends_ex, cum_ex, end_all, cum_all = scan_ends(
        mixer_in, step_size, in_wide, reset_wide, rates
    )
    entering, cums = state_before(cum_all, end_all, rates, "hs")
    downs = from_half(after(down_own, entering))
    scan_out, gated_low, gated_t = scan_outputs(
        mixer_in,
        step_size,
        in_wide,
        out_wide,
        reset_wide,
        rates,
        ends_ex,
        cum_ex,
        entering,
        skip_row,
        inner_gate,

    )
    mixer_out = mm(gated_low, out_proj)
    middle = tokens_float + mixer_out * real_rows[:, None]
    normed_two, norm_two_back = jax.vjp(scaled_norm, middle, gain_ffn)
    router_probs = jax.nn.softmax(
        jnp.dot(normed_two, router, precision=highest, preferred_element_type=float_type), axis=1
    )
    chosen = (routes[:, None] == jnp.arange(experts, dtype=jnp.int32)[None, :]).astype(float_type)
    gate_value = jnp.sum(router_probs * chosen, axis=1)
    column = routes * capacity + slot_index
    placed = (
        (column[:, None] == jnp.arange(experts * capacity, dtype=jnp.int32)[None, :])
        & (slot_index[:, None] >= 0)
    ).astype(low_type)
    grad_out = out_grad.astype(float_type)
    token_grad = grad_out * gate_value[:, None]

    rows_low = t_mm(placed, normed_two.astype(low_type)).astype(low_type)
    rows_own = blocks_home(rows_low.reshape(experts, capacity, model_width)).reshape(
        -1, model_width
    )
    rows_pair = to_other_half(rows_own)
    grads_low = t_mm(placed, token_grad.astype(low_type)).astype(low_type)
    grads_own = blocks_home(grads_low.reshape(experts, capacity, model_width)).reshape(
        -1, model_width
    )
    grads_pair = to_other_half(after(grads_own, rows_pair))
    gated_blocks = blocks_home(after(gated_t, grads_own).reshape(groups, -1, length))
    rows = jnp.concatenate([rows_own, rows_pair], axis=0)

    def near_parts(gathered):
        return [
            lax.dynamic_index_in_dim(gathered, jnp.bitwise_xor(place, k), 0, False)
            for k in range(shares)
        ]

    up_all, down_all = near_parts(ups), near_parts(downs)
    pre_all = [mm(rows, up) for up in up_all]
    hidden_all, gelu_backs = zip(*[jax.vjp(gelu_tanh, pre) for pre in pre_all])
    hidden_all = [hidden.astype(low_type) for hidden in hidden_all]
    expert_part = sum(mm(hidden, down) for hidden, down in zip(hidden_all, down_all))
    count = rows_own.shape[0]

    def pair_sum(partial, *earlier):
        other = to_other_half(after(partial[count:].astype(low_type), *earlier))
        return (partial[:count] + other.astype(float_type)).astype(low_type), other

    back_rows, rows_other = pair_sum(expert_part, grads_pair)
    home_rows = blocks_home(back_rows.reshape(groups, -1, model_width))
    grads = jnp.concatenate([grads_own, after(grads_pair, expert_part)], axis=0)
    pre_grads = [
        back(mm_t(grads, down))[0].astype(low_type) for back, down in zip(gelu_backs, down_all)
    ]
    grad_part = sum(mm_t(pre_grad, up) for pre_grad, up in zip(pre_grads, up_all))
    up_parts = [t_mm(rows, pre_grad) for pre_grad in pre_grads]
    down_parts = [t_mm(hidden, grads) for hidden in hidden_all]
    up_sent = jnp.stack([part.astype(low_type) for part in up_parts[1:]])
    down_sent = jnp.stack([part.astype(low_type) for part in down_parts[1:]])
    grad_rows, _ = pair_sum(grad_part, rows_other)
    up_grad, down_grad = up_parts[0], down_parts[0]
    grad_rows, up_sent, down_sent, up_grad, down_grad = lax.optimization_barrier(
        (grad_rows, up_sent, down_sent, up_grad, down_grad)
    )
    up_sent = from_half(up_sent)
    home_grad = blocks_home(after(grad_rows, home_rows).reshape(groups, -1, model_width))

    expert_out = mm(placed, home_rows.reshape(experts * capacity, model_width))
    block_out = (middle + gate_value[:, None] * expert_out).astype(low_type)
    gate_grad = jnp.sum(grad_out * expert_out, axis=1)
    logit_grad = router_probs * gate_grad[:, None] * (chosen - gate_value[:, None])
    router_grad = lax.dot_general(
        normed_two, logit_grad, ROWS_FIRST, precision=highest, preferred_element_type=float_type
    )
    normed_two_grad = mm(
        placed, home_grad.reshape(experts * capacity, model_width)
    ) + lax.dot_general(
        logit_grad, router, LAST_DIMS, precision=highest, preferred_element_type=float_type
    )
    middle_norm_grad, gain_ffn_grad = norm_two_back(normed_two_grad)
    middle_grad = grad_out + middle_norm_grad
    mixer_grad = (middle_grad * real_rows[:, None]).astype(low_type)
    mixer_grad_all = lax.all_gather(mixer_grad, "ep")
    gated_grad = mm_t(mixer_grad, out_proj)
    scan_grad, gate_pre_low, gate_pre_t, adj_ex, back_cum_ex, adj_all = scan_adjoints(
        gated_grad,
        inner_gate,
        scan_out,
        step_size,
        out_wide,
        reset_wide,
        rates,

    )
    returning = state_after(cums, adj_all, rates, "hs")
    gate_blocks = blocks_home(after(by_owner(gate_pre_t), returning))
    down_sent = from_half(after(down_sent, returning))
    scan_in_grad, size_grad, wide_grads, log_grad, skip_grad = scan_grads(
        mixer_in,
        step_size,
        in_wide,
        out_wide,
        reset_wide,
        rates,
        ends_ex,
        cum_ex,
        entering,
        skip_row,
        scan_grad,
        adj_ex,
        back_cum_ex,
        returning,
        waits=[gated_blocks],
    )
    size_grad = after(size_grad, gate_blocks)
    pre_step_grad, dt_bias_grad = step_back(size_grad)
    pre_step_low = pre_step_grad.astype(low_type)
    rank_grad = mm_t(pre_step_low, dt_proj)
    small_grad = jnp.concatenate([rank_grad, fold_maps(wide_grads)], axis=1).astype(low_type)
    head = CONV - 1
    head_grad = scan_in_grad[:head] + mm_t(small_grad[:head], x_proj)

    def conv_head(rows_part):
        return conv_mix(inner_x[:head], rows_part, start_flags[:head], conv_weight, conv_bias)

    halo_grad = jax.vjp(conv_head, halo_rows)[1](head_grad)[0]
    edge_grad = shifted_2(halo_grad, "hs", -1) * edge_mask
    here = member[None]
    out_gate = block_shares(
        [gated_blocks, gate_blocks], [mixer_grad_all, normed_all], here, members
    )

    inner_low, inner_t, conv_weight_grad, conv_bias_grad = conv_back(
        edge_start[None],
        scan_in_grad,
        small_grad,
        x_proj,
        inner_x,
        jnp.pad(halo_rows, ((8 - head, 0), (0, 0))),
        jnp.pad(edge_grad, ((0, 8 - head), (0, 0))),
        valid,
        conv_weight,
        conv_bias[None, :],
        waits=[out_gate],
    )

    inner_sent = by_owner(inner_t)
    inner_blocks = blocks_home(inner_sent)
    small_rows = [
        log_grad,
        dt_bias_grad[None, :],
        skip_grad,
        router_grad.reshape(inner_width, -1).T,
        conv_weight_grad,
        conv_bias_grad,
    ]
    sizes = [row.shape[0] for row in small_rows]
    packed = channel_pack(
        mixer_low,
        jnp.pad(small_grad, ((0, 0), (0, LANES - small_grad.shape[1]))),
        pre_step_low,
        jnp.pad(rank_low, ((0, 0), (0, LANES - DT_RANK))),
        small_rows,
        waits=[inner_sent],
    )
    inner_part = block_shares(
        [inner_blocks], [normed_all], here, members, waits=[out_gate, packed]
    )
    packed = blocks_home(after(packed, inner_part).reshape(groups, -1, 2 * LANES))
    packed_part = jnp.sum(packed.astype(float_type), axis=0).astype(low_type)
    packed_sum = summed_shares(packed_part.reshape(members, -1, 2 * LANES), "hs")
    inner_low = after(inner_low, inner_part)
    normed_one_grad = mm_t(inner_low, in_proj[:, :inner_width]) + mm_t(
        gate_pre_low, in_proj[:, inner_width:]
    )
    tokens_norm_grad, gain_mix_grad = norm_one_back(normed_one_grad)
    tokens_grad = middle_grad + tokens_norm_grad
    gains = jnp.concatenate([gain_mix_grad, gain_ffn_grad]).reshape(groups * members, -1)
    gains = lax.all_to_all(
        after(gains, packed), ("ep", "hs"), split_axis=0, concat_axis=0, tiled=True
    )
    gains_sum = jnp.sum(gains, axis=0)
    for k in range(1, shares):
        sender = jnp.bitwise_xor(place, k)
        up_other = lax.dynamic_index_in_dim(up_sent, sender, 0, False)[k - 1]
        down_other = lax.dynamic_index_in_dim(after(down_sent, inner_part), sender, 0, False)[k - 1]
        up_grad = up_grad + up_other.astype(float_type)
        down_grad = down_grad + down_other.astype(float_type)

    out_proj_sum, gate_sum = summed_ahead(out_gate, "hs", inner_part)
    inner_sum = summed_ahead(inner_part, "hs")[0]
    given = jnp.where(upper, inner_sum, gate_sum).astype(low_type)
    kept = jnp.where(upper, gate_sum, inner_sum)
    taken = crossed(given, "ep", half).astype(float_type)
    in_proj_sum = jnp.concatenate(
        [jnp.where(upper, taken, kept), jnp.where(upper, kept, taken)], axis=0
    ).T
    cut, at = [], LANES + DT_RANK
    for size in sizes:
        cut.append(packed_sum[:, at : at + size])
        at += size
    return (
        block_out,
        tokens_grad,
        gains_sum,
        cut[3].reshape(-1),
        in_proj_sum,
        cut[4].T,
        cut[5][:, 0],
        packed_sum[:, : DT_RANK + 2 * STATE],
        packed_sum[:, LANES : LANES + DT_RANK].T,
        cut[1][:, 0],
        cut[0],
        cut[2][:, 0],
        out_proj_sum,
        up_grad[None],
        down_grad[None],
    )


def solution(mesh):
    return jax.shard_map(
        body,
        mesh=mesh,
        in_specs=(
            P(("ep", "hs"), None),
            P(("ep", "hs")),
            P(("ep", "hs")),
            P(("ep", "hs")),
            P(("ep", "hs")),
            P(),
            P(),
            P(),
            P(),
            P(),
            P(),
            P(),
            P(),
            P(),
            P(),
            P(),
            P(),
            P("ep", None, "hs"),
            P("ep", "hs", None),
            P(("ep", "hs"), None),
        ),
        out_specs=(
            P(("ep", "hs"), None),
            P(("ep", "hs"), None),
            P(("ep", "hs")),
            P(("ep", "hs")),
            P(None, ("ep", "hs")),
            P(None, ("ep", "hs")),
            P(("ep", "hs")),
            P(("ep", "hs"), None),
            P(None, ("ep", "hs")),
            P(("ep", "hs")),
            P(("ep", "hs"), None),
            P(("ep", "hs")),
            P(("ep", "hs"), None),
            P("ep", None, "hs"),
            P("ep", "hs", None),
        ),
        check_vma=False,
    )
```

```python
import jax
import jax.numpy as jnp
from jax import lax
from jax.experimental import pallas as pl
from jax.experimental.pallas import tpu as pltpu
from jax.sharding import PartitionSpec as P

DT_RANK = 72
CONV = 4
STATE = 16
SEGMENTS = 8
LANES = 128
TILES = 3
RESET = 1e30
LN2 = 0.6931471805599453


def widened(values):
    shaped = values.reshape(SEGMENTS, -1, values.shape[1])
    shaped = jnp.transpose(shaped, (1, 2, 0))[..., None]
    return jnp.broadcast_to(shaped, shaped.shape[:3] + (LANES,))


def each_tile(work):
    @pl.loop(0, TILES)
    def _(k):
        work(pl.ds(pl.multiple_of(k * LANES, LANES), LANES))


def spread_rates(target, rates, lanes):
    for n in range(STATE):
        target[n] = jnp.broadcast_to(rates[n : n + 1, lanes], (SEGMENTS, LANES))


def ends_kernel(x, dt, in_wide, big, rates, ends_ex, cum_ex, end_all, cum_all,
                rate_wide, end_scr, sum_scr, x_scr, dt_scr):
    steps = x.shape[0] // SEGMENTS

    def work(lanes):
        spread_rates(rate_wide, rates, lanes)
        x_scr[...] = x[:, lanes]
        dt_scr[...] = dt[:, lanes]

        def step(i, carry):
            total, states = carry[0], carry[1:]
            rows = pl.ds(i, SEGMENTS, stride=steps)
            stride = dt_scr[rows, :]
            driven = stride * x_scr[rows, :]
            stride = stride + big[i, 0]
            new = [total + stride]
            for n in range(STATE):
                new.append(jnp.exp2(stride * rate_wide[n]) * states[n] + driven * in_wide[i, n])
            return tuple(new)

        zero = jnp.zeros((SEGMENTS, LANES), jnp.float32)
        done = lax.fori_loop(0, steps, step, (zero,) * (STATE + 1), unroll=True)
        sum_scr[...] = done[0]
        for n in range(STATE):
            end_scr[n * SEGMENTS : (n + 1) * SEGMENTS, :] = done[1 + n]
        state = jnp.zeros((STATE, LANES), jnp.float32)
        cum = jnp.zeros((1, LANES), jnp.float32)
        for s in range(SEGMENTS):
            ends_ex[s * STATE : (s + 1) * STATE, lanes] = state
            cum_ex[s : s + 1, lanes] = cum
            own = sum_scr[s : s + 1, :]
            state = (
                jnp.exp2(own * rates[:, lanes]) * state
                + end_scr[pl.ds(s, STATE, stride=SEGMENTS), :]
            )
            cum = cum + own
        end_all[:, lanes] = state
        cum_all[:, lanes] = cum

    each_tile(work)


def opening_states(cum, rate_wide, entering, ends_ex, end_scr, lanes):
    end_scr[...] = ends_ex[:, lanes]
    return tuple(
        jnp.exp2(cum * rate_wide[n]) * entering[n : n + 1, lanes]
        + end_scr[pl.ds(n, SEGMENTS, stride=STATE), :]
        for n in range(STATE)
    )


def outputs_kernel(x, dt, in_wide, out_wide, big, rates, ends_ex, cum_ex, entering, skip, gate,
                   scan_out, gated, gated_t, rate_wide, end_scr, x_scr, dt_scr, out_scr):
    steps = x.shape[0] // SEGMENTS

    def work(lanes):
        spread_rates(rate_wide, rates, lanes)
        x_scr[...] = x[:, lanes]
        dt_scr[...] = dt[:, lanes]
        opening = opening_states(cum_ex[:, lanes], rate_wide, entering, ends_ex, end_scr, lanes)

        def step(i, states):
            rows = pl.ds(i, SEGMENTS, stride=steps)
            stride = dt_scr[rows, :]
            driven = stride * x_scr[rows, :]
            stride = stride + big[i, 0]
            new, total = [], None
            for n in range(STATE):
                state = jnp.exp2(stride * rate_wide[n]) * states[n] + driven * in_wide[i, n]
                new.append(state)
                term = state * out_wide[i, n]
                total = term if total is None else total + term
            out_scr[rows, :] = total
            return tuple(new)

        lax.fori_loop(0, steps, step, opening, unroll=True)
        value = out_scr[...] + skip[:, lanes] * x_scr[...]
        scan_out[:, lanes] = value
        product = value * jax.nn.silu(gate[:, lanes])
        gated[:, lanes] = product.astype(gated.dtype)
        gated_t[lanes, :] = product.T.astype(gated.dtype)

    each_tile(work)


def adjoint_kernel(gated_grad, gate, scan_out, dt, out_wide, big, rates,
                   scan_grad, gate_grad, gate_grad_t, adj_ex, cum_ex, adj_all,
                   rate_wide, end_scr, sum_scr, grad_scr, dt_scr):
    steps = dt.shape[0] // SEGMENTS

    def work(lanes):
        spread_rates(rate_wide, rates, lanes)
        incoming = gated_grad[:, lanes]
        gate_in = gate[:, lanes]
        chance = jax.nn.sigmoid(gate_in)
        moved = incoming * (gate_in * chance)
        scan_grad[:, lanes] = moved
        grad_scr[...] = moved
        dt_scr[...] = dt[:, lanes]
        product = incoming * scan_out[:, lanes] * (chance * (1.0 + gate_in * (1.0 - chance)))
        gate_grad[:, lanes] = product.astype(gate_grad.dtype)
        gate_grad_t[lanes, :] = product.T.astype(gate_grad.dtype)

        def step(k, carry):
            i = steps - 1 - k
            total, tails = carry[0], carry[1:]
            rows = pl.ds(i, SEGMENTS, stride=steps)
            grad = grad_scr[rows, :]
            stride = dt_scr[rows, :] + big[i, 0]
            new = [total + stride]
            for n in range(STATE):
                new.append(jnp.exp2(stride * rate_wide[n]) * (grad * out_wide[i, n] + tails[n]))
            return tuple(new)

        zero = jnp.zeros((SEGMENTS, LANES), jnp.float32)
        done = lax.fori_loop(0, steps, step, (zero,) * (STATE + 1), unroll=True)
        sum_scr[...] = done[0]
        for n in range(STATE):
            end_scr[n * SEGMENTS : (n + 1) * SEGMENTS, :] = done[1 + n]
        tail = jnp.zeros((STATE, LANES), jnp.float32)
        cum = jnp.zeros((1, LANES), jnp.float32)
        for s in reversed(range(SEGMENTS)):
            adj_ex[s * STATE : (s + 1) * STATE, lanes] = tail
            cum_ex[s : s + 1, lanes] = cum
            own = sum_scr[s : s + 1, :]
            tail = (
                jnp.exp2(own * rates[:, lanes]) * tail
                + end_scr[pl.ds(s, STATE, stride=SEGMENTS), :]
            )
            cum = cum + own
        adj_all[:, lanes] = tail

    each_tile(work)


def grads_kernel(x, dt, in_wide, out_wide, big, rates, ends_ex, cum_ex, entering, skip,
                 scan_grad, adj_ex, back_cum_ex, returning, step_pre, step_bias, masks,
                 x_grad, step_grad, map_grad, log_grad, skip_grad, bias_grad,
                 rate_wide, kept, log_scr, end_scr, x_scr, dt_scr, grad_scr, x_out, dt_out):
    steps = x.shape[0] // SEGMENTS

    @pl.when(pl.program_id(0) == 0)
    def _():
        map_grad[...] = jnp.zeros_like(map_grad)

    def work(lanes):
        spread_rates(rate_wide, rates, lanes)
        x_scr[...] = x[:, lanes]
        dt_scr[...] = dt[:, lanes]
        grad_scr[...] = scan_grad[:, lanes]
        opening = opening_states(cum_ex[:, lanes], rate_wide, entering, ends_ex, end_scr, lanes)
        for n in range(STATE):
            kept[0, n] = opening[n]

        def forward(i, states):
            rows = pl.ds(i, SEGMENTS, stride=steps)
            stride = dt_scr[rows, :]
            driven = stride * x_scr[rows, :]
            stride = stride + big[i, 0]
            new = []
            for n in range(STATE):
                state = jnp.exp2(stride * rate_wide[n]) * states[n] + driven * in_wide[i, n]
                kept[i + 1, n] = state
                new.append(state)
            return tuple(new)

        lax.fori_loop(0, steps, forward, opening, unroll=True)
        tails = opening_states(back_cum_ex[:, lanes], rate_wide, returning, adj_ex, end_scr, lanes)
        zero = jnp.zeros((SEGMENTS, LANES), jnp.float32)
        for n in range(STATE):
            log_scr[n] = zero

        def backward(k, tails):
            i = steps - 1 - k
            rows = pl.ds(i, SEGMENTS, stride=steps)
            stride = dt_scr[rows, :]
            value = x_scr[rows, :]
            driven = stride * value
            grad = grad_scr[rows, :]
            marked = stride + big[i, 0]
            new = []
            drive_sum, rate_sum = None, None
            for n in range(STATE):
                rate = rate_wide[n]
                adjoint = grad * out_wide[i, n] + tails[n]
                map_grad[1, i, n] += grad * kept[i + 1, n]
                map_grad[0, i, n] += adjoint * driven
                drive = adjoint * in_wide[i, n]
                tail = jnp.exp2(marked * rate) * adjoint
                touched = tail * kept[i, n]
                slope = touched * rate
                log_scr[n] += touched * stride
                drive_sum = drive if drive_sum is None else drive_sum + drive
                rate_sum = slope if rate_sum is None else rate_sum + slope
                new.append(tail)
            x_out[rows, :] = stride * drive_sum
            dt_out[rows, :] = value * drive_sum + LN2 * rate_sum
            return tuple(new)

        lax.fori_loop(0, steps, backward, tails, unroll=True)
        for n in range(STATE):
            log_grad[n : n + 1, lanes] = (
                jnp.sum(log_scr[n], axis=0, keepdims=True) * rates[n : n + 1, lanes] * LN2
            )
        chance = jax.nn.sigmoid(step_pre[:, lanes] + step_bias[:, lanes])
        moved = dt_out[...] * masks[:, 0:1] * chance
        step_grad[:, lanes] = moved.astype(step_grad.dtype)
        bias_grad[:, lanes] = jnp.sum(moved, axis=0, keepdims=True)
        x_grad[:, lanes] = x_out[...] + skip[:, lanes] * grad_scr[...]
        skip_grad[:, lanes] = jnp.sum(grad_scr[...] * x_scr[...], axis=0, keepdims=True)

    each_tile(work)


def tile(rows):
    return pl.BlockSpec((rows, TILES * LANES), lambda j: (0, j))


def turned(rows):
    return pl.BlockSpec((TILES * LANES, rows), lambda j: (j, 0))


def whole(shape):
    return pl.BlockSpec(shape, lambda j: (0,) * len(shape))


def shape_of(rows, width, dtype=jnp.float32):
    return jax.ShapeDtypeStruct((rows, width), dtype)


PARAMS = pltpu.CompilerParams(
    dimension_semantics=("arbitrary",), vmem_limit_bytes=56 * 1024 * 1024
)
RATE = pltpu.VMEM((STATE, SEGMENTS, LANES), jnp.float32)
ENDS = pltpu.VMEM((SEGMENTS * STATE, LANES), jnp.float32)
SUMS = pltpu.VMEM((SEGMENTS, LANES), jnp.float32)


def call(kernel, waits, micros, **options):
    specs = options.pop("in_specs")

    def waiting(*refs):
        kernel(*refs[: len(specs)], *refs[len(specs) + len(waits) :])

    waiting.__name__ = options["name"]
    run = pl.pallas_call(
        waiting,
        in_specs=specs + [pl.BlockSpec(memory_space=pl.ANY)] * len(waits),
        compiler_params=PARAMS,
        cost_estimate=pl.CostEstimate(
            flops=0, bytes_accessed=micros * 3_000_000, transcendentals=0
        ),
        **options,
    )
    return lambda *operands: run(*operands, *waits)


def rows_of(rows):
    return pltpu.VMEM((rows, LANES), jnp.float32)


def scan_ends(x, dt, in_wide, big, rates, waits=()):
    rows, width = x.shape
    return call(
        ends_kernel,
        waits,
        15,
        grid=(width // (TILES * LANES),),
        in_specs=[tile(rows), tile(rows), whole(in_wide.shape), whole(big.shape), tile(STATE)],
        out_specs=[tile(SEGMENTS * STATE), tile(SEGMENTS), tile(STATE), tile(1)],
        out_shape=[shape_of(SEGMENTS * STATE, width), shape_of(SEGMENTS, width),
                   shape_of(STATE, width), shape_of(1, width)],
        scratch_shapes=[RATE, ENDS, SUMS, rows_of(rows), rows_of(rows)],
        name="scan_ends",
    )(x, dt, in_wide, big, rates)


def scan_outputs(x, dt, in_wide, out_wide, big, rates, ends_ex, cum_ex, entering, skip, gate, waits=()):
    rows, width = x.shape
    return call(
        outputs_kernel,
        waits,
        20,
        grid=(width // (TILES * LANES),),
        in_specs=[tile(rows), tile(rows), whole(in_wide.shape), whole(out_wide.shape),
                  whole(big.shape), tile(STATE), tile(SEGMENTS * STATE), tile(SEGMENTS),
                  tile(STATE), tile(1), tile(rows)],
        out_specs=[tile(rows), tile(rows), turned(rows)],
        out_shape=[shape_of(rows, width), shape_of(rows, width, jnp.bfloat16),
                   shape_of(width, rows, jnp.bfloat16)],
        scratch_shapes=[RATE, ENDS] + [rows_of(rows)] * 3,
        name="scan_outputs",
    )(x, dt, in_wide, out_wide, big, rates, ends_ex, cum_ex, entering, skip, gate)


def scan_adjoints(gated_grad, gate, scan_out, dt, out_wide, big, rates, waits=()):
    rows, width = dt.shape
    return call(
        adjoint_kernel,
        waits,
        17,
        grid=(width // (TILES * LANES),),
        in_specs=[tile(rows), tile(rows), tile(rows), tile(rows), whole(out_wide.shape),
                  whole(big.shape), tile(STATE)],
        out_specs=[tile(rows), tile(rows), turned(rows), tile(SEGMENTS * STATE), tile(SEGMENTS),
                   tile(STATE)],
        out_shape=[shape_of(rows, width), shape_of(rows, width, jnp.bfloat16),
                   shape_of(width, rows, jnp.bfloat16),
                   shape_of(SEGMENTS * STATE, width), shape_of(SEGMENTS, width),
                   shape_of(STATE, width)],
        scratch_shapes=[RATE, ENDS, SUMS, rows_of(rows), rows_of(rows)],
        name="scan_adjoints",
    )(gated_grad, gate, scan_out, dt, out_wide, big, rates)


def scan_grads(x, dt, in_wide, out_wide, big, rates, ends_ex, cum_ex, entering, skip,
               scan_grad, adj_ex, back_cum_ex, returning, step_pre, step_bias, masks, waits=()):
    rows, width = x.shape
    steps = rows // SEGMENTS
    wide_shape = (steps, STATE, SEGMENTS, LANES)
    return call(
        grads_kernel,
        waits,
        55,
        grid=(width // (TILES * LANES),),
        in_specs=[tile(rows), tile(rows), whole(in_wide.shape), whole(out_wide.shape),
                  whole(big.shape), tile(STATE), tile(SEGMENTS * STATE), tile(SEGMENTS),
                  tile(STATE), tile(1), tile(rows), tile(SEGMENTS * STATE), tile(SEGMENTS),
                  tile(STATE), tile(rows), tile(1), whole(masks.shape)],
        out_specs=[tile(rows), tile(rows), whole((2,) + wide_shape), tile(STATE), tile(1),
                   tile(1)],
        out_shape=[shape_of(rows, width), shape_of(rows, width, jnp.bfloat16),
                   jax.ShapeDtypeStruct((2,) + wide_shape, jnp.float32),
                   shape_of(STATE, width), shape_of(1, width), shape_of(1, width)],
        scratch_shapes=[RATE, pltpu.VMEM((steps + 1,) + wide_shape[1:], jnp.float32), RATE, ENDS]
        + [rows_of(rows)] * 5,
        name="scan_grads",
    )(x, dt, in_wide, out_wide, big, rates, ends_ex, cum_ex, entering, skip, scan_grad, adj_ex,
      back_cum_ex, returning, step_pre, step_bias, masks)


def fold_maps(wide):
    summed = jnp.sum(wide, axis=4)
    return jnp.transpose(summed, (3, 1, 0, 2)).reshape(-1, 2 * STATE)


def conv_back_kernel(edge_start, scan_grad, small_grad, x_proj, x, halo, edge, valid, weight, bias,
                     x_grad, x_grad_t, weight_grad, bias_grad, x_ext, g_ext, valid_wide):
    rows = x.shape[0]
    taps = weight.shape[0]
    position = lax.broadcasted_iota(jnp.int32, (rows, LANES), 0)
    first = edge_start[0]

    @pl.when(pl.program_id(0) == 0)
    def _():
        for k in range(1, taps):
            valid_wide[k] = jnp.broadcast_to(valid[:, k : k + 1], (rows, LANES))
        g_ext[rows : rows + 8, :] = jnp.zeros((8, LANES), jnp.float32)

    def work(lanes):
        grad = scan_grad[:, lanes] + lax.dot_general(
            small_grad[...], x_proj[:, lanes], (((1,), (0,)), ((), ())),
            preferred_element_type=jnp.float32,
        )
        x_ext[0:8, :] = halo[:, lanes]
        x_ext[8 : 8 + rows, :] = x[:, lanes]
        pre = bias[:, lanes] + weight[taps - 1 : taps, lanes] * x[:, lanes]
        for k in range(1, taps):
            tap = weight[taps - 1 - k : taps - k, lanes]
            pre = pre + tap * x_ext[8 - k : 8 - k + rows, :] * valid_wide[k]
        chance = jax.nn.sigmoid(pre)
        grad = grad * (chance * (1.0 + pre * (1.0 - chance)))
        bias_grad[:, lanes] = jnp.sum(grad, axis=0, keepdims=True)
        weight_grad[taps - 1 : taps, lanes] = jnp.sum(grad * x[:, lanes], axis=0, keepdims=True)
        total = weight[taps - 1 : taps, lanes] * grad
        for k in range(1, taps):
            masked = grad * valid_wide[k]
            weight_grad[taps - 1 - k : taps - k, lanes] = jnp.sum(
                masked * x_ext[8 - k : 8 - k + rows, :], axis=0, keepdims=True
            )
            g_ext[0:rows, :] = masked
            total = total + weight[taps - 1 - k : taps - k, lanes] * g_ext[k : k + rows, :]
        for j in range(taps - 1):
            total = total + jnp.where(position == first + j, edge[j : j + 1, lanes], 0.0)
        x_grad[:, lanes] = total.astype(x_grad.dtype)
        x_grad_t[lanes, :] = total.T.astype(x_grad_t.dtype)

    each_tile(work)


def conv_back(edge_start, scan_grad, small_grad, x_proj, x, halo, edge, valid, weight, bias,
              waits=()):
    rows, width = scan_grad.shape
    taps = weight.shape[0]
    scratch = pltpu.VMEM((rows + 8, LANES), jnp.float32)
    return call(
        conv_back_kernel,
        waits,
        6,
        grid=(width // (TILES * LANES),),
        in_specs=[pl.BlockSpec(memory_space=pltpu.SMEM), tile(rows), whole(small_grad.shape),
                  tile(x_proj.shape[0]), tile(rows),
                  tile(8), tile(8), whole(valid.shape), tile(taps), tile(1)],
        out_specs=[tile(rows), turned(rows), tile(taps), tile(1)],
        out_shape=[shape_of(rows, width, jnp.bfloat16), shape_of(width, rows, jnp.bfloat16),
                   shape_of(taps, width), shape_of(1, width)],
        scratch_shapes=[scratch, scratch, pltpu.VMEM((taps, rows, LANES), jnp.float32)],
        name="conv_back",
    )(edge_start, scan_grad, small_grad, x_proj, x, halo, edge, valid, weight, bias)


def shares_kernel(place, *refs):
    out, pairs = refs[-1], len(refs) // 2
    members, wide = out.shape[0], out.shape[2]
    for p in range(pairs):
        left, right = refs[p], refs[pairs + p]
        blocks = left.shape[0]
        whole_left = jnp.concatenate([left[b] for b in range(blocks)], axis=1)
        whole_right = right[...].reshape(-1, right.shape[2])
        total = jnp.dot(whole_left, whole_right, preferred_element_type=jnp.float32)
        for h in range(members):
            after_this = lax.rem(h - place[0] + members, members)
            out[after_this, p] = total[h * wide : (h + 1) * wide].astype(out.dtype)


def block_shares(lefts, rights, place, members, waits=()):
    blocks, channels, tokens = lefts[0].shape
    width = rights[0].shape[2]
    columns = TILES * LANES
    out = (members, len(lefts), channels // members)
    return call(
        shares_kernel,
        waits,
        0,
        grid=(width // columns,),
        in_specs=[pl.BlockSpec(memory_space=pltpu.SMEM)]
        + [whole(lefts[0].shape)] * len(lefts)
        + [pl.BlockSpec((blocks, tokens, columns), lambda j: (0, 0, j))] * len(lefts),
        out_specs=pl.BlockSpec(out + (columns,), lambda j: (0, 0, 0, j)),
        out_shape=jax.ShapeDtypeStruct(out + (width,), jnp.bfloat16),
        scratch_shapes=[],
        name="block_shares",
    )(place, *lefts, *rights)


def pack_kernel(mixer, small, step, rank, *refs):
    out, rows = refs[-1], refs[:-1]
    first = (((0,), (0,)), ((), ()))
    out[:, :LANES] = lax.dot_general(
        mixer[...], small[...], first, preferred_element_type=jnp.float32
    ).astype(out.dtype)
    total = lax.dot_general(step[...], rank[...], first, preferred_element_type=jnp.float32)
    at = DT_RANK
    for row in rows:
        size = row.shape[0]
        line = lax.broadcasted_iota(jnp.int32, (size, LANES), 0)
        lane = lax.broadcasted_iota(jnp.int32, (size, LANES), 1)
        spot = (lane == line + at).astype(jnp.float32).astype(out.dtype)
        total = total + lax.dot_general(
            row[...].astype(out.dtype), spot, first, preferred_element_type=jnp.float32
        )
        at += size
    out[:, LANES:] = total.astype(out.dtype)


def channel_pack(mixer, small, step, rank, rows, waits=()):
    length, width = mixer.shape
    return call(
        pack_kernel,
        waits,
        3,
        grid=(width // (TILES * LANES),),
        in_specs=[tile(length), whole(small.shape), tile(length), whole(rank.shape)]
        + [tile(row.shape[0]) for row in rows],
        out_specs=pl.BlockSpec((TILES * LANES, 2 * LANES), lambda j: (j, 0)),
        out_shape=shape_of(width, 2 * LANES, jnp.bfloat16),
        scratch_shapes=[],
        name="channel_pack",
    )(mixer, small, step, rank, *rows)


norm_epsilon = 1e-05
highest = lax.Precision.HIGHEST
ROWS_FIRST = (((0,), (0,)), ((), ()))
LAST_DIMS = (((1,), (1,)), ((), ()))


def shifted_2(block, axis, distance):
    devices = range(lax.axis_size(axis))
    route = [(i - distance, i) for i in devices if i - distance in devices]
    return lax.ppermute(block, axis, route)


def crossed(block, axis, mask):
    return lax.ppermute(block, axis, [(i, i ^ mask) for i in range(lax.axis_size(axis))])


def exchanged(blocks, axis):
    return [block if k == 0 else crossed(block, axis, k) for k, block in enumerate(blocks)]


def after(value, *others):
    return lax.optimization_barrier((value,) + others)[0]


def summed_ahead(parts, axis, *others):
    count = lax.axis_size(axis)
    total = parts[0].astype(jnp.float32)
    for k in range(1, count):
        route = [(i, (i + k) % count) for i in range(count)]
        total = total + after(lax.ppermute(parts[k], axis, route), *others).astype(jnp.float32)
    return total


def summed_shares(parts, axis):
    count, mine = lax.axis_size(axis), lax.axis_index(axis)
    return summed_ahead(
        [
            lax.dynamic_index_in_dim(parts, lax.rem(mine + k, count), 0, False)
            for k in range(count)
        ],
        axis,
    )


def around(value, axis):
    count = lax.axis_size(axis)
    return [value] + [
        lax.ppermute(value, axis, [(i, (i + k) % count) for i in range(count)])
        for k in range(1, count)
    ]


def state_before(cum, end, rates, axis):
    count, mine = lax.axis_size(axis), lax.axis_index(axis)
    first = lax.reduce_precision(cum, 8, 7)
    second = lax.reduce_precision(cum - first, 8, 7)
    sent = jnp.concatenate([end, first, second, cum - first - second], axis=0)
    got = [part.astype(jnp.float32) for part in around(sent.astype(jnp.bfloat16), axis)]
    cums = [jnp.sum(part[end.shape[0] :], axis=0, keepdims=True) for part in got]
    state = jnp.zeros_like(end)
    for k in reversed(range(1, count)):
        longer = jnp.exp2(cums[k] * rates) * state + got[k][: end.shape[0]]
        state = jnp.where(k <= mine, longer, state)
    return state, cums


def state_after(cums, tail, rates, axis):
    count, mine = lax.axis_size(axis), lax.axis_index(axis)
    got = [part.astype(jnp.float32) for part in around(tail.astype(jnp.bfloat16), axis)]
    state = jnp.zeros_like(tail)
    for k in range(1, count):
        longer = jnp.exp2(cums[k] * rates) * state + got[k]
        state = jnp.where(mine + count - k < count, longer, state)
    return state


def rms_scale(values):
    return lax.rsqrt(jnp.mean(values * values, axis=1, keepdims=True) + norm_epsilon)


def scaled_norm(values, gain_row):
    return values * rms_scale(values) * gain_row[None, :]


def gelu_tanh(values):
    return jax.nn.gelu(values, approximate=True)


def conv_mix(x_inner, halo_rows, start_flags, conv_w, conv_b):
    tap_count = conv_w.shape[0]
    length = x_inner.shape[0]
    extended = jnp.concatenate([halo_rows, x_inner], axis=0)
    flag_line = jnp.concatenate([jnp.zeros((tap_count - 1,), jnp.float32), start_flags], axis=0)
    result = conv_b[None, :] + conv_w[tap_count - 1][None, :] * x_inner
    survive = jnp.ones((length,), jnp.float32)
    for offset in range(1, tap_count):
        survive = survive * (1.0 - flag_line[tap_count - offset : tap_count - offset + length])
        shifted = extended[tap_count - 1 - offset : tap_count - 1 - offset + length]
        result = result + conv_w[tap_count - 1 - offset][None, :] * shifted * survive[:, None]
    return jax.nn.silu(result)


def delta_apply(step_pre, bias_row, real_rows):
    return jax.nn.softplus(step_pre + bias_row[None, :]) * real_rows[:, None]


def mm(left, right):
    return jnp.dot(left, right, preferred_element_type=jnp.float32)


def mm_t(left, right):
    return lax.dot_general(left, right, LAST_DIMS, preferred_element_type=jnp.float32)


def t_mm(left, right):
    return lax.dot_general(left, right, ROWS_FIRST, preferred_element_type=jnp.float32)


def body(
    tokens,
    starts,
    counts,
    routes,
    slot_index,
    gain_mix,
    in_proj,
    conv_weight,
    conv_bias,
    x_proj,
    dt_proj,
    dt_bias,
    a_log,
    skip_gain,
    out_proj,
    gain_ffn,
    router,
    up_proj,
    down_proj,
    out_grad,
):
    float_type = jnp.float32
    low_type = jnp.bfloat16
    length = tokens.shape[0]
    model_width = tokens.shape[1]
    inner_width = conv_bias.shape[0]
    experts = router.shape[1]
    capacity = 5 * length // (4 * experts)
    groups, members = lax.axis_size("ep"), lax.axis_size("hs")
    group, member = lax.axis_index("ep"), lax.axis_index("hs")
    half = groups // 2
    upper = group >= half

    def blocks_home(values):
        return lax.all_to_all(values, "ep", split_axis=0, concat_axis=0, tiled=True)

    def by_owner(values):
        wide = inner_width // (half * members * 2)
        shaped = values.reshape(half, members, 2, wide, length)
        return jnp.transpose(shaped, (2, 0, 1, 3, 4)).reshape(groups, -1, length)

    up_own, down_own = up_proj[0], down_proj[0]
    shares = members // 2
    ones = [2 * k + k.bit_count() % 2 for k in range(shares)]
    alike = []
    for g in range(groups):
        if g % 2 == 0:
            halves = [range(shares), range(shares, members)]
        else:
            halves = [ones, [mask ^ 1 for mask in ones]]
        alike += [[g * members + h for h in chosen_half] for chosen_half in halves]
    odd_group = lax.rem(group, 2)
    place = jnp.where(odd_group == 0, lax.rem(member, shares), member // 2)

    def to_other_half(block):
        masks = [shares, 1]
        route = [
            (g * members + h, g * members + (h ^ masks[g % 2]))
            for g in range(groups)
            for h in range(members)
        ]
        return lax.ppermute(block, ("ep", "hs"), route)

    def from_half(block):
        return lax.all_gather(block, ("ep", "hs"), axis_index_groups=alike)


    edge_start = counts[0] - (CONV - 1)
    start_flags = starts.astype(float_type)
    real_rows = (jnp.arange(length, dtype=jnp.int32) < counts[0]).astype(float_type)
    tokens_float = tokens.astype(float_type)
    normed_one, norm_one_back = jax.vjp(scaled_norm, tokens_float, gain_mix)
    normed_low = normed_one.astype(low_type)
    normed_all = lax.all_gather(normed_low, "ep")
    projected = mm(normed_low, in_proj)
    inner_x = projected[:, :inner_width]
    inner_gate = projected[:, inner_width:]
    edge_rows = lax.dynamic_slice_in_dim(inner_x, edge_start, CONV - 1, 0)
    edge_flags = lax.dynamic_slice_in_dim(start_flags, edge_start, CONV - 1, 0)
    later = [jnp.prod(1.0 - edge_flags[k + 1 :]) for k in range(CONV - 1)]
    edge_mask = jnp.stack(later)[:, None]
    halo_rows = shifted_2(edge_rows * edge_mask, "hs", 1)
    kept_taps = [jnp.ones((length,), float_type)]
    flag_line = jnp.concatenate([jnp.zeros((CONV - 1,), float_type), start_flags])
    for k in range(1, CONV):
        kept_taps.append(kept_taps[-1] * (1.0 - flag_line[CONV - k : CONV - k + length]))
    masks = jnp.stack([real_rows] + kept_taps[1:], axis=1)

    ups = from_half(after(up_own, halo_rows))

    mixer_in = conv_mix(inner_x, halo_rows, start_flags, conv_weight, conv_bias)
    mixer_low = mixer_in.astype(low_type)
    small_proj = mm(mixer_low, x_proj)
    rank_low = small_proj[:, :DT_RANK].astype(low_type)
    step_pre = mm(rank_low, dt_proj)
    input_map = small_proj[:, DT_RANK : DT_RANK + STATE]
    output_map = small_proj[:, DT_RANK + STATE :]

    step_size = delta_apply(step_pre, dt_bias, real_rows)
    in_wide, out_wide = widened(input_map), widened(output_map)
    reset_wide = widened(start_flags[:, None] * RESET)
    rates = -(jnp.exp(a_log) / LN2).T
    skip_row = skip_gain[None, :]
    ends_ex, cum_ex, end_all, cum_all = scan_ends(
        mixer_in, step_size, in_wide, reset_wide, rates
    )
    entering, cums = state_before(cum_all, end_all, rates, "hs")
    downs = from_half(after(down_own, entering))
    scan_out, gated_low, gated_t = scan_outputs(
        mixer_in,
        step_size,
        in_wide,
        out_wide,
        reset_wide,
        rates,
        ends_ex,
        cum_ex,
        entering,
        skip_row,
        inner_gate,

    )
    mixer_out = mm(gated_low, out_proj)
    middle = tokens_float + mixer_out * real_rows[:, None]
    normed_two, norm_two_back = jax.vjp(scaled_norm, middle, gain_ffn)
    router_probs = jax.nn.softmax(
        jnp.dot(normed_two, router, precision=highest, preferred_element_type=float_type), axis=1
    )
    chosen = (routes[:, None] == jnp.arange(experts, dtype=jnp.int32)[None, :]).astype(float_type)
    gate_value = jnp.sum(router_probs * chosen, axis=1)
    column = routes * capacity + slot_index
    placed = (
        (column[:, None] == jnp.arange(experts * capacity, dtype=jnp.int32)[None, :])
        & (slot_index[:, None] >= 0)
    ).astype(low_type)
    grad_out = out_grad.astype(float_type)
    token_grad = grad_out * gate_value[:, None]

    rows_low = t_mm(placed, normed_two.astype(low_type)).astype(low_type)
    rows_own = blocks_home(rows_low.reshape(experts, capacity, model_width)).reshape(
        -1, model_width
    )
    rows_pair = to_other_half(rows_own)
    grads_low = t_mm(placed, token_grad.astype(low_type)).astype(low_type)
    grads_own = blocks_home(grads_low.reshape(experts, capacity, model_width)).reshape(
        -1, model_width
    )
    grads_pair = to_other_half(after(grads_own, rows_pair))
    gated_blocks = blocks_home(after(gated_t, grads_own).reshape(groups, -1, length))
    rows = jnp.concatenate([rows_own, rows_pair], axis=0)

    def near_parts(gathered):
        return [
            lax.dynamic_index_in_dim(gathered, jnp.bitwise_xor(place, k), 0, False)
            for k in range(shares)
        ]

    up_all, down_all = near_parts(ups), near_parts(downs)
    pre_all = [mm(rows, up) for up in up_all]
    hidden_all, gelu_backs = zip(*[jax.vjp(gelu_tanh, pre) for pre in pre_all])
    hidden_all = [hidden.astype(low_type) for hidden in hidden_all]
    expert_part = sum(mm(hidden, down) for hidden, down in zip(hidden_all, down_all))
    count = rows_own.shape[0]

    def pair_sum(partial, *earlier):
        other = to_other_half(after(partial[count:].astype(low_type), *earlier))
        return (partial[:count] + other.astype(float_type)).astype(low_type), other

    back_rows, rows_other = pair_sum(expert_part, grads_pair)
    home_rows = blocks_home(back_rows.reshape(groups, -1, model_width))
    grads = jnp.concatenate([grads_own, after(grads_pair, expert_part)], axis=0)
    pre_grads = [
        back(mm_t(grads, down))[0].astype(low_type) for back, down in zip(gelu_backs, down_all)
    ]
    grad_part = sum(mm_t(pre_grad, up) for pre_grad, up in zip(pre_grads, up_all))
    rows, grads = after(rows, rows_other), after(grads, rows_other)
    up_parts = [t_mm(rows, pre_grad) for pre_grad in pre_grads]
    down_parts = [t_mm(hidden, grads) for hidden in hidden_all]
    up_sent = jnp.stack([part.astype(low_type) for part in up_parts[1:]])
    down_sent = jnp.stack([part.astype(low_type) for part in down_parts[1:]])
    grad_rows, _ = pair_sum(grad_part, rows_other)
    up_grad, down_grad = up_parts[0], down_parts[0]
    grad_rows, up_sent, down_sent, up_grad, down_grad = lax.optimization_barrier(
        (grad_rows, up_sent, down_sent, up_grad, down_grad)
    )
    up_sent = from_half(up_sent)
    home_grad = blocks_home(after(grad_rows, home_rows).reshape(groups, -1, model_width))

    expert_out = mm(placed, home_rows.reshape(experts * capacity, model_width))
    block_out = (middle + gate_value[:, None] * expert_out).astype(low_type)
    gate_grad = jnp.sum(grad_out * expert_out, axis=1)
    logit_grad = router_probs * gate_grad[:, None] * (chosen - gate_value[:, None])
    router_grad = lax.dot_general(
        normed_two, logit_grad, ROWS_FIRST, precision=highest, preferred_element_type=float_type
    )
    normed_two_grad = mm(
        placed, home_grad.reshape(experts * capacity, model_width)
    ) + lax.dot_general(
        logit_grad, router, LAST_DIMS, precision=highest, preferred_element_type=float_type
    )
    middle_norm_grad, gain_ffn_grad = norm_two_back(normed_two_grad)
    middle_grad = grad_out + middle_norm_grad
    mixer_grad = (middle_grad * real_rows[:, None]).astype(low_type)
    mixer_grad_all = lax.all_gather(mixer_grad, "ep")
    gated_grad = mm_t(mixer_grad, out_proj)
    scan_grad, gate_pre_low, gate_pre_t, adj_ex, back_cum_ex, adj_all = scan_adjoints(
        gated_grad,
        inner_gate,
        scan_out,
        step_size,
        out_wide,
        reset_wide,
        rates,

    )
    returning = state_after(cums, adj_all, rates, "hs")
    gate_blocks = blocks_home(after(by_owner(gate_pre_t), returning))
    down_sent = from_half(after(down_sent, returning))
    scan_in_grad, pre_step_low, wide_grads, log_grad, skip_grad, dt_bias_grad = scan_grads(
        mixer_in,
        step_size,
        in_wide,
        out_wide,
        reset_wide,
        rates,
        ends_ex,
        cum_ex,
        entering,
        skip_row,
        scan_grad,
        adj_ex,
        back_cum_ex,
        returning,
        step_pre,
        dt_bias[None, :],
        masks,
        waits=[gated_blocks],
    )
    pre_step_low = after(pre_step_low, gate_blocks)
    rank_grad = mm_t(pre_step_low, dt_proj)
    small_grad = jnp.concatenate([rank_grad, fold_maps(wide_grads)], axis=1).astype(low_type)
    head = CONV - 1
    head_grad = scan_in_grad[:head] + mm_t(small_grad[:head], x_proj)

    def conv_head(rows_part):
        return conv_mix(inner_x[:head], rows_part, start_flags[:head], conv_weight, conv_bias)

    halo_grad = jax.vjp(conv_head, halo_rows)[1](head_grad)[0]
    here = member[None]
    out_gate = block_shares(
        [gated_blocks, gate_blocks], [mixer_grad_all, normed_all], here, members
    )
    edge_grad = after(shifted_2(halo_grad, "hs", -1), out_gate) * edge_mask
    inner_low, inner_t, conv_weight_grad, conv_bias_grad = conv_back(
        edge_start[None],
        scan_in_grad,
        small_grad,
        x_proj.T,
        inner_x,
        jnp.pad(halo_rows, ((8 - head, 0), (0, 0))),
        jnp.pad(edge_grad, ((0, 8 - head), (0, 0))),
        masks,
        conv_weight,
        conv_bias[None, :],
        waits=[out_gate],
    )

    inner_sent = by_owner(inner_t)
    inner_blocks = blocks_home(inner_sent)
    small_rows = [
        log_grad,
        dt_bias_grad,
        skip_grad,
        after(router_grad, inner_sent).reshape(inner_width, -1).T,
        conv_weight_grad,
        conv_bias_grad,
    ]
    sizes = [row.shape[0] for row in small_rows]
    packed = channel_pack(
        mixer_low,
        jnp.pad(small_grad, ((0, 0), (0, LANES - small_grad.shape[1]))),
        pre_step_low,
        jnp.pad(rank_low, ((0, 0), (0, LANES - DT_RANK))),
        small_rows,
        waits=[inner_sent],
    )
    inner_part = block_shares(
        [inner_blocks], [normed_all], here, members, waits=[out_gate, packed]
    )
    packed = blocks_home(after(packed, inner_part).reshape(groups, -1, 2 * LANES))
    packed_part = jnp.sum(packed.astype(float_type), axis=0).astype(low_type)
    packed_sum = summed_shares(packed_part.reshape(members, -1, 2 * LANES), "hs")
    inner_low = after(inner_low, inner_part)
    normed_one_grad = mm_t(inner_low, in_proj[:, :inner_width]) + mm_t(
        after(gate_pre_low, inner_part), in_proj[:, inner_width:]
    )
    tokens_norm_grad, gain_mix_grad = norm_one_back(normed_one_grad)
    tokens_grad = middle_grad + tokens_norm_grad
    gains = jnp.concatenate([gain_mix_grad, gain_ffn_grad]).reshape(groups * members, -1)
    gains = lax.all_to_all(
        after(gains, packed), ("ep", "hs"), split_axis=0, concat_axis=0, tiled=True
    )
    gains_sum = jnp.sum(gains, axis=0)
    for k in range(1, shares):
        sender = jnp.bitwise_xor(place, k)
        up_other = lax.dynamic_index_in_dim(after(up_sent, inner_part), sender, 0, False)[k - 1]
        down_other = lax.dynamic_index_in_dim(after(down_sent, inner_part), sender, 0, False)[k - 1]
        up_grad = up_grad + up_other.astype(float_type)
        down_grad = down_grad + down_other.astype(float_type)

    inner_sum = summed_ahead(inner_part, "hs")[0]
    out_proj_sum, gate_sum = summed_ahead(out_gate, "hs", inner_sum)
    given = jnp.where(upper, inner_sum, gate_sum).astype(low_type)
    given = after(given, gains_sum, packed_sum)
    kept = jnp.where(upper, gate_sum, inner_sum)
    taken = crossed(given, "ep", half).astype(float_type)
    in_proj_sum = jnp.concatenate(
        [jnp.where(upper, taken, kept), jnp.where(upper, kept, taken)], axis=0
    ).T
    cut, at = [], LANES + DT_RANK
    for size in sizes:
        cut.append(packed_sum[:, at : at + size])
        at += size
    return (
        block_out,
        tokens_grad,
        gains_sum,
        cut[3].reshape(-1),
        in_proj_sum,
        cut[4].T,
        cut[5][:, 0],
        packed_sum[:, : DT_RANK + 2 * STATE],
        packed_sum[:, LANES : LANES + DT_RANK].T,
        cut[1][:, 0],
        cut[0],
        cut[2][:, 0],
        out_proj_sum,
        up_grad[None],
        down_grad[None],
    )


def solution(mesh):
    return jax.shard_map(
        body,
        mesh=mesh,
        in_specs=(
            P(("ep", "hs"), None),
            P(("ep", "hs")),
            P(("ep", "hs")),
            P(("ep", "hs")),
            P(("ep", "hs")),
            P(),
            P(),
            P(),
            P(),
            P(),
            P(),
            P(),
            P(),
            P(),
            P(),
            P(),
            P(),
            P("ep", None, "hs"),
            P("ep", "hs", None),
            P(("ep", "hs"), None),
        ),
        out_specs=(
            P(("ep", "hs"), None),
            P(("ep", "hs"), None),
            P(("ep", "hs")),
            P(("ep", "hs")),
            P(None, ("ep", "hs")),
            P(None, ("ep", "hs")),
            P(("ep", "hs")),
            P(("ep", "hs"), None),
            P(None, ("ep", "hs")),
            P(("ep", "hs")),
            P(("ep", "hs"), None),
            P(("ep", "hs")),
            P(("ep", "hs"), None),
            P("ep", None, "hs"),
            P("ep", "hs", None),
        ),
        check_vma=False,
    )
```

```python
import jax
import jax.numpy as jnp
from jax import lax
from jax.experimental import pallas as pl
from jax.experimental.pallas import tpu as pltpu
from jax.sharding import PartitionSpec as P

DT_RANK = 72
CONV = 4
STATE = 16
SEGMENTS = 8
LANES = 128
TILES = 3
RESET = 1e30
LN2 = 0.6931471805599453


def widened(values):
    shaped = values.reshape(SEGMENTS, -1, values.shape[1])
    shaped = jnp.transpose(shaped, (1, 2, 0))[..., None]
    return jnp.broadcast_to(shaped, shaped.shape[:3] + (LANES,))


def each_tile(work):
    @pl.loop(0, TILES)
    def _(k):
        work(pl.ds(pl.multiple_of(k * LANES, LANES), LANES))


def spread_rates(target, rates, lanes):
    for n in range(STATE):
        target[n] = jnp.broadcast_to(rates[n : n + 1, lanes], (SEGMENTS, LANES))


def ends_kernel(x, dt, in_wide, big, rates, ends_ex, cum_ex, end_all, cum_all,
                rate_wide, end_scr, sum_scr, x_scr, dt_scr):
    steps = x.shape[0] // SEGMENTS

    def work(lanes):
        spread_rates(rate_wide, rates, lanes)
        x_scr[...] = x[:, lanes]
        dt_scr[...] = dt[:, lanes]

        def step(i, carry):
            total, states = carry[0], carry[1:]
            rows = pl.ds(i, SEGMENTS, stride=steps)
            stride = dt_scr[rows, :]
            driven = stride * x_scr[rows, :]
            stride = stride + big[i, 0]
            new = [total + stride]
            for n in range(STATE):
                new.append(jnp.exp2(stride * rate_wide[n]) * states[n] + driven * in_wide[i, n])
            return tuple(new)

        zero = jnp.zeros((SEGMENTS, LANES), jnp.float32)
        done = lax.fori_loop(0, steps, step, (zero,) * (STATE + 1), unroll=True)
        sum_scr[...] = done[0]
        for n in range(STATE):
            end_scr[n * SEGMENTS : (n + 1) * SEGMENTS, :] = done[1 + n]
        state = jnp.zeros((STATE, LANES), jnp.float32)
        cum = jnp.zeros((1, LANES), jnp.float32)
        for s in range(SEGMENTS):
            ends_ex[s * STATE : (s + 1) * STATE, lanes] = state
            cum_ex[s : s + 1, lanes] = cum
            own = sum_scr[s : s + 1, :]
            state = (
                jnp.exp2(own * rates[:, lanes]) * state
                + end_scr[pl.ds(s, STATE, stride=SEGMENTS), :]
            )
            cum = cum + own
        end_all[:, lanes] = state
        cum_all[:, lanes] = cum

    each_tile(work)


def opening_states(cum, rate_wide, entering, ends_ex, end_scr, lanes):
    end_scr[...] = ends_ex[:, lanes]
    return tuple(
        jnp.exp2(cum * rate_wide[n]) * entering[n : n + 1, lanes]
        + end_scr[pl.ds(n, SEGMENTS, stride=STATE), :]
        for n in range(STATE)
    )


def outputs_kernel(x, dt, in_wide, out_wide, big, rates, ends_ex, cum_ex, entering, skip, gate,
                   scan_out, gated, gated_t, rate_wide, end_scr, x_scr, dt_scr, out_scr):
    steps = x.shape[0] // SEGMENTS

    def work(lanes):
        spread_rates(rate_wide, rates, lanes)
        x_scr[...] = x[:, lanes]
        dt_scr[...] = dt[:, lanes]
        opening = opening_states(cum_ex[:, lanes], rate_wide, entering, ends_ex, end_scr, lanes)

        def step(i, states):
            rows = pl.ds(i, SEGMENTS, stride=steps)
            stride = dt_scr[rows, :]
            driven = stride * x_scr[rows, :]
            stride = stride + big[i, 0]
            new, total = [], None
            for n in range(STATE):
                state = jnp.exp2(stride * rate_wide[n]) * states[n] + driven * in_wide[i, n]
                new.append(state)
                term = state * out_wide[i, n]
                total = term if total is None else total + term
            out_scr[rows, :] = total
            return tuple(new)

        lax.fori_loop(0, steps, step, opening, unroll=True)
        value = out_scr[...] + skip[:, lanes] * x_scr[...]
        scan_out[:, lanes] = value
        product = value * jax.nn.silu(gate[:, lanes])
        gated[:, lanes] = product.astype(gated.dtype)
        gated_t[lanes, :] = product.T.astype(gated.dtype)

    each_tile(work)


def adjoint_kernel(gated_grad, gate, scan_out, dt, out_wide, big, rates,
                   scan_grad, gate_grad, gate_grad_t, adj_ex, cum_ex, adj_all,
                   rate_wide, end_scr, sum_scr, grad_scr, dt_scr):
    steps = dt.shape[0] // SEGMENTS

    def work(lanes):
        spread_rates(rate_wide, rates, lanes)
        incoming = gated_grad[:, lanes]
        gate_in = gate[:, lanes]
        chance = jax.nn.sigmoid(gate_in)
        moved = incoming * (gate_in * chance)
        scan_grad[:, lanes] = moved
        grad_scr[...] = moved
        dt_scr[...] = dt[:, lanes]
        product = incoming * scan_out[:, lanes] * (chance * (1.0 + gate_in * (1.0 - chance)))
        gate_grad[:, lanes] = product.astype(gate_grad.dtype)
        gate_grad_t[lanes, :] = product.T.astype(gate_grad.dtype)

        def step(k, carry):
            i = steps - 1 - k
            total, tails = carry[0], carry[1:]
            rows = pl.ds(i, SEGMENTS, stride=steps)
            grad = grad_scr[rows, :]
            stride = dt_scr[rows, :] + big[i, 0]
            new = [total + stride]
            for n in range(STATE):
                new.append(jnp.exp2(stride * rate_wide[n]) * (grad * out_wide[i, n] + tails[n]))
            return tuple(new)

        zero = jnp.zeros((SEGMENTS, LANES), jnp.float32)
        done = lax.fori_loop(0, steps, step, (zero,) * (STATE + 1), unroll=True)
        sum_scr[...] = done[0]
        for n in range(STATE):
            end_scr[n * SEGMENTS : (n + 1) * SEGMENTS, :] = done[1 + n]
        tail = jnp.zeros((STATE, LANES), jnp.float32)
        cum = jnp.zeros((1, LANES), jnp.float32)
        for s in reversed(range(SEGMENTS)):
            adj_ex[s * STATE : (s + 1) * STATE, lanes] = tail
            cum_ex[s : s + 1, lanes] = cum
            own = sum_scr[s : s + 1, :]
            tail = (
                jnp.exp2(own * rates[:, lanes]) * tail
                + end_scr[pl.ds(s, STATE, stride=SEGMENTS), :]
            )
            cum = cum + own
        adj_all[:, lanes] = tail

    each_tile(work)


def grads_kernel(x, dt, in_wide, out_wide, big, rates, ends_ex, cum_ex, entering, skip,
                 scan_grad, adj_ex, back_cum_ex, returning, step_pre, step_bias, masks,
                 x_grad, step_grad, map_grad, log_grad, skip_grad, bias_grad,
                 rate_wide, kept, log_scr, end_scr, x_scr, dt_scr, grad_scr, x_out, dt_out):
    steps = x.shape[0] // SEGMENTS

    @pl.when(pl.program_id(0) == 0)
    def _():
        map_grad[...] = jnp.zeros_like(map_grad)

    def work(lanes):
        spread_rates(rate_wide, rates, lanes)
        x_scr[...] = x[:, lanes]
        dt_scr[...] = dt[:, lanes]
        grad_scr[...] = scan_grad[:, lanes]
        opening = opening_states(cum_ex[:, lanes], rate_wide, entering, ends_ex, end_scr, lanes)
        for n in range(STATE):
            kept[0, n] = opening[n]

        def forward(i, states):
            rows = pl.ds(i, SEGMENTS, stride=steps)
            stride = dt_scr[rows, :]
            driven = stride * x_scr[rows, :]
            stride = stride + big[i, 0]
            new = []
            for n in range(STATE):
                state = jnp.exp2(stride * rate_wide[n]) * states[n] + driven * in_wide[i, n]
                kept[i + 1, n] = state
                new.append(state)
            return tuple(new)

        lax.fori_loop(0, steps, forward, opening, unroll=True)
        tails = opening_states(back_cum_ex[:, lanes], rate_wide, returning, adj_ex, end_scr, lanes)
        zero = jnp.zeros((SEGMENTS, LANES), jnp.float32)
        for n in range(STATE):
            log_scr[n] = zero

        def backward(k, tails):
            i = steps - 1 - k
            rows = pl.ds(i, SEGMENTS, stride=steps)
            stride = dt_scr[rows, :]
            value = x_scr[rows, :]
            driven = stride * value
            grad = grad_scr[rows, :]
            marked = stride + big[i, 0]
            new = []
            drive_sum, rate_sum = None, None
            for n in range(STATE):
                rate = rate_wide[n]
                adjoint = grad * out_wide[i, n] + tails[n]
                map_grad[1, i, n] += grad * kept[i + 1, n]
                map_grad[0, i, n] += adjoint * driven
                drive = adjoint * in_wide[i, n]
                tail = jnp.exp2(marked * rate) * adjoint
                touched = tail * kept[i, n]
                slope = touched * rate
                log_scr[n] += touched * stride
                drive_sum = drive if drive_sum is None else drive_sum + drive
                rate_sum = slope if rate_sum is None else rate_sum + slope
                new.append(tail)
            x_out[rows, :] = stride * drive_sum
            dt_out[rows, :] = value * drive_sum + LN2 * rate_sum
            return tuple(new)

        lax.fori_loop(0, steps, backward, tails, unroll=True)
        for n in range(STATE):
            log_grad[n : n + 1, lanes] = (
                jnp.sum(log_scr[n], axis=0, keepdims=True) * rates[n : n + 1, lanes] * LN2
            )
        chance = jax.nn.sigmoid(step_pre[:, lanes] + step_bias[:, lanes])
        moved = dt_out[...] * masks[:, 0:1] * chance
        step_grad[:, lanes] = moved.astype(step_grad.dtype)
        bias_grad[:, lanes] = jnp.sum(moved, axis=0, keepdims=True)
        x_grad[:, lanes] = x_out[...] + skip[:, lanes] * grad_scr[...]
        skip_grad[:, lanes] = jnp.sum(grad_scr[...] * x_scr[...], axis=0, keepdims=True)

    each_tile(work)


def tile(rows):
    return pl.BlockSpec((rows, TILES * LANES), lambda j: (0, j))


def turned(rows):
    return pl.BlockSpec((TILES * LANES, rows), lambda j: (j, 0))


def whole(shape):
    return pl.BlockSpec(shape, lambda j: (0,) * len(shape))


def shape_of(rows, width, dtype=jnp.float32):
    return jax.ShapeDtypeStruct((rows, width), dtype)


PARAMS = pltpu.CompilerParams(
    dimension_semantics=("arbitrary",), vmem_limit_bytes=56 * 1024 * 1024
)
RATE = pltpu.VMEM((STATE, SEGMENTS, LANES), jnp.float32)
ENDS = pltpu.VMEM((SEGMENTS * STATE, LANES), jnp.float32)
SUMS = pltpu.VMEM((SEGMENTS, LANES), jnp.float32)


def call(kernel, waits, micros, **options):
    specs = options.pop("in_specs")

    def waiting(*refs):
        kernel(*refs[: len(specs)], *refs[len(specs) + len(waits) :])

    waiting.__name__ = options["name"]
    run = pl.pallas_call(
        waiting,
        in_specs=specs + [pl.BlockSpec(memory_space=pl.ANY)] * len(waits),
        compiler_params=PARAMS,
        cost_estimate=pl.CostEstimate(
            flops=0, bytes_accessed=micros * 3_000_000, transcendentals=0
        ),
        **options,
    )
    return lambda *operands: run(*operands, *waits)


def rows_of(rows):
    return pltpu.VMEM((rows, LANES), jnp.float32)


def scan_ends(x, dt, in_wide, big, rates, waits=()):
    rows, width = x.shape
    return call(
        ends_kernel,
        waits,
        15,
        grid=(width // (TILES * LANES),),
        in_specs=[tile(rows), tile(rows), whole(in_wide.shape), whole(big.shape), tile(STATE)],
        out_specs=[tile(SEGMENTS * STATE), tile(SEGMENTS), tile(STATE), tile(1)],
        out_shape=[shape_of(SEGMENTS * STATE, width), shape_of(SEGMENTS, width),
                   shape_of(STATE, width), shape_of(1, width)],
        scratch_shapes=[RATE, ENDS, SUMS, rows_of(rows), rows_of(rows)],
        name="scan_ends",
    )(x, dt, in_wide, big, rates)


def scan_outputs(x, dt, in_wide, out_wide, big, rates, ends_ex, cum_ex, entering, skip, gate, waits=()):
    rows, width = x.shape
    return call(
        outputs_kernel,
        waits,
        20,
        grid=(width // (TILES * LANES),),
        in_specs=[tile(rows), tile(rows), whole(in_wide.shape), whole(out_wide.shape),
                  whole(big.shape), tile(STATE), tile(SEGMENTS * STATE), tile(SEGMENTS),
                  tile(STATE), tile(1), tile(rows)],
        out_specs=[tile(rows), tile(rows), turned(rows)],
        out_shape=[shape_of(rows, width), shape_of(rows, width, jnp.bfloat16),
                   shape_of(width, rows, jnp.bfloat16)],
        scratch_shapes=[RATE, ENDS] + [rows_of(rows)] * 3,
        name="scan_outputs",
    )(x, dt, in_wide, out_wide, big, rates, ends_ex, cum_ex, entering, skip, gate)


def scan_adjoints(gated_grad, gate, scan_out, dt, out_wide, big, rates, waits=()):
    rows, width = dt.shape
    return call(
        adjoint_kernel,
        waits,
        17,
        grid=(width // (TILES * LANES),),
        in_specs=[tile(rows), tile(rows), tile(rows), tile(rows), whole(out_wide.shape),
                  whole(big.shape), tile(STATE)],
        out_specs=[tile(rows), tile(rows), turned(rows), tile(SEGMENTS * STATE), tile(SEGMENTS),
                   tile(STATE)],
        out_shape=[shape_of(rows, width), shape_of(rows, width, jnp.bfloat16),
                   shape_of(width, rows, jnp.bfloat16),
                   shape_of(SEGMENTS * STATE, width), shape_of(SEGMENTS, width),
                   shape_of(STATE, width)],
        scratch_shapes=[RATE, ENDS, SUMS, rows_of(rows), rows_of(rows)],
        name="scan_adjoints",
    )(gated_grad, gate, scan_out, dt, out_wide, big, rates)


def scan_grads(x, dt, in_wide, out_wide, big, rates, ends_ex, cum_ex, entering, skip,
               scan_grad, adj_ex, back_cum_ex, returning, step_pre, step_bias, masks, waits=()):
    rows, width = x.shape
    steps = rows // SEGMENTS
    wide_shape = (steps, STATE, SEGMENTS, LANES)
    return call(
        grads_kernel,
        waits,
        55,
        grid=(width // (TILES * LANES),),
        in_specs=[tile(rows), tile(rows), whole(in_wide.shape), whole(out_wide.shape),
                  whole(big.shape), tile(STATE), tile(SEGMENTS * STATE), tile(SEGMENTS),
                  tile(STATE), tile(1), tile(rows), tile(SEGMENTS * STATE), tile(SEGMENTS),
                  tile(STATE), tile(rows), tile(1), whole(masks.shape)],
        out_specs=[tile(rows), tile(rows), whole((2,) + wide_shape), tile(STATE), tile(1),
                   tile(1)],
        out_shape=[shape_of(rows, width), shape_of(rows, width, jnp.bfloat16),
                   jax.ShapeDtypeStruct((2,) + wide_shape, jnp.float32),
                   shape_of(STATE, width), shape_of(1, width), shape_of(1, width)],
        scratch_shapes=[RATE, pltpu.VMEM((steps + 1,) + wide_shape[1:], jnp.float32), RATE, ENDS]
        + [rows_of(rows)] * 5,
        name="scan_grads",
    )(x, dt, in_wide, out_wide, big, rates, ends_ex, cum_ex, entering, skip, scan_grad, adj_ex,
      back_cum_ex, returning, step_pre, step_bias, masks)


def fold_maps(wide):
    summed = jnp.sum(wide, axis=4)
    return jnp.transpose(summed, (3, 1, 0, 2)).reshape(-1, 2 * STATE)


def conv_back_kernel(edge_start, scan_grad, small_grad, x_proj, x, halo, edge, valid, weight, bias,
                     x_grad, x_grad_t, weight_grad, bias_grad, x_ext, g_ext, valid_wide):
    rows = x.shape[0]
    taps = weight.shape[0]
    position = lax.broadcasted_iota(jnp.int32, (rows, LANES), 0)
    first = edge_start[0]

    @pl.when(pl.program_id(0) == 0)
    def _():
        for k in range(1, taps):
            valid_wide[k] = jnp.broadcast_to(valid[:, k : k + 1], (rows, LANES))
        g_ext[rows : rows + 8, :] = jnp.zeros((8, LANES), jnp.float32)

    def work(lanes):
        grad = scan_grad[:, lanes] + lax.dot_general(
            small_grad[...], x_proj[:, lanes], (((1,), (0,)), ((), ())),
            preferred_element_type=jnp.float32,
        )
        x_ext[0:8, :] = halo[:, lanes]
        x_ext[8 : 8 + rows, :] = x[:, lanes]
        pre = bias[:, lanes] + weight[taps - 1 : taps, lanes] * x[:, lanes]
        for k in range(1, taps):
            tap = weight[taps - 1 - k : taps - k, lanes]
            pre = pre + tap * x_ext[8 - k : 8 - k + rows, :] * valid_wide[k]
        chance = jax.nn.sigmoid(pre)
        grad = grad * (chance * (1.0 + pre * (1.0 - chance)))
        bias_grad[:, lanes] = jnp.sum(grad, axis=0, keepdims=True)
        weight_grad[taps - 1 : taps, lanes] = jnp.sum(grad * x[:, lanes], axis=0, keepdims=True)
        total = weight[taps - 1 : taps, lanes] * grad
        for k in range(1, taps):
            masked = grad * valid_wide[k]
            weight_grad[taps - 1 - k : taps - k, lanes] = jnp.sum(
                masked * x_ext[8 - k : 8 - k + rows, :], axis=0, keepdims=True
            )
            g_ext[0:rows, :] = masked
            total = total + weight[taps - 1 - k : taps - k, lanes] * g_ext[k : k + rows, :]
        for j in range(taps - 1):
            total = total + jnp.where(position == first + j, edge[j : j + 1, lanes], 0.0)
        x_grad[:, lanes] = total.astype(x_grad.dtype)
        x_grad_t[lanes, :] = total.T.astype(x_grad_t.dtype)

    each_tile(work)


def conv_back(edge_start, scan_grad, small_grad, x_proj, x, halo, edge, valid, weight, bias,
              waits=()):
    rows, width = scan_grad.shape
    taps = weight.shape[0]
    scratch = pltpu.VMEM((rows + 8, LANES), jnp.float32)
    return call(
        conv_back_kernel,
        waits,
        6,
        grid=(width // (TILES * LANES),),
        in_specs=[pl.BlockSpec(memory_space=pltpu.SMEM), tile(rows), whole(small_grad.shape),
                  tile(x_proj.shape[0]), tile(rows),
                  tile(8), tile(8), whole(valid.shape), tile(taps), tile(1)],
        out_specs=[tile(rows), turned(rows), tile(taps), tile(1)],
        out_shape=[shape_of(rows, width, jnp.bfloat16), shape_of(width, rows, jnp.bfloat16),
                   shape_of(taps, width), shape_of(1, width)],
        scratch_shapes=[scratch, scratch, pltpu.VMEM((taps, rows, LANES), jnp.float32)],
        name="conv_back",
    )(edge_start, scan_grad, small_grad, x_proj, x, halo, edge, valid, weight, bias)


def shares_kernel(place, *refs):
    out, pairs = refs[-1], len(refs) // 2
    members, wide = out.shape[0], out.shape[2]
    for p in range(pairs):
        left, right = refs[p], refs[pairs + p]
        blocks = left.shape[0]
        whole_left = jnp.concatenate([left[b] for b in range(blocks)], axis=1)
        whole_right = right[...].reshape(-1, right.shape[2])
        total = jnp.dot(whole_left, whole_right, preferred_element_type=jnp.float32)
        for h in range(members):
            after_this = lax.rem(h - place[0] + members, members)
            out[after_this, p] = total[h * wide : (h + 1) * wide].astype(out.dtype)


def block_shares(lefts, rights, place, members, waits=()):
    blocks, channels, tokens = lefts[0].shape
    width = rights[0].shape[2]
    columns = TILES * LANES
    out = (members, len(lefts), channels // members)
    return call(
        shares_kernel,
        waits,
        0,
        grid=(width // columns,),
        in_specs=[pl.BlockSpec(memory_space=pltpu.SMEM)]
        + [whole(lefts[0].shape)] * len(lefts)
        + [pl.BlockSpec((blocks, tokens, columns), lambda j: (0, 0, j))] * len(lefts),
        out_specs=pl.BlockSpec(out + (columns,), lambda j: (0, 0, 0, j)),
        out_shape=jax.ShapeDtypeStruct(out + (width,), jnp.bfloat16),
        scratch_shapes=[],
        name="block_shares",
    )(place, *lefts, *rights)


def pack_kernel(mixer, small, step, rank, *refs):
    out, rows = refs[-1], refs[:-1]
    first = (((0,), (0,)), ((), ()))
    out[:, :LANES] = lax.dot_general(
        mixer[...], small[...], first, preferred_element_type=jnp.float32
    ).astype(out.dtype)
    total = lax.dot_general(step[...], rank[...], first, preferred_element_type=jnp.float32)
    at = DT_RANK
    for row in rows:
        size = row.shape[0]
        line = lax.broadcasted_iota(jnp.int32, (size, LANES), 0)
        lane = lax.broadcasted_iota(jnp.int32, (size, LANES), 1)
        spot = (lane == line + at).astype(jnp.float32).astype(out.dtype)
        total = total + lax.dot_general(
            row[...].astype(out.dtype), spot, first, preferred_element_type=jnp.float32
        )
        at += size
    out[:, LANES:] = total.astype(out.dtype)


def channel_pack(mixer, small, step, rank, rows, waits=()):
    length, width = mixer.shape
    return call(
        pack_kernel,
        waits,
        3,
        grid=(width // (TILES * LANES),),
        in_specs=[tile(length), whole(small.shape), tile(length), whole(rank.shape)]
        + [tile(row.shape[0]) for row in rows],
        out_specs=pl.BlockSpec((TILES * LANES, 2 * LANES), lambda j: (j, 0)),
        out_shape=shape_of(width, 2 * LANES, jnp.bfloat16),
        scratch_shapes=[],
        name="channel_pack",
    )(mixer, small, step, rank, *rows)


norm_epsilon = 1e-05
highest = lax.Precision.HIGHEST
ROWS_FIRST = (((0,), (0,)), ((), ()))
LAST_DIMS = (((1,), (1,)), ((), ()))


def shifted_2(block, axis, distance):
    devices = range(lax.axis_size(axis))
    route = [(i - distance, i) for i in devices if i - distance in devices]
    return lax.ppermute(block, axis, route)


def crossed(block, axis, mask):
    return lax.ppermute(block, axis, [(i, i ^ mask) for i in range(lax.axis_size(axis))])


def exchanged(blocks, axis):
    return [block if k == 0 else crossed(block, axis, k) for k, block in enumerate(blocks)]


def after(value, *others):
    return lax.optimization_barrier((value,) + others)[0]


def summed_ahead(parts, axis, *others):
    count = lax.axis_size(axis)
    total = parts[0].astype(jnp.float32)
    for k in range(1, count):
        route = [(i, (i + k) % count) for i in range(count)]
        total = total + after(lax.ppermute(parts[k], axis, route), *others).astype(jnp.float32)
    return total


def summed_shares(parts, axis):
    count, mine = lax.axis_size(axis), lax.axis_index(axis)
    return summed_ahead(
        [
            lax.dynamic_index_in_dim(parts, lax.rem(mine + k, count), 0, False)
            for k in range(count)
        ],
        axis,
    )


def around(value, axis):
    count = lax.axis_size(axis)
    return [value] + [
        lax.ppermute(value, axis, [(i, (i + k) % count) for i in range(count)])
        for k in range(1, count)
    ]


def state_before(cum, end, rates, axis):
    count, mine = lax.axis_size(axis), lax.axis_index(axis)
    first = lax.reduce_precision(cum, 8, 7)
    second = lax.reduce_precision(cum - first, 8, 7)
    sent = jnp.concatenate([end, first, second, cum - first - second], axis=0)
    got = [part.astype(jnp.float32) for part in around(sent.astype(jnp.bfloat16), axis)]
    cums = [jnp.sum(part[end.shape[0] :], axis=0, keepdims=True) for part in got]
    state = jnp.zeros_like(end)
    for k in reversed(range(1, count)):
        longer = jnp.exp2(cums[k] * rates) * state + got[k][: end.shape[0]]
        state = jnp.where(k <= mine, longer, state)
    return state, cums


def state_after(cums, tail, rates, axis):
    count, mine = lax.axis_size(axis), lax.axis_index(axis)
    got = [part.astype(jnp.float32) for part in around(tail.astype(jnp.bfloat16), axis)]
    state = jnp.zeros_like(tail)
    for k in range(1, count):
        longer = jnp.exp2(cums[k] * rates) * state + got[k]
        state = jnp.where(mine + count - k < count, longer, state)
    return state


def rms_scale(values):
    return lax.rsqrt(jnp.mean(values * values, axis=1, keepdims=True) + norm_epsilon)


def scaled_norm(values, gain_row):
    return values * rms_scale(values) * gain_row[None, :]


def gelu_tanh(values):
    return jax.nn.gelu(values, approximate=True)


def conv_mix(x_inner, halo_rows, start_flags, conv_w, conv_b):
    tap_count = conv_w.shape[0]
    length = x_inner.shape[0]
    extended = jnp.concatenate([halo_rows, x_inner], axis=0)
    flag_line = jnp.concatenate([jnp.zeros((tap_count - 1,), jnp.float32), start_flags], axis=0)
    result = conv_b[None, :] + conv_w[tap_count - 1][None, :] * x_inner
    survive = jnp.ones((length,), jnp.float32)
    for offset in range(1, tap_count):
        survive = survive * (1.0 - flag_line[tap_count - offset : tap_count - offset + length])
        shifted = extended[tap_count - 1 - offset : tap_count - 1 - offset + length]
        result = result + conv_w[tap_count - 1 - offset][None, :] * shifted * survive[:, None]
    return jax.nn.silu(result)


def delta_apply(step_pre, bias_row, real_rows):
    return jax.nn.softplus(step_pre + bias_row[None, :]) * real_rows[:, None]


def mm(left, right):
    return jnp.dot(left, right, preferred_element_type=jnp.float32)


def mm_t(left, right):
    return lax.dot_general(left, right, LAST_DIMS, preferred_element_type=jnp.float32)


def t_mm(left, right):
    return lax.dot_general(left, right, ROWS_FIRST, preferred_element_type=jnp.float32)


def body(
    tokens,
    starts,
    counts,
    routes,
    slot_index,
    gain_mix,
    in_proj,
    conv_weight,
    conv_bias,
    x_proj,
    dt_proj,
    dt_bias,
    a_log,
    skip_gain,
    out_proj,
    gain_ffn,
    router,
    up_proj,
    down_proj,
    out_grad,
):
    float_type = jnp.float32
    low_type = jnp.bfloat16
    length = tokens.shape[0]
    model_width = tokens.shape[1]
    inner_width = conv_bias.shape[0]
    experts = router.shape[1]
    capacity = 5 * length // (4 * experts)
    groups, members = lax.axis_size("ep"), lax.axis_size("hs")
    group, member = lax.axis_index("ep"), lax.axis_index("hs")
    half = groups // 2
    upper = group >= half

    def blocks_home(values):
        return lax.all_to_all(values, "ep", split_axis=0, concat_axis=0, tiled=True)

    def by_owner(values):
        wide = inner_width // (half * members * 2)
        shaped = values.reshape(half, members, 2, wide, length)
        return jnp.transpose(shaped, (2, 0, 1, 3, 4)).reshape(groups, -1, length)

    up_own, down_own = up_proj[0], down_proj[0]
    shares = members // 2
    ones = [2 * k + k.bit_count() % 2 for k in range(shares)]
    alike = []
    for g in range(groups):
        if g % 2 == 0:
            halves = [range(shares), range(shares, members)]
        else:
            halves = [ones, [mask ^ 1 for mask in ones]]
        alike += [[g * members + h for h in chosen_half] for chosen_half in halves]
    odd_group = lax.rem(group, 2)
    place = jnp.where(odd_group == 0, lax.rem(member, shares), member // 2)

    def to_other_half(block):
        masks = [shares, 1]
        route = [
            (g * members + h, g * members + (h ^ masks[g % 2]))
            for g in range(groups)
            for h in range(members)
        ]
        return lax.ppermute(block, ("ep", "hs"), route)

    def from_half(block):
        return lax.all_gather(block, ("ep", "hs"), axis_index_groups=alike)


    edge_start = counts[0] - (CONV - 1)
    start_flags = starts.astype(float_type)
    real_rows = (jnp.arange(length, dtype=jnp.int32) < counts[0]).astype(float_type)
    tokens_float = tokens.astype(float_type)
    normed_one, norm_one_back = jax.vjp(scaled_norm, tokens_float, gain_mix)
    normed_low = normed_one.astype(low_type)
    normed_all = lax.all_gather(normed_low, "ep")
    projected = mm(normed_low, in_proj)
    inner_x = projected[:, :inner_width]
    inner_gate = projected[:, inner_width:]
    edge_rows = lax.dynamic_slice_in_dim(inner_x, edge_start, CONV - 1, 0)
    edge_flags = lax.dynamic_slice_in_dim(start_flags, edge_start, CONV - 1, 0)
    later = [jnp.prod(1.0 - edge_flags[k + 1 :]) for k in range(CONV - 1)]
    edge_mask = jnp.stack(later)[:, None]
    halo_rows = shifted_2(edge_rows * edge_mask, "hs", 1)
    kept_taps = [jnp.ones((length,), float_type)]
    flag_line = jnp.concatenate([jnp.zeros((CONV - 1,), float_type), start_flags])
    for k in range(1, CONV):
        kept_taps.append(kept_taps[-1] * (1.0 - flag_line[CONV - k : CONV - k + length]))
    masks = jnp.stack([real_rows] + kept_taps[1:], axis=1)

    ups = from_half(after(up_own, halo_rows))

    mixer_in = conv_mix(inner_x, halo_rows, start_flags, conv_weight, conv_bias)
    mixer_low = mixer_in.astype(low_type)
    small_proj = mm(mixer_low, x_proj)
    rank_low = small_proj[:, :DT_RANK].astype(low_type)
    step_pre = mm(rank_low, dt_proj)
    input_map = small_proj[:, DT_RANK : DT_RANK + STATE]
    output_map = small_proj[:, DT_RANK + STATE :]

    step_size = delta_apply(step_pre, dt_bias, real_rows)
    in_wide, out_wide = widened(input_map), widened(output_map)
    reset_wide = widened(start_flags[:, None] * RESET)
    rates = -(jnp.exp(a_log) / LN2).T
    skip_row = skip_gain[None, :]
    ends_ex, cum_ex, end_all, cum_all = scan_ends(
        mixer_in, step_size, in_wide, reset_wide, rates
    )
    entering, cums = state_before(cum_all, end_all, rates, "hs")
    downs = from_half(after(down_own, entering))
    scan_out, gated_low, gated_t = scan_outputs(
        mixer_in,
        step_size,
        in_wide,
        out_wide,
        reset_wide,
        rates,
        ends_ex,
        cum_ex,
        entering,
        skip_row,
        inner_gate,

    )
    mixer_out = mm(gated_low, out_proj)
    middle = tokens_float + mixer_out * real_rows[:, None]
    normed_two, norm_two_back = jax.vjp(scaled_norm, middle, gain_ffn)
    router_probs = jax.nn.softmax(
        jnp.dot(normed_two, router, precision=highest, preferred_element_type=float_type), axis=1
    )
    chosen = (routes[:, None] == jnp.arange(experts, dtype=jnp.int32)[None, :]).astype(float_type)
    gate_value = jnp.sum(router_probs * chosen, axis=1)
    column = routes * capacity + slot_index
    placed = (
        (column[:, None] == jnp.arange(experts * capacity, dtype=jnp.int32)[None, :])
        & (slot_index[:, None] >= 0)
    ).astype(low_type)
    grad_out = out_grad.astype(float_type)
    token_grad = grad_out * gate_value[:, None]

    rows_low = t_mm(placed, normed_two.astype(low_type)).astype(low_type)
    rows_own = blocks_home(rows_low.reshape(experts, capacity, model_width)).reshape(
        -1, model_width
    )
    rows_pair = to_other_half(rows_own)
    grads_low = t_mm(placed, token_grad.astype(low_type)).astype(low_type)
    grads_own = blocks_home(grads_low.reshape(experts, capacity, model_width)).reshape(
        -1, model_width
    )
    grads_pair = to_other_half(after(grads_own, rows_pair))
    gated_blocks = blocks_home(after(gated_t, grads_own).reshape(groups, -1, length))
    rows = jnp.concatenate([rows_own, rows_pair], axis=0)

    def near_parts(gathered):
        return [
            lax.dynamic_index_in_dim(gathered, jnp.bitwise_xor(place, k), 0, False)
            for k in range(shares)
        ]

    up_all, down_all = near_parts(ups), near_parts(downs)
    pre_all = [mm(rows, up) for up in up_all]
    hidden_all, gelu_backs = zip(*[jax.vjp(gelu_tanh, pre) for pre in pre_all])
    hidden_all = [hidden.astype(low_type) for hidden in hidden_all]
    expert_part = sum(mm(hidden, down) for hidden, down in zip(hidden_all, down_all))
    count = rows_own.shape[0]

    def pair_sum(partial, *earlier):
        other = to_other_half(after(partial[count:].astype(low_type), *earlier))
        return (partial[:count] + other.astype(float_type)).astype(low_type), other

    back_rows, rows_other = pair_sum(expert_part, grads_pair)
    home_rows = blocks_home(back_rows.reshape(groups, -1, model_width))
    grads = jnp.concatenate([grads_own, after(grads_pair, expert_part)], axis=0)
    pre_grads = [
        back(mm_t(grads, down))[0].astype(low_type) for back, down in zip(gelu_backs, down_all)
    ]
    grad_part = sum(mm_t(pre_grad, up) for pre_grad, up in zip(pre_grads, up_all))
    rows, grads = after(rows, back_rows), after(grads, back_rows)
    up_parts = [t_mm(rows, pre_grad) for pre_grad in pre_grads]
    down_parts = [t_mm(hidden, grads) for hidden in hidden_all]
    up_sent = jnp.stack([part.astype(low_type) for part in up_parts[1:]])
    down_sent = jnp.stack([part.astype(low_type) for part in down_parts[1:]])
    grad_rows, _ = pair_sum(grad_part, rows_other)
    up_grad, down_grad = up_parts[0], down_parts[0]
    grad_rows, up_sent, down_sent, up_grad, down_grad = lax.optimization_barrier(
        (grad_rows, up_sent, down_sent, up_grad, down_grad)
    )
    up_sent = from_half(up_sent)
    home_grad = blocks_home(after(grad_rows, home_rows).reshape(groups, -1, model_width))

    expert_out = mm(placed, home_rows.reshape(experts * capacity, model_width))
    block_out = (middle + gate_value[:, None] * expert_out).astype(low_type)
    gate_grad = jnp.sum(grad_out * expert_out, axis=1)
    logit_grad = router_probs * gate_grad[:, None] * (chosen - gate_value[:, None])
    router_grad = lax.dot_general(
        normed_two, logit_grad, ROWS_FIRST, precision=highest, preferred_element_type=float_type
    )
    normed_two_grad = mm(
        placed, home_grad.reshape(experts * capacity, model_width)
    ) + lax.dot_general(
        logit_grad, router, LAST_DIMS, precision=highest, preferred_element_type=float_type
    )
    middle_norm_grad, gain_ffn_grad = norm_two_back(normed_two_grad)
    middle_grad = grad_out + middle_norm_grad
    mixer_grad = (middle_grad * real_rows[:, None]).astype(low_type)
    mixer_grad_all = lax.all_gather(mixer_grad, "ep")
    gated_grad = mm_t(mixer_grad, out_proj)
    scan_grad, gate_pre_low, gate_pre_t, adj_ex, back_cum_ex, adj_all = scan_adjoints(
        gated_grad,
        inner_gate,
        scan_out,
        step_size,
        out_wide,
        reset_wide,
        rates,

    )
    returning = state_after(cums, adj_all, rates, "hs")
    gate_blocks = blocks_home(after(by_owner(gate_pre_t), returning))
    down_sent = from_half(after(down_sent, returning))
    scan_in_grad, pre_step_low, wide_grads, log_grad, skip_grad, dt_bias_grad = scan_grads(
        mixer_in,
        step_size,
        in_wide,
        out_wide,
        reset_wide,
        rates,
        ends_ex,
        cum_ex,
        entering,
        skip_row,
        scan_grad,
        adj_ex,
        back_cum_ex,
        returning,
        step_pre,
        dt_bias[None, :],
        masks,
        waits=[gated_blocks],
    )
    pre_step_low = after(pre_step_low, gate_blocks)
    rank_grad = mm_t(pre_step_low, dt_proj)
    small_grad = jnp.concatenate([rank_grad, fold_maps(wide_grads)], axis=1).astype(low_type)
    head = CONV - 1
    head_grad = scan_in_grad[:head] + mm_t(small_grad[:head], x_proj)

    def conv_head(rows_part):
        return conv_mix(inner_x[:head], rows_part, start_flags[:head], conv_weight, conv_bias)

    halo_grad = jax.vjp(conv_head, halo_rows)[1](head_grad)[0]
    here = member[None]
    out_gate = block_shares(
        [gated_blocks, gate_blocks], [mixer_grad_all, normed_all], here, members
    )
    edge_grad = after(shifted_2(halo_grad, "hs", -1), out_gate) * edge_mask
    inner_low, inner_t, conv_weight_grad, conv_bias_grad = conv_back(
        edge_start[None],
        scan_in_grad,
        small_grad,
        x_proj.T,
        inner_x,
        jnp.pad(halo_rows, ((8 - head, 0), (0, 0))),
        jnp.pad(edge_grad, ((0, 8 - head), (0, 0))),
        masks,
        conv_weight,
        conv_bias[None, :],
        waits=[out_gate],
    )

    inner_sent = by_owner(inner_t)
    inner_blocks = blocks_home(inner_sent)
    small_rows = [
        log_grad,
        dt_bias_grad,
        skip_grad,
        after(router_grad, inner_sent).reshape(inner_width, -1).T,
        conv_weight_grad,
        conv_bias_grad,
    ]
    sizes = [row.shape[0] for row in small_rows]
    packed = channel_pack(
        mixer_low,
        jnp.pad(small_grad, ((0, 0), (0, LANES - small_grad.shape[1]))),
        pre_step_low,
        jnp.pad(rank_low, ((0, 0), (0, LANES - DT_RANK))),
        small_rows,
        waits=[inner_sent],
    )
    inner_part = block_shares(
        [inner_blocks], [normed_all], here, members, waits=[out_gate, packed]
    )
    packed = blocks_home(after(packed, inner_part).reshape(groups, -1, 2 * LANES))
    packed_part = jnp.sum(packed.astype(float_type), axis=0).astype(low_type)
    packed_sum = summed_shares(packed_part.reshape(members, -1, 2 * LANES), "hs")
    inner_low = after(inner_low, inner_part)
    normed_one_grad = mm_t(inner_low, in_proj[:, :inner_width]) + mm_t(
        after(gate_pre_low, inner_part), in_proj[:, inner_width:]
    )
    tokens_norm_grad, gain_mix_grad = norm_one_back(normed_one_grad)
    tokens_grad = middle_grad + tokens_norm_grad
    gains = jnp.concatenate([gain_mix_grad, gain_ffn_grad]).reshape(groups * members, -1)
    gains = lax.all_to_all(
        after(gains, packed), ("ep", "hs"), split_axis=0, concat_axis=0, tiled=True
    )
    gains_sum = jnp.sum(gains, axis=0)
    for k in range(1, shares):
        sender = jnp.bitwise_xor(place, k)
        up_other = lax.dynamic_index_in_dim(after(up_sent, inner_part), sender, 0, False)[k - 1]
        down_other = lax.dynamic_index_in_dim(after(down_sent, inner_part), sender, 0, False)[k - 1]
        up_grad = up_grad + up_other.astype(float_type)
        down_grad = down_grad + down_other.astype(float_type)

    inner_sum = summed_ahead(inner_part, "hs")[0]
    out_proj_sum, gate_sum = summed_ahead(out_gate, "hs", inner_sum)
    given = jnp.where(upper, inner_sum, gate_sum).astype(low_type)
    given = after(given, gains_sum, packed_sum)
    kept = jnp.where(upper, gate_sum, inner_sum)
    taken = crossed(given, "ep", half).astype(float_type)
    in_proj_sum = jnp.concatenate(
        [jnp.where(upper, taken, kept), jnp.where(upper, kept, taken)], axis=0
    ).T
    cut, at = [], LANES + DT_RANK
    for size in sizes:
        cut.append(packed_sum[:, at : at + size])
        at += size
    return (
        block_out,
        tokens_grad,
        gains_sum,
        cut[3].reshape(-1),
        in_proj_sum,
        cut[4].T,
        cut[5][:, 0],
        packed_sum[:, : DT_RANK + 2 * STATE],
        packed_sum[:, LANES : LANES + DT_RANK].T,
        cut[1][:, 0],
        cut[0],
        cut[2][:, 0],
        out_proj_sum,
        up_grad[None],
        down_grad[None],
    )


def solution(mesh):
    return jax.shard_map(
        body,
        mesh=mesh,
        in_specs=(
            P(("ep", "hs"), None),
            P(("ep", "hs")),
            P(("ep", "hs")),
            P(("ep", "hs")),
            P(("ep", "hs")),
            P(),
            P(),
            P(),
            P(),
            P(),
            P(),
            P(),
            P(),
            P(),
            P(),
            P(),
            P(),
            P("ep", None, "hs"),
            P("ep", "hs", None),
            P(("ep", "hs"), None),
        ),
        out_specs=(
            P(("ep", "hs"), None),
            P(("ep", "hs"), None),
            P(("ep", "hs")),
            P(("ep", "hs")),
            P(None, ("ep", "hs")),
            P(None, ("ep", "hs")),
            P(("ep", "hs")),
            P(("ep", "hs"), None),
            P(None, ("ep", "hs")),
            P(("ep", "hs")),
            P(("ep", "hs"), None),
            P(("ep", "hs")),
            P(("ep", "hs"), None),
            P("ep", None, "hs"),
            P("ep", "hs", None),
        ),
        check_vma=False,
    )
```

```python
import jax
import jax.numpy as jnp
from jax import lax
from jax.experimental import pallas as pl
from jax.experimental.pallas import tpu as pltpu
from jax.sharding import PartitionSpec as P

DT_RANK = 72
CONV = 4
STATE = 16
SEGMENTS = 8
LANES = 128
TILES = 3
RESET = 1e30
LN2 = 0.6931471805599453


def widened(values):
    shaped = values.reshape(SEGMENTS, -1, values.shape[1])
    shaped = jnp.transpose(shaped, (1, 2, 0))[..., None]
    return jnp.broadcast_to(shaped, shaped.shape[:3] + (LANES,))


def each_tile(work):
    @pl.loop(0, TILES)
    def _(k):
        work(pl.ds(pl.multiple_of(k * LANES, LANES), LANES))


def spread_rates(target, rates, lanes):
    for n in range(STATE):
        target[n] = jnp.broadcast_to(rates[n : n + 1, lanes], (SEGMENTS, LANES))


def ends_kernel(x, dt, in_wide, big, rates, ends_ex, cum_ex, end_all, cum_all,
                rate_wide, end_scr, sum_scr, x_scr, dt_scr):
    steps = x.shape[0] // SEGMENTS

    def work(lanes):
        spread_rates(rate_wide, rates, lanes)
        x_scr[...] = x[:, lanes]
        dt_scr[...] = dt[:, lanes]

        def step(i, carry):
            total, states = carry[0], carry[1:]
            rows = pl.ds(i, SEGMENTS, stride=steps)
            stride = dt_scr[rows, :]
            driven = stride * x_scr[rows, :]
            stride = stride + big[i, 0]
            new = [total + stride]
            for n in range(STATE):
                new.append(jnp.exp2(stride * rate_wide[n]) * states[n] + driven * in_wide[i, n])
            return tuple(new)

        zero = jnp.zeros((SEGMENTS, LANES), jnp.float32)
        done = lax.fori_loop(0, steps, step, (zero,) * (STATE + 1), unroll=True)
        sum_scr[...] = done[0]
        for n in range(STATE):
            end_scr[n * SEGMENTS : (n + 1) * SEGMENTS, :] = done[1 + n]
        state = jnp.zeros((STATE, LANES), jnp.float32)
        cum = jnp.zeros((1, LANES), jnp.float32)
        for s in range(SEGMENTS):
            ends_ex[s * STATE : (s + 1) * STATE, lanes] = state
            cum_ex[s : s + 1, lanes] = cum
            own = sum_scr[s : s + 1, :]
            state = (
                jnp.exp2(own * rates[:, lanes]) * state
                + end_scr[pl.ds(s, STATE, stride=SEGMENTS), :]
            )
            cum = cum + own
        end_all[:, lanes] = state
        cum_all[:, lanes] = cum

    each_tile(work)


def opening_states(cum, rate_wide, entering, ends_ex, end_scr, lanes):
    end_scr[...] = ends_ex[:, lanes]
    return tuple(
        jnp.exp2(cum * rate_wide[n]) * entering[n : n + 1, lanes]
        + end_scr[pl.ds(n, SEGMENTS, stride=STATE), :]
        for n in range(STATE)
    )


def outputs_kernel(x, dt, in_wide, out_wide, big, rates, ends_ex, cum_ex, entering, skip, gate,
                   scan_out, gated, gated_t, rate_wide, end_scr, x_scr, dt_scr, out_scr):
    steps = x.shape[0] // SEGMENTS

    def work(lanes):
        spread_rates(rate_wide, rates, lanes)
        x_scr[...] = x[:, lanes]
        dt_scr[...] = dt[:, lanes]
        opening = opening_states(cum_ex[:, lanes], rate_wide, entering, ends_ex, end_scr, lanes)

        def step(i, states):
            rows = pl.ds(i, SEGMENTS, stride=steps)
            stride = dt_scr[rows, :]
            driven = stride * x_scr[rows, :]
            stride = stride + big[i, 0]
            new, total = [], None
            for n in range(STATE):
                state = jnp.exp2(stride * rate_wide[n]) * states[n] + driven * in_wide[i, n]
                new.append(state)
                term = state * out_wide[i, n]
                total = term if total is None else total + term
            out_scr[rows, :] = total
            return tuple(new)

        lax.fori_loop(0, steps, step, opening, unroll=True)
        value = out_scr[...] + skip[:, lanes] * x_scr[...]
        scan_out[:, lanes] = value
        product = value * jax.nn.silu(gate[:, lanes])
        gated[:, lanes] = product.astype(gated.dtype)
        gated_t[lanes, :] = product.T.astype(gated.dtype)

    each_tile(work)


def adjoint_kernel(gated_grad, gate, scan_out, dt, out_wide, big, rates,
                   scan_grad, gate_grad, gate_grad_t, adj_ex, cum_ex, adj_all,
                   rate_wide, end_scr, sum_scr, grad_scr, dt_scr):
    steps = dt.shape[0] // SEGMENTS

    def work(lanes):
        spread_rates(rate_wide, rates, lanes)
        incoming = gated_grad[:, lanes]
        gate_in = gate[:, lanes]
        chance = jax.nn.sigmoid(gate_in)
        moved = incoming * (gate_in * chance)
        scan_grad[:, lanes] = moved
        grad_scr[...] = moved
        dt_scr[...] = dt[:, lanes]
        product = incoming * scan_out[:, lanes] * (chance * (1.0 + gate_in * (1.0 - chance)))
        gate_grad[:, lanes] = product.astype(gate_grad.dtype)
        gate_grad_t[lanes, :] = product.T.astype(gate_grad.dtype)

        def step(k, carry):
            i = steps - 1 - k
            total, tails = carry[0], carry[1:]
            rows = pl.ds(i, SEGMENTS, stride=steps)
            grad = grad_scr[rows, :]
            stride = dt_scr[rows, :] + big[i, 0]
            new = [total + stride]
            for n in range(STATE):
                new.append(jnp.exp2(stride * rate_wide[n]) * (grad * out_wide[i, n] + tails[n]))
            return tuple(new)

        zero = jnp.zeros((SEGMENTS, LANES), jnp.float32)
        done = lax.fori_loop(0, steps, step, (zero,) * (STATE + 1), unroll=True)
        sum_scr[...] = done[0]
        for n in range(STATE):
            end_scr[n * SEGMENTS : (n + 1) * SEGMENTS, :] = done[1 + n]
        tail = jnp.zeros((STATE, LANES), jnp.float32)
        cum = jnp.zeros((1, LANES), jnp.float32)
        for s in reversed(range(SEGMENTS)):
            adj_ex[s * STATE : (s + 1) * STATE, lanes] = tail
            cum_ex[s : s + 1, lanes] = cum
            own = sum_scr[s : s + 1, :]
            tail = (
                jnp.exp2(own * rates[:, lanes]) * tail
                + end_scr[pl.ds(s, STATE, stride=SEGMENTS), :]
            )
            cum = cum + own
        adj_all[:, lanes] = tail

    each_tile(work)


def grads_kernel(x, dt, in_wide, out_wide, big, rates, ends_ex, cum_ex, entering, skip,
                 scan_grad, adj_ex, back_cum_ex, returning, step_pre, step_bias, masks,
                 x_grad, step_grad, map_grad, log_grad, skip_grad, bias_grad,
                 rate_wide, kept, log_scr, end_scr, x_scr, dt_scr, grad_scr, x_out, dt_out):
    steps = x.shape[0] // SEGMENTS

    @pl.when(pl.program_id(0) == 0)
    def _():
        map_grad[...] = jnp.zeros_like(map_grad)

    def work(lanes):
        spread_rates(rate_wide, rates, lanes)
        x_scr[...] = x[:, lanes]
        dt_scr[...] = dt[:, lanes]
        grad_scr[...] = scan_grad[:, lanes]
        opening = opening_states(cum_ex[:, lanes], rate_wide, entering, ends_ex, end_scr, lanes)
        for n in range(STATE):
            kept[0, n] = opening[n]

        def forward(i, states):
            rows = pl.ds(i, SEGMENTS, stride=steps)
            stride = dt_scr[rows, :]
            driven = stride * x_scr[rows, :]
            stride = stride + big[i, 0]
            new = []
            for n in range(STATE):
                state = jnp.exp2(stride * rate_wide[n]) * states[n] + driven * in_wide[i, n]
                kept[i + 1, n] = state
                new.append(state)
            return tuple(new)

        lax.fori_loop(0, steps, forward, opening, unroll=True)
        tails = opening_states(back_cum_ex[:, lanes], rate_wide, returning, adj_ex, end_scr, lanes)
        zero = jnp.zeros((SEGMENTS, LANES), jnp.float32)
        for n in range(STATE):
            log_scr[n] = zero

        def backward(k, tails):
            i = steps - 1 - k
            rows = pl.ds(i, SEGMENTS, stride=steps)
            stride = dt_scr[rows, :]
            value = x_scr[rows, :]
            driven = stride * value
            grad = grad_scr[rows, :]
            marked = stride + big[i, 0]
            new = []
            drive_sum, rate_sum = None, None
            for n in range(STATE):
                rate = rate_wide[n]
                adjoint = grad * out_wide[i, n] + tails[n]
                map_grad[1, i, n] += grad * kept[i + 1, n]
                map_grad[0, i, n] += adjoint * driven
                drive = adjoint * in_wide[i, n]
                tail = jnp.exp2(marked * rate) * adjoint
                touched = tail * kept[i, n]
                slope = touched * rate
                log_scr[n] += touched * stride
                drive_sum = drive if drive_sum is None else drive_sum + drive
                rate_sum = slope if rate_sum is None else rate_sum + slope
                new.append(tail)
            x_out[rows, :] = stride * drive_sum
            dt_out[rows, :] = value * drive_sum + LN2 * rate_sum
            return tuple(new)

        lax.fori_loop(0, steps, backward, tails, unroll=True)
        for n in range(STATE):
            log_grad[n : n + 1, lanes] = (
                jnp.sum(log_scr[n], axis=0, keepdims=True) * rates[n : n + 1, lanes] * LN2
            )
        chance = jax.nn.sigmoid(step_pre[:, lanes] + step_bias[:, lanes])
        moved = dt_out[...] * masks[:, 0:1] * chance
        step_grad[:, lanes] = moved.astype(step_grad.dtype)
        bias_grad[:, lanes] = jnp.sum(moved, axis=0, keepdims=True)
        x_grad[:, lanes] = x_out[...] + skip[:, lanes] * grad_scr[...]
        skip_grad[:, lanes] = jnp.sum(grad_scr[...] * x_scr[...], axis=0, keepdims=True)

    each_tile(work)


def tile(rows):
    return pl.BlockSpec((rows, TILES * LANES), lambda j: (0, j))


def turned(rows):
    return pl.BlockSpec((TILES * LANES, rows), lambda j: (j, 0))


def whole(shape):
    return pl.BlockSpec(shape, lambda j: (0,) * len(shape))


def shape_of(rows, width, dtype=jnp.float32):
    return jax.ShapeDtypeStruct((rows, width), dtype)


PARAMS = pltpu.CompilerParams(
    dimension_semantics=("arbitrary",), vmem_limit_bytes=56 * 1024 * 1024
)
RATE = pltpu.VMEM((STATE, SEGMENTS, LANES), jnp.float32)
ENDS = pltpu.VMEM((SEGMENTS * STATE, LANES), jnp.float32)
SUMS = pltpu.VMEM((SEGMENTS, LANES), jnp.float32)


def call(kernel, waits, micros, **options):
    specs = options.pop("in_specs")

    def waiting(*refs):
        kernel(*refs[: len(specs)], *refs[len(specs) + len(waits) :])

    waiting.__name__ = options["name"]
    run = pl.pallas_call(
        waiting,
        in_specs=specs + [pl.BlockSpec(memory_space=pl.ANY)] * len(waits),
        compiler_params=PARAMS,
        cost_estimate=pl.CostEstimate(
            flops=0, bytes_accessed=micros * 3_000_000, transcendentals=0
        ),
        **options,
    )
    return lambda *operands: run(*operands, *waits)


def rows_of(rows):
    return pltpu.VMEM((rows, LANES), jnp.float32)


def scan_ends(x, dt, in_wide, big, rates, waits=()):
    rows, width = x.shape
    return call(
        ends_kernel,
        waits,
        15,
        grid=(width // (TILES * LANES),),
        in_specs=[tile(rows), tile(rows), whole(in_wide.shape), whole(big.shape), tile(STATE)],
        out_specs=[tile(SEGMENTS * STATE), tile(SEGMENTS), tile(STATE), tile(1)],
        out_shape=[shape_of(SEGMENTS * STATE, width), shape_of(SEGMENTS, width),
                   shape_of(STATE, width), shape_of(1, width)],
        scratch_shapes=[RATE, ENDS, SUMS, rows_of(rows), rows_of(rows)],
        name="scan_ends",
    )(x, dt, in_wide, big, rates)


def scan_outputs(x, dt, in_wide, out_wide, big, rates, ends_ex, cum_ex, entering, skip, gate, waits=()):
    rows, width = x.shape
    return call(
        outputs_kernel,
        waits,
        20,
        grid=(width // (TILES * LANES),),
        in_specs=[tile(rows), tile(rows), whole(in_wide.shape), whole(out_wide.shape),
                  whole(big.shape), tile(STATE), tile(SEGMENTS * STATE), tile(SEGMENTS),
                  tile(STATE), tile(1), tile(rows)],
        out_specs=[tile(rows), tile(rows), turned(rows)],
        out_shape=[shape_of(rows, width), shape_of(rows, width, jnp.bfloat16),
                   shape_of(width, rows, jnp.bfloat16)],
        scratch_shapes=[RATE, ENDS] + [rows_of(rows)] * 3,
        name="scan_outputs",
    )(x, dt, in_wide, out_wide, big, rates, ends_ex, cum_ex, entering, skip, gate)


def scan_adjoints(gated_grad, gate, scan_out, dt, out_wide, big, rates, waits=()):
    rows, width = dt.shape
    return call(
        adjoint_kernel,
        waits,
        17,
        grid=(width // (TILES * LANES),),
        in_specs=[tile(rows), tile(rows), tile(rows), tile(rows), whole(out_wide.shape),
                  whole(big.shape), tile(STATE)],
        out_specs=[tile(rows), tile(rows), turned(rows), tile(SEGMENTS * STATE), tile(SEGMENTS),
                   tile(STATE)],
        out_shape=[shape_of(rows, width), shape_of(rows, width, jnp.bfloat16),
                   shape_of(width, rows, jnp.bfloat16),
                   shape_of(SEGMENTS * STATE, width), shape_of(SEGMENTS, width),
                   shape_of(STATE, width)],
        scratch_shapes=[RATE, ENDS, SUMS, rows_of(rows), rows_of(rows)],
        name="scan_adjoints",
    )(gated_grad, gate, scan_out, dt, out_wide, big, rates)


def scan_grads(x, dt, in_wide, out_wide, big, rates, ends_ex, cum_ex, entering, skip,
               scan_grad, adj_ex, back_cum_ex, returning, step_pre, step_bias, masks, waits=()):
    rows, width = x.shape
    steps = rows // SEGMENTS
    wide_shape = (steps, STATE, SEGMENTS, LANES)
    return call(
        grads_kernel,
        waits,
        55,
        grid=(width // (TILES * LANES),),
        in_specs=[tile(rows), tile(rows), whole(in_wide.shape), whole(out_wide.shape),
                  whole(big.shape), tile(STATE), tile(SEGMENTS * STATE), tile(SEGMENTS),
                  tile(STATE), tile(1), tile(rows), tile(SEGMENTS * STATE), tile(SEGMENTS),
                  tile(STATE), tile(rows), tile(1), whole(masks.shape)],
        out_specs=[tile(rows), tile(rows), whole((2,) + wide_shape), tile(STATE), tile(1),
                   tile(1)],
        out_shape=[shape_of(rows, width), shape_of(rows, width, jnp.bfloat16),
                   jax.ShapeDtypeStruct((2,) + wide_shape, jnp.float32),
                   shape_of(STATE, width), shape_of(1, width), shape_of(1, width)],
        scratch_shapes=[RATE, pltpu.VMEM((steps + 1,) + wide_shape[1:], jnp.float32), RATE, ENDS]
        + [rows_of(rows)] * 5,
        name="scan_grads",
    )(x, dt, in_wide, out_wide, big, rates, ends_ex, cum_ex, entering, skip, scan_grad, adj_ex,
      back_cum_ex, returning, step_pre, step_bias, masks)


def fold_maps(wide):
    summed = jnp.sum(wide, axis=4)
    return jnp.transpose(summed, (3, 1, 0, 2)).reshape(-1, 2 * STATE)


def conv_back_kernel(edge_start, scan_grad, small_grad, x_proj, x, halo, edge, valid, weight, bias,
                     x_grad, x_grad_t, weight_grad, bias_grad, x_ext, g_ext, valid_wide):
    rows = x.shape[0]
    taps = weight.shape[0]
    position = lax.broadcasted_iota(jnp.int32, (rows, LANES), 0)
    first = edge_start[0]

    @pl.when(pl.program_id(0) == 0)
    def _():
        for k in range(1, taps):
            valid_wide[k] = jnp.broadcast_to(valid[:, k : k + 1], (rows, LANES))
        g_ext[rows : rows + 8, :] = jnp.zeros((8, LANES), jnp.float32)

    def work(lanes):
        grad = scan_grad[:, lanes] + lax.dot_general(
            small_grad[...], x_proj[:, lanes], (((1,), (0,)), ((), ())),
            preferred_element_type=jnp.float32,
        )
        x_ext[0:8, :] = halo[:, lanes]
        x_ext[8 : 8 + rows, :] = x[:, lanes]
        pre = bias[:, lanes] + weight[taps - 1 : taps, lanes] * x[:, lanes]
        for k in range(1, taps):
            tap = weight[taps - 1 - k : taps - k, lanes]
            pre = pre + tap * x_ext[8 - k : 8 - k + rows, :] * valid_wide[k]
        chance = jax.nn.sigmoid(pre)
        grad = grad * (chance * (1.0 + pre * (1.0 - chance)))
        bias_grad[:, lanes] = jnp.sum(grad, axis=0, keepdims=True)
        weight_grad[taps - 1 : taps, lanes] = jnp.sum(grad * x[:, lanes], axis=0, keepdims=True)
        total = weight[taps - 1 : taps, lanes] * grad
        for k in range(1, taps):
            masked = grad * valid_wide[k]
            weight_grad[taps - 1 - k : taps - k, lanes] = jnp.sum(
                masked * x_ext[8 - k : 8 - k + rows, :], axis=0, keepdims=True
            )
            g_ext[0:rows, :] = masked
            total = total + weight[taps - 1 - k : taps - k, lanes] * g_ext[k : k + rows, :]
        for j in range(taps - 1):
            total = total + jnp.where(position == first + j, edge[j : j + 1, lanes], 0.0)
        x_grad[:, lanes] = total.astype(x_grad.dtype)
        x_grad_t[lanes, :] = total.T.astype(x_grad_t.dtype)

    each_tile(work)


def conv_back(edge_start, scan_grad, small_grad, x_proj, x, halo, edge, valid, weight, bias,
              waits=()):
    rows, width = scan_grad.shape
    taps = weight.shape[0]
    scratch = pltpu.VMEM((rows + 8, LANES), jnp.float32)
    return call(
        conv_back_kernel,
        waits,
        6,
        grid=(width // (TILES * LANES),),
        in_specs=[pl.BlockSpec(memory_space=pltpu.SMEM), tile(rows), whole(small_grad.shape),
                  tile(x_proj.shape[0]), tile(rows),
                  tile(8), tile(8), whole(valid.shape), tile(taps), tile(1)],
        out_specs=[tile(rows), turned(rows), tile(taps), tile(1)],
        out_shape=[shape_of(rows, width, jnp.bfloat16), shape_of(width, rows, jnp.bfloat16),
                   shape_of(taps, width), shape_of(1, width)],
        scratch_shapes=[scratch, scratch, pltpu.VMEM((taps, rows, LANES), jnp.float32)],
        name="conv_back",
    )(edge_start, scan_grad, small_grad, x_proj, x, halo, edge, valid, weight, bias)


def shares_kernel(place, *refs):
    out, pairs = refs[-1], len(refs) // 2
    members, wide = out.shape[0], out.shape[2]
    for p in range(pairs):
        left, right = refs[p], refs[pairs + p]
        blocks = left.shape[0]
        whole_left = jnp.concatenate([left[b] for b in range(blocks)], axis=1)
        whole_right = right[...].reshape(-1, right.shape[2])
        total = jnp.dot(whole_left, whole_right, preferred_element_type=jnp.float32)
        for h in range(members):
            after_this = lax.rem(h - place[0] + members, members)
            out[after_this, p] = total[h * wide : (h + 1) * wide].astype(out.dtype)


def block_shares(lefts, rights, place, members, waits=()):
    blocks, channels, tokens = lefts[0].shape
    width = rights[0].shape[2]
    columns = TILES * LANES
    out = (members, len(lefts), channels // members)
    return call(
        shares_kernel,
        waits,
        0,
        grid=(width // columns,),
        in_specs=[pl.BlockSpec(memory_space=pltpu.SMEM)]
        + [whole(lefts[0].shape)] * len(lefts)
        + [pl.BlockSpec((blocks, tokens, columns), lambda j: (0, 0, j))] * len(lefts),
        out_specs=pl.BlockSpec(out + (columns,), lambda j: (0, 0, 0, j)),
        out_shape=jax.ShapeDtypeStruct(out + (width,), jnp.bfloat16),
        scratch_shapes=[],
        name="block_shares",
    )(place, *lefts, *rights)


def pack_kernel(mixer, small, step, rank, *refs):
    out, rows = refs[-1], refs[:-1]
    first = (((0,), (0,)), ((), ()))
    out[:, :LANES] = lax.dot_general(
        mixer[...], small[...], first, preferred_element_type=jnp.float32
    ).astype(out.dtype)
    total = lax.dot_general(step[...], rank[...], first, preferred_element_type=jnp.float32)
    at = DT_RANK
    for row in rows:
        size = row.shape[0]
        line = lax.broadcasted_iota(jnp.int32, (size, LANES), 0)
        lane = lax.broadcasted_iota(jnp.int32, (size, LANES), 1)
        spot = (lane == line + at).astype(jnp.float32).astype(out.dtype)
        total = total + lax.dot_general(
            row[...].astype(out.dtype), spot, first, preferred_element_type=jnp.float32
        )
        at += size
    out[:, LANES:] = total.astype(out.dtype)


def channel_pack(mixer, small, step, rank, rows, waits=()):
    length, width = mixer.shape
    return call(
        pack_kernel,
        waits,
        3,
        grid=(width // (TILES * LANES),),
        in_specs=[tile(length), whole(small.shape), tile(length), whole(rank.shape)]
        + [tile(row.shape[0]) for row in rows],
        out_specs=pl.BlockSpec((TILES * LANES, 2 * LANES), lambda j: (j, 0)),
        out_shape=shape_of(width, 2 * LANES, jnp.bfloat16),
        scratch_shapes=[],
        name="channel_pack",
    )(mixer, small, step, rank, *rows)


norm_epsilon = 1e-05
highest = lax.Precision.HIGHEST
ROWS_FIRST = (((0,), (0,)), ((), ()))
LAST_DIMS = (((1,), (1,)), ((), ()))


def shifted_2(block, axis, distance):
    devices = range(lax.axis_size(axis))
    route = [(i - distance, i) for i in devices if i - distance in devices]
    return lax.ppermute(block, axis, route)


def crossed(block, axis, mask):
    return lax.ppermute(block, axis, [(i, i ^ mask) for i in range(lax.axis_size(axis))])


def exchanged(blocks, axis):
    return [block if k == 0 else crossed(block, axis, k) for k, block in enumerate(blocks)]


def after(value, *others):
    return lax.optimization_barrier((value,) + others)[0]


def summed_ahead(parts, axis, *others):
    count = lax.axis_size(axis)
    total = parts[0].astype(jnp.float32)
    for k in range(1, count):
        route = [(i, (i + k) % count) for i in range(count)]
        total = total + after(lax.ppermute(parts[k], axis, route), *others).astype(jnp.float32)
    return total


def summed_shares(parts, axis):
    count, mine = lax.axis_size(axis), lax.axis_index(axis)
    return summed_ahead(
        [
            lax.dynamic_index_in_dim(parts, lax.rem(mine + k, count), 0, False)
            for k in range(count)
        ],
        axis,
    )


def around(value, axis):
    count = lax.axis_size(axis)
    return [value] + [
        lax.ppermute(value, axis, [(i, (i + k) % count) for i in range(count)])
        for k in range(1, count)
    ]


def state_before(cum, end, rates, axis):
    count, mine = lax.axis_size(axis), lax.axis_index(axis)
    first = lax.reduce_precision(cum, 8, 7)
    second = lax.reduce_precision(cum - first, 8, 7)
    sent = jnp.concatenate([end, first, second, cum - first - second], axis=0)
    got = [part.astype(jnp.float32) for part in around(sent.astype(jnp.bfloat16), axis)]
    cums = [jnp.sum(part[end.shape[0] :], axis=0, keepdims=True) for part in got]
    state = jnp.zeros_like(end)
    for k in reversed(range(1, count)):
        longer = jnp.exp2(cums[k] * rates) * state + got[k][: end.shape[0]]
        state = jnp.where(k <= mine, longer, state)
    return state, cums


def state_after(cums, tail, rates, axis):
    count, mine = lax.axis_size(axis), lax.axis_index(axis)
    got = [part.astype(jnp.float32) for part in around(tail.astype(jnp.bfloat16), axis)]
    state = jnp.zeros_like(tail)
    for k in range(1, count):
        longer = jnp.exp2(cums[k] * rates) * state + got[k]
        state = jnp.where(mine + count - k < count, longer, state)
    return state


def rms_scale(values):
    return lax.rsqrt(jnp.mean(values * values, axis=1, keepdims=True) + norm_epsilon)


def scaled_norm(values, gain_row):
    return values * rms_scale(values) * gain_row[None, :]


def gelu_tanh(values):
    return jax.nn.gelu(values, approximate=True)


def conv_mix(x_inner, halo_rows, start_flags, conv_w, conv_b):
    tap_count = conv_w.shape[0]
    length = x_inner.shape[0]
    extended = jnp.concatenate([halo_rows, x_inner], axis=0)
    flag_line = jnp.concatenate([jnp.zeros((tap_count - 1,), jnp.float32), start_flags], axis=0)
    result = conv_b[None, :] + conv_w[tap_count - 1][None, :] * x_inner
    survive = jnp.ones((length,), jnp.float32)
    for offset in range(1, tap_count):
        survive = survive * (1.0 - flag_line[tap_count - offset : tap_count - offset + length])
        shifted = extended[tap_count - 1 - offset : tap_count - 1 - offset + length]
        result = result + conv_w[tap_count - 1 - offset][None, :] * shifted * survive[:, None]
    return jax.nn.silu(result)


def delta_apply(step_pre, bias_row, real_rows):
    return jax.nn.softplus(step_pre + bias_row[None, :]) * real_rows[:, None]


def mm(left, right):
    return jnp.dot(left, right, preferred_element_type=jnp.float32)


def mm_t(left, right):
    return lax.dot_general(left, right, LAST_DIMS, preferred_element_type=jnp.float32)


def t_mm(left, right):
    return lax.dot_general(left, right, ROWS_FIRST, preferred_element_type=jnp.float32)


def body(
    tokens,
    starts,
    counts,
    routes,
    slot_index,
    gain_mix,
    in_proj,
    conv_weight,
    conv_bias,
    x_proj,
    dt_proj,
    dt_bias,
    a_log,
    skip_gain,
    out_proj,
    gain_ffn,
    router,
    up_proj,
    down_proj,
    out_grad,
):
    float_type = jnp.float32
    low_type = jnp.bfloat16
    length = tokens.shape[0]
    model_width = tokens.shape[1]
    inner_width = conv_bias.shape[0]
    experts = router.shape[1]
    capacity = 5 * length // (4 * experts)
    groups, members = lax.axis_size("ep"), lax.axis_size("hs")
    group, member = lax.axis_index("ep"), lax.axis_index("hs")
    half = groups // 2
    upper = group >= half

    def blocks_home(values):
        return lax.all_to_all(values, "ep", split_axis=0, concat_axis=0, tiled=True)

    def by_owner(values):
        wide = inner_width // (half * members * 2)
        shaped = values.reshape(half, members, 2, wide, length)
        return jnp.transpose(shaped, (2, 0, 1, 3, 4)).reshape(groups, -1, length)

    up_own, down_own = up_proj[0], down_proj[0]
    shares = members // 2
    ones = [2 * k + k.bit_count() % 2 for k in range(shares)]
    alike = []
    for g in range(groups):
        if g % 2 == 0:
            halves = [range(shares), range(shares, members)]
        else:
            halves = [ones, [mask ^ 1 for mask in ones]]
        alike += [[g * members + h for h in chosen_half] for chosen_half in halves]
    odd_group = lax.rem(group, 2)
    place = jnp.where(odd_group == 0, lax.rem(member, shares), member // 2)

    def to_other_half(block):
        masks = [shares, 1]
        route = [
            (g * members + h, g * members + (h ^ masks[g % 2]))
            for g in range(groups)
            for h in range(members)
        ]
        return lax.ppermute(block, ("ep", "hs"), route)

    def from_half(block):
        return lax.all_gather(block, ("ep", "hs"), axis_index_groups=alike)


    edge_start = counts[0] - (CONV - 1)
    start_flags = starts.astype(float_type)
    real_rows = (jnp.arange(length, dtype=jnp.int32) < counts[0]).astype(float_type)
    tokens_float = tokens.astype(float_type)
    normed_one, norm_one_back = jax.vjp(scaled_norm, tokens_float, gain_mix)
    normed_low = normed_one.astype(low_type)
    normed_all = lax.all_gather(normed_low, "ep")
    projected = mm(normed_low, in_proj)
    inner_x = projected[:, :inner_width]
    inner_gate = projected[:, inner_width:]
    edge_rows = lax.dynamic_slice_in_dim(inner_x, edge_start, CONV - 1, 0)
    edge_flags = lax.dynamic_slice_in_dim(start_flags, edge_start, CONV - 1, 0)
    later = [jnp.prod(1.0 - edge_flags[k + 1 :]) for k in range(CONV - 1)]
    edge_mask = jnp.stack(later)[:, None]
    halo_rows = shifted_2(edge_rows * edge_mask, "hs", 1)
    kept_taps = [jnp.ones((length,), float_type)]
    flag_line = jnp.concatenate([jnp.zeros((CONV - 1,), float_type), start_flags])
    for k in range(1, CONV):
        kept_taps.append(kept_taps[-1] * (1.0 - flag_line[CONV - k : CONV - k + length]))
    masks = jnp.stack([real_rows] + kept_taps[1:], axis=1)

    ups = from_half(after(up_own, halo_rows))

    mixer_in = conv_mix(inner_x, halo_rows, start_flags, conv_weight, conv_bias)
    mixer_low = mixer_in.astype(low_type)
    small_proj = mm(mixer_low, x_proj)
    rank_low = small_proj[:, :DT_RANK].astype(low_type)
    step_pre = mm(rank_low, dt_proj)
    input_map = small_proj[:, DT_RANK : DT_RANK + STATE]
    output_map = small_proj[:, DT_RANK + STATE :]

    step_size = delta_apply(step_pre, dt_bias, real_rows)
    in_wide, out_wide = widened(input_map), widened(output_map)
    reset_wide = widened(start_flags[:, None] * RESET)
    rates = -(jnp.exp(a_log) / LN2).T
    skip_row = skip_gain[None, :]
    ends_ex, cum_ex, end_all, cum_all = scan_ends(
        mixer_in, step_size, in_wide, reset_wide, rates
    )
    entering, cums = state_before(cum_all, end_all, rates, "hs")
    downs = from_half(after(down_own, entering))
    halo_wide = jnp.pad(halo_rows, ((8 - (CONV - 1), 0), (0, 0)))
    rank_wide = jnp.pad(rank_low, ((0, 0), (0, LANES - DT_RANK)))
    scan_out, gated_low, gated_t = scan_outputs(
        mixer_in,
        step_size,
        in_wide,
        out_wide,
        reset_wide,
        rates,
        ends_ex,
        cum_ex,
        entering,
        skip_row,
        inner_gate,
        waits=[masks, halo_wide, rank_wide],
    )
    mixer_out = mm(gated_low, out_proj)
    middle = tokens_float + mixer_out * real_rows[:, None]
    normed_two, norm_two_back = jax.vjp(scaled_norm, middle, gain_ffn)
    router_probs = jax.nn.softmax(
        jnp.dot(normed_two, router, precision=highest, preferred_element_type=float_type), axis=1
    )
    chosen = (routes[:, None] == jnp.arange(experts, dtype=jnp.int32)[None, :]).astype(float_type)
    gate_value = jnp.sum(router_probs * chosen, axis=1)
    column = routes * capacity + slot_index
    placed = (
        (column[:, None] == jnp.arange(experts * capacity, dtype=jnp.int32)[None, :])
        & (slot_index[:, None] >= 0)
    ).astype(low_type)
    grad_out = out_grad.astype(float_type)
    token_grad = grad_out * gate_value[:, None]

    rows_low = t_mm(placed, normed_two.astype(low_type)).astype(low_type)
    rows_own = blocks_home(rows_low.reshape(experts, capacity, model_width)).reshape(
        -1, model_width
    )
    rows_pair = to_other_half(rows_own)
    grads_low = t_mm(placed, token_grad.astype(low_type)).astype(low_type)
    grads_own = blocks_home(grads_low.reshape(experts, capacity, model_width)).reshape(
        -1, model_width
    )
    grads_pair = to_other_half(after(grads_own, rows_pair))
    gated_blocks = blocks_home(after(gated_t, grads_own).reshape(groups, -1, length))
    rows = jnp.concatenate([rows_own, rows_pair], axis=0)

    def near_parts(gathered):
        return [
            lax.dynamic_index_in_dim(gathered, jnp.bitwise_xor(place, k), 0, False)
            for k in range(shares)
        ]

    up_all, down_all = near_parts(ups), near_parts(downs)
    pre_all = [mm(rows, up) for up in up_all]
    hidden_all, gelu_backs = zip(*[jax.vjp(gelu_tanh, pre) for pre in pre_all])
    hidden_all = [hidden.astype(low_type) for hidden in hidden_all]
    expert_part = sum(mm(hidden, down) for hidden, down in zip(hidden_all, down_all))
    count = rows_own.shape[0]

    def pair_sum(partial, *earlier):
        other = to_other_half(after(partial[count:].astype(low_type), *earlier))
        return (partial[:count] + other.astype(float_type)).astype(low_type), other

    back_rows, rows_other = pair_sum(expert_part, grads_pair)
    home_rows = blocks_home(back_rows.reshape(groups, -1, model_width))
    grads = jnp.concatenate([grads_own, after(grads_pair, expert_part)], axis=0)
    pre_grads = [
        back(mm_t(grads, down))[0].astype(low_type) for back, down in zip(gelu_backs, down_all)
    ]
    grad_part = sum(mm_t(pre_grad, up) for pre_grad, up in zip(pre_grads, up_all))
    rows, grads = after(rows, back_rows), after(grads, back_rows)
    up_parts = [t_mm(rows, pre_grad) for pre_grad in pre_grads]
    down_parts = [t_mm(hidden, grads) for hidden in hidden_all]
    up_sent = jnp.stack([part.astype(low_type) for part in up_parts[1:]])
    down_sent = jnp.stack([part.astype(low_type) for part in down_parts[1:]])
    grad_rows, _ = pair_sum(grad_part, rows_other)
    up_grad, down_grad = up_parts[0], down_parts[0]
    grad_rows, up_sent, down_sent, up_grad, down_grad = lax.optimization_barrier(
        (grad_rows, up_sent, down_sent, up_grad, down_grad)
    )
    up_sent = from_half(up_sent)
    home_grad = blocks_home(after(grad_rows, home_rows).reshape(groups, -1, model_width))

    expert_out = mm(placed, home_rows.reshape(experts * capacity, model_width))
    block_out = (middle + gate_value[:, None] * expert_out).astype(low_type)
    gate_grad = jnp.sum(grad_out * expert_out, axis=1)
    logit_grad = router_probs * gate_grad[:, None] * (chosen - gate_value[:, None])
    router_grad = lax.dot_general(
        normed_two, logit_grad, ROWS_FIRST, precision=highest, preferred_element_type=float_type
    )
    normed_two_grad = mm(
        placed, home_grad.reshape(experts * capacity, model_width)
    ) + lax.dot_general(
        logit_grad, router, LAST_DIMS, precision=highest, preferred_element_type=float_type
    )
    middle_norm_grad, gain_ffn_grad = norm_two_back(normed_two_grad)
    middle_grad = grad_out + middle_norm_grad
    mixer_grad = (middle_grad * real_rows[:, None]).astype(low_type)
    mixer_grad_all = lax.all_gather(mixer_grad, "ep")
    gated_grad = mm_t(mixer_grad, out_proj)
    scan_grad, gate_pre_low, gate_pre_t, adj_ex, back_cum_ex, adj_all = scan_adjoints(
        gated_grad,
        inner_gate,
        scan_out,
        step_size,
        out_wide,
        reset_wide,
        rates,

    )
    returning = state_after(cums, adj_all, rates, "hs")
    gate_blocks = blocks_home(after(by_owner(gate_pre_t), returning))
    down_sent = from_half(after(down_sent, returning))
    scan_in_grad, pre_step_low, wide_grads, log_grad, skip_grad, dt_bias_grad = scan_grads(
        mixer_in,
        step_size,
        in_wide,
        out_wide,
        reset_wide,
        rates,
        ends_ex,
        cum_ex,
        entering,
        skip_row,
        scan_grad,
        adj_ex,
        back_cum_ex,
        returning,
        step_pre,
        dt_bias[None, :],
        masks,
        waits=[gated_blocks],
    )
    pre_step_low = after(pre_step_low, gate_blocks)
    rank_grad = mm_t(pre_step_low, dt_proj)
    small_grad = jnp.concatenate([rank_grad, fold_maps(wide_grads)], axis=1).astype(low_type)
    head = CONV - 1
    head_grad = scan_in_grad[:head] + mm_t(small_grad[:head], x_proj)

    def conv_head(rows_part):
        return conv_mix(inner_x[:head], rows_part, start_flags[:head], conv_weight, conv_bias)

    halo_grad = jax.vjp(conv_head, halo_rows)[1](head_grad)[0]
    here = member[None]
    out_gate = block_shares(
        [gated_blocks, gate_blocks], [mixer_grad_all, normed_all], here, members
    )
    edge_grad = after(shifted_2(halo_grad, "hs", -1), out_gate) * edge_mask
    inner_low, inner_t, conv_weight_grad, conv_bias_grad = conv_back(
        edge_start[None],
        scan_in_grad,
        small_grad,
        x_proj.T,
        inner_x,
        halo_wide,
        jnp.pad(edge_grad, ((0, 8 - head), (0, 0))),
        masks,
        conv_weight,
        conv_bias[None, :],
        waits=[out_gate],
    )

    inner_sent = by_owner(inner_t)
    inner_blocks = blocks_home(inner_sent)
    small_rows = [
        log_grad,
        dt_bias_grad,
        skip_grad,
        after(router_grad, inner_sent).reshape(inner_width, -1).T,
        conv_weight_grad,
        conv_bias_grad,
    ]
    sizes = [row.shape[0] for row in small_rows]
    packed = channel_pack(
        mixer_low,
        jnp.pad(small_grad, ((0, 0), (0, LANES - small_grad.shape[1]))),
        pre_step_low,
        rank_wide,
        small_rows,
        waits=[inner_sent],
    )
    inner_part = block_shares(
        [inner_blocks], [normed_all], here, members, waits=[out_gate, packed]
    )
    packed = blocks_home(after(packed, inner_part).reshape(groups, -1, 2 * LANES))
    packed_part = jnp.sum(packed.astype(float_type), axis=0).astype(low_type)
    packed_sum = summed_shares(packed_part.reshape(members, -1, 2 * LANES), "hs")
    inner_low = after(inner_low, inner_part)
    normed_one_grad = mm_t(inner_low, in_proj[:, :inner_width]) + mm_t(
        after(gate_pre_low, inner_part), in_proj[:, inner_width:]
    )
    tokens_norm_grad, gain_mix_grad = norm_one_back(normed_one_grad)
    tokens_grad = middle_grad + tokens_norm_grad
    gains = jnp.concatenate([gain_mix_grad, gain_ffn_grad]).reshape(groups * members, -1)
    gains = lax.all_to_all(
        after(gains, packed), ("ep", "hs"), split_axis=0, concat_axis=0, tiled=True
    )
    gains_sum = jnp.sum(gains, axis=0)
    for k in range(1, shares):
        sender = jnp.bitwise_xor(place, k)
        up_other = lax.dynamic_index_in_dim(after(up_sent, inner_part), sender, 0, False)[k - 1]
        down_other = lax.dynamic_index_in_dim(after(down_sent, inner_part), sender, 0, False)[k - 1]
        up_grad = up_grad + up_other.astype(float_type)
        down_grad = down_grad + down_other.astype(float_type)

    inner_sum = summed_ahead(inner_part, "hs")[0]
    out_proj_sum, gate_sum = summed_ahead(out_gate, "hs", inner_sum)
    given = jnp.where(upper, inner_sum, gate_sum).astype(low_type)
    given = after(given, gains_sum, packed_sum)
    kept = jnp.where(upper, gate_sum, inner_sum)
    taken = crossed(given, "ep", half).astype(float_type)
    in_proj_sum = jnp.concatenate(
        [jnp.where(upper, taken, kept), jnp.where(upper, kept, taken)], axis=0
    ).T
    cut, at = [], LANES + DT_RANK
    for size in sizes:
        cut.append(packed_sum[:, at : at + size])
        at += size
    return (
        block_out,
        tokens_grad,
        gains_sum,
        cut[3].reshape(-1),
        in_proj_sum,
        cut[4].T,
        cut[5][:, 0],
        packed_sum[:, : DT_RANK + 2 * STATE],
        packed_sum[:, LANES : LANES + DT_RANK].T,
        cut[1][:, 0],
        cut[0],
        cut[2][:, 0],
        out_proj_sum,
        up_grad[None],
        down_grad[None],
    )


def solution(mesh):
    return jax.shard_map(
        body,
        mesh=mesh,
        in_specs=(
            P(("ep", "hs"), None),
            P(("ep", "hs")),
            P(("ep", "hs")),
            P(("ep", "hs")),
            P(("ep", "hs")),
            P(),
            P(),
            P(),
            P(),
            P(),
            P(),
            P(),
            P(),
            P(),
            P(),
            P(),
            P(),
            P("ep", None, "hs"),
            P("ep", "hs", None),
            P(("ep", "hs"), None),
        ),
        out_specs=(
            P(("ep", "hs"), None),
            P(("ep", "hs"), None),
            P(("ep", "hs")),
            P(("ep", "hs")),
            P(None, ("ep", "hs")),
            P(None, ("ep", "hs")),
            P(("ep", "hs")),
            P(("ep", "hs"), None),
            P(None, ("ep", "hs")),
            P(("ep", "hs")),
            P(("ep", "hs"), None),
            P(("ep", "hs")),
            P(("ep", "hs"), None),
            P("ep", None, "hs"),
            P("ep", "hs", None),
        ),
        check_vma=False,
    )
```
